128 devices in a mesh: grp: 4 (over z_hi, core), seq: 32 (over x, y, z_lo).
Axes of the slice: x: 4, y: 4, z: 4 (z_hi: 2, z_lo: 2; z = z_hi * 2 + z_lo), core: 2. Of those that a mesh axis runs over, the one named last changes fastest.
Arguments:
- inputs: bfloat16 [16, 4096, 512], P('grp', 'seq'), may hold values from -6 to 6
- history: int32 [16, 4096], P('grp', 'seq'), may hold values from 0 to 65535
- lengths: int32 [16], replicated, may hold values from 1024 to 4096
- w_joined: bfloat16 [512, 2048], replicated, may hold values from -0.25 to 0.25
- w_out: bfloat16 [512, 512], replicated, may hold values from -0.25 to 0.25
- neg_emb: bfloat16 [65536, 512], P(('grp', 'seq')), may hold values from -6 to 6
- neg_ids: int32 [65536], P(('grp', 'seq')), may hold values from 0 to 65535
Outputs:
- grad_joined: float32 [512, 2048], replicated
- grad_out: float32 [512, 512], replicated
- loss: float32 [], replicated
The draws below stay inside these ranges and needn't reach their ends.
All inputs are finite; a program needn't handle non-finite values.
Results may differ from the reference program's by a relative error of at most 0.013.
Values may be sent and summed in bfloat16 or wider, within the bound.
A program may use at most 128 MiB of HBM per device.

```python
import math
import jax
import jax.numpy as jnp
import numpy as np
from jax import lax

D = 512
HEADS = 8
LENGTH = 4096
NEG = 512
CATALOG = 65536
BATCH = 16
NEG_ALL = 65536
N_GRP = 4
N_SEQ = 32


def draw_lengths(key, part):
    key = jax.random.fold_in(key, 7)
    key_vals, key_pick = jax.random.split(key)
    values = jax.random.randint(key_vals, (BATCH,), LENGTH // 4, LENGTH + 1)
    chosen = jax.random.randint(key_pick, (), 0, BATCH)
    return jnp.where(jnp.arange(BATCH) == chosen, LENGTH, values).astype(jnp.int32)


def with_ends(drawn, rng, smallest, top_value):
    index_at = [jax.random.randint(jax.random.fold_in(rng, axis), (), 0, length) for axis, length in enumerate(drawn.shape)]
    main_axis = drawn.shape.index(max(drawn.shape))
    beside = index_at[:main_axis] + [(index_at[main_axis] + 1) % drawn.shape[main_axis]] + index_at[main_axis + 1:]
    return drawn.at[tuple(index_at)].set(smallest).at[tuple(beside)].set(top_value)


def level_of(key, extent, cuts, least, top_value):
    gain = 1.0
    for axis_at, blocks in cuts:
        steps = jax.random.uniform(jax.random.fold_in(jax.random.fold_in(key, 6), axis_at), (blocks,), jnp.float32, least / len(cuts), top_value / len(cuts))
        gain = gain * jnp.repeat(jnp.exp(steps), extent[axis_at] // blocks).reshape((-1,) + (1,) * (len(extent) - 1 - axis_at))
    return gain


def rank_bounds(amount, slope):
    portions = [(1 << 20) // math.isqrt(rank ** slope) + 1 for rank in range(1, amount + 1)]
    deviation = 1 + sum(portions) // (1 << 30)
    return np.cumsum(np.array([max(1, weight // deviation) for weight in portions]))


def skewed_ids(stream_key, dims, count, skew):
    listing = rank_bounds(count, skew)
    pick = jax.random.randint(jax.random.fold_in(stream_key, 1), dims, 0, int(listing[count - 1]))
    grade = jnp.searchsorted(jnp.asarray(listing, jnp.int32), pick, side="right")
    return jax.random.permutation(jax.random.fold_in(stream_key, 2), count)[grade].astype(jnp.int32)


def centred(key, extent, scale, reach, cuts=(), held_as=jnp.bfloat16):
    factor_of = level_of(key, extent, cuts, -0.22, 0.18) if cuts else 1.0
    result = jax.random.normal(key, extent, jnp.float32) * scale * factor_of
    return jnp.minimum(jnp.maximum(result, -reach), reach).astype(held_as)


def setup_inputs(seed: int = 0) -> dict:
    arg_keys = jax.random.split(jax.random.key(seed), 8)
    inputs = centred(arg_keys[0], (BATCH, LENGTH, D), 1.0, 6.0, ((0, 4), (1, 32)))
    history = with_ends(skewed_ids(arg_keys[1], (BATCH, LENGTH), CATALOG, 2), jax.random.fold_in(arg_keys[1], 3), 0, CATALOG - 1).astype(jnp.int32)
    lengths = draw_lengths(jax.random.fold_in(arg_keys[7], 71), 0)
    w_joined = centred(arg_keys[3], (D, 4 * D), D ** -0.5, 0.25)
    w_out = centred(arg_keys[4], (D, D), D ** -0.5, 0.25)
    neg_emb = centred(arg_keys[5], (NEG_ALL, D), 1.0, 6.0, ((0, 128),))
    neg_ids = with_ends(skewed_ids(arg_keys[6], (NEG_ALL,), CATALOG, 2), jax.random.fold_in(arg_keys[6], 3), 0, CATALOG - 1).astype(jnp.int32)
    return dict(inputs=inputs, history=history, lengths=lengths, w_joined=w_joined, w_out=w_out, neg_emb=neg_emb, neg_ids=neg_ids)


eps_norm = 1e-06
logit_scale = 64.0

def rounded(values):
    return lax.optimization_barrier(values.astype(jnp.bfloat16))

def layer_norm(values):
    centered = values - lax.optimization_barrier(jnp.mean(values, axis=-1, keepdims=True))
    inv_std = lax.rsqrt(lax.optimization_barrier(jnp.mean(centered * centered, axis=-1, keepdims=True)) + eps_norm)
    return (centered * inv_std, inv_std)

def unit_rows(values):
    return values * lax.rsqrt(lax.optimization_barrier(jnp.sum(values * values, axis=-1, keepdims=True)) + eps_norm)

def silu_slope(values):
    sig_part = jax.nn.sigmoid(values)
    return sig_part * (1.0 + values * (1.0 - sig_part))

def reference(inputs, history, lengths, w_joined, w_out, neg_emb, neg_ids):
    block = LENGTH // N_SEQ
    head_dim = D // HEADS
    neg_unit = rounded(unit_rows(neg_emb.astype(jnp.float32)))
    neg_sets = neg_unit.reshape(N_GRP, N_SEQ, NEG, D).transpose(1, 0, 2, 3).reshape(N_SEQ, N_GRP * NEG, D).astype(jnp.float32)
    id_sets = neg_ids.reshape(N_GRP, N_SEQ, NEG).transpose(1, 0, 2).reshape(N_SEQ, N_GRP * NEG)
    id_rows = jnp.repeat(id_sets, block, axis=0)
    target_count = jnp.sum(lengths - 1).astype(jnp.float32)
    positions = jnp.arange(LENGTH, dtype=jnp.int32)

    def to_heads(values):
        return values.astype(jnp.float32).reshape(LENGTH, HEADS, head_dim).transpose(1, 0, 2)

    def to_rows(values):
        return values.astype(jnp.float32).transpose(1, 0, 2).reshape(LENGTH, D)

    def one_sequence(carry, item):
        tokens, ids, seq_len = item
        x_float = tokens.astype(jnp.float32)
        normed_in, _ = layer_norm(x_float)
        x_normed = normed_in.astype(jnp.bfloat16)
        pre_act = jnp.dot(x_normed, w_joined, preferred_element_type=jnp.float32)
        activated = jax.nn.silu(pre_act)
        u_part = rounded(activated[:, :D])
        v_heads = to_heads(rounded(activated[:, D:2 * D]))
        q_heads = to_heads(rounded(activated[:, 2 * D:3 * D]))
        k_heads = to_heads(rounded(activated[:, 3 * D:]))
        len_float = seq_len.astype(jnp.float32)
        key_mask = (positions[None, :] <= positions[:, None]) & (positions[None, :] < seq_len)

        def head_probs(q_one, k_one):
            scores = jnp.einsum('ld,md->lm', q_one, k_one)
            att_probs = rounded(jnp.where(key_mask, jax.nn.silu(scores), 0.0) / len_float)
            return (scores, att_probs)

        def head_forward(item_head):
            q_one, k_one, v_one = item_head
            _, att_probs = head_probs(q_one, k_one)
            return rounded(jnp.einsum('lm,md->ld', att_probs.astype(jnp.float32), v_one))
        attended = lax.map(head_forward, (q_heads, k_heads, v_heads))
        normed, inv_att = layer_norm(to_rows(attended))
        gated = (normed * u_part.astype(jnp.float32)).astype(jnp.bfloat16)
        out_rows = x_float + jnp.dot(gated, w_out, preferred_element_type=jnp.float32)
        inv_y = lax.rsqrt(lax.optimization_barrier(jnp.sum(out_rows * out_rows, axis=-1, keepdims=True)) + eps_norm)
        unit_y = out_rows * inv_y
        unit_b = rounded(unit_y).astype(jnp.float32)
        next_rows = jnp.concatenate([x_float[1:], jnp.zeros((1, D), jnp.float32)], axis=0)
        pos_unit = rounded(unit_rows(next_rows)).astype(jnp.float32)
        next_ids = jnp.concatenate([ids[1:], jnp.zeros((1,), jnp.int32)], axis=0)
        pos_logit = logit_scale * lax.optimization_barrier(jnp.sum(unit_b * pos_unit, axis=-1))
        neg_logit = logit_scale * jnp.einsum('icd,ind->icn', unit_b.reshape(N_SEQ, block, D), neg_sets).reshape(LENGTH, N_GRP * NEG)
        hit_mask = id_rows == next_ids[:, None]
        neg_exp = jnp.where(hit_mask, 0.0, jnp.exp(neg_logit))
        pos_exp = jnp.exp(pos_logit)
        denom_sum = pos_exp + lax.optimization_barrier(jnp.sum(neg_exp, axis=-1))
        valid = positions + 1 < seq_len
        loss_part = jnp.sum(jnp.where(valid, jnp.log(denom_sum) - pos_logit, 0.0))
        row_weight = jnp.where(valid, 1.0 / target_count, 0.0)
        d_pos = row_weight * (pos_exp / denom_sum - 1.0)
        d_neg = rounded(row_weight[:, None] * neg_exp / denom_sum[:, None]).astype(jnp.float32)
        neg_back = jnp.einsum('icn,ind->icd', d_neg.reshape(N_SEQ, block, N_GRP * NEG), neg_sets).reshape(LENGTH, D)
        d_unit = logit_scale * (d_pos[:, None] * pos_unit + neg_back)
        d_out = ((d_unit - unit_y * lax.optimization_barrier(jnp.sum(unit_y * d_unit, axis=-1, keepdims=True))) * inv_y).astype(jnp.bfloat16)
        d_gate = jnp.dot(d_out, w_out.T, preferred_element_type=jnp.float32)
        grad_out_part = jnp.dot(gated.T, d_out, preferred_element_type=jnp.float32)
        d_u = d_gate * normed
        d_norm = d_gate * u_part.astype(jnp.float32)
        d_att = inv_att * (d_norm - lax.optimization_barrier(jnp.mean(d_norm, axis=-1, keepdims=True)) - normed * lax.optimization_barrier(jnp.mean(d_norm * normed, axis=-1, keepdims=True)))
        d_att_h = to_heads(rounded(d_att))

        def head_backward(item_head):
            q_one, k_one, v_one, d_one = item_head
            scores, att_probs = head_probs(q_one, k_one)
            d_probs = jnp.einsum('ld,md->lm', d_one, v_one)
            d_v = rounded(jnp.einsum('lm,ld->md', att_probs.astype(jnp.float32), d_one))
            d_scores = rounded(jnp.where(key_mask, d_probs * silu_slope(scores), 0.0) / len_float).astype(jnp.float32)
            d_q = rounded(jnp.einsum('lm,md->ld', d_scores, k_one))
            d_k = rounded(jnp.einsum('lm,ld->md', d_scores, q_one))
            return (d_v, d_q, d_k)
        d_v, d_q, d_k = lax.map(head_backward, (q_heads, k_heads, v_heads, d_att_h))
        d_act = jnp.concatenate([d_u, to_rows(d_v), to_rows(d_q), to_rows(d_k)], axis=-1)
        d_pre = (d_act * silu_slope(pre_act)).astype(jnp.bfloat16)
        grad_joined_part = jnp.dot(x_normed.T, d_pre, preferred_element_type=jnp.float32)
        return ((carry[0] + grad_joined_part, carry[1] + grad_out_part, carry[2] + loss_part), None)
    init = (jnp.zeros((D, 4 * D), jnp.float32), jnp.zeros((D, D), jnp.float32), jnp.zeros((), jnp.float32))
    totals, _ = lax.scan(one_sequence, init, (inputs, history, lengths))
    return (totals[0], totals[1], totals[2] / target_count)
```

```python
import functools

import jax
import jax.numpy as jnp
from jax import lax
from jax.experimental import pallas as pl
from jax.experimental.pallas import tpu as pltpu
from jax.sharding import PartitionSpec as P

HEADS = 8
HEAD = 64
WIDTH = 512
PAIRS = 4
BLOCK = 128
TILE = 512
eps_norm = 1e-06
logit_scale = 64.0

MESH = pl.DeviceIdType.MESH
F32 = jnp.float32
BF16 = jnp.bfloat16
VMEM = pl.BlockSpec(memory_space=pltpu.VMEM)
SMEM = pl.BlockSpec(memory_space=pltpu.SMEM)


def dot_nn(a, b):
    return lax.dot_general(a, b, (((1,), (0,)), ((), ())), preferred_element_type=F32)


def dot_nt(a, b):
    return lax.dot_general(a, b, (((1,), (1,)), ((), ())), preferred_element_type=F32)


def dot_tn(a, b):
    return lax.dot_general(a, b, (((0,), (0,)), ((), ())), preferred_element_type=F32)


def low_lanes(shape):
    return lax.broadcasted_iota(jnp.int32, shape, 1) < HEAD


def turned(a):
    return pltpu.roll(a, HEAD, axis=1)


def swapped(a, b):
    low = low_lanes(a.shape)
    return jnp.where(low, a, turned(b)), jnp.where(low, turned(a), b)


def seq_barrier(me, n_seq):
    barrier = pltpu.get_barrier_semaphore()

    @pl.loop(1, n_seq)
    def _(step):
        pl.semaphore_signal(
            barrier, inc=1, device_id={"seq": lax.rem(me + step, n_seq)}, device_id_type=MESH
        )

    pl.semaphore_wait(barrier, n_seq - 1)


def push(src, dst, send_sem, recv_sem, where):
    pltpu.make_async_remote_copy(
        src_ref=src, dst_ref=dst, send_sem=send_sem, recv_sem=recv_sem,
        device_id=where, device_id_type=MESH,
    ).start()


def await_bytes(ref, sem):
    pltpu.make_async_copy(ref, ref, sem).wait()


def project_kernel(n_seq, x_ref, w_ref, xn_ref, u_ref, slope_ref, got_ref, send_ref, send_sem, recv_sem):
    me = lax.axis_index("seq")
    n_here = x_ref.shape[0]
    seq_barrier(me, n_seq)

    @pl.loop(0, n_here)
    def _(step):
        b = lax.rem(me // HEADS + step, n_here)
        x = x_ref[b].astype(F32)
        centered = x - jnp.mean(x, axis=-1, keepdims=True)
        var = jnp.mean(centered * centered, axis=-1, keepdims=True)
        xn = (centered * lax.rsqrt(var + eps_norm)).astype(BF16)
        xn_ref[b] = xn

        def activated(part):
            half = 0.5 * dot_nn(xn, w_ref[:, part * WIDTH:(part + 1) * WIDTH])
            th = jnp.tanh(half)
            slope = (0.5 + 0.5 * th) * (1.0 + half * (1.0 - th))
            slope_ref[b, :, part * WIDTH:(part + 1) * WIDTH] = slope.astype(BF16)
            return half + half * th

        v = activated(1)
        q = activated(2)
        k = activated(3)
        for pair in range(PAIRS):
            cols = slice(pair * 2 * HEAD, (pair + 1) * 2 * HEAD)
            kv = swapped(k[:, cols], v[:, cols])
            qs = swapped(q[:HEAD, cols], q[HEAD:, cols])
            for odd in range(2):
                j = b * HEADS + 2 * pair + odd
                send_ref[j, :BLOCK] = kv[odd].astype(BF16)
                send_ref[j, BLOCK:] = qs[odd].astype(BF16)

        @pl.loop(0, HEADS)
        def _(turn):
            j = b * HEADS + lax.rem(me + turn, HEADS)

            @pl.when(j != me)
            def _():
                push(send_ref.at[j], got_ref.at[me], send_sem, recv_sem, {"seq": j})

            @pl.when(j == me)
            def _():
                got_ref[me] = send_ref[me]

        u_ref[b] = activated(0).astype(BF16)

    await_bytes(send_ref.at[pl.ds(0, n_seq - 1)], send_sem)
    await_bytes(got_ref.at[pl.ds(0, n_seq - 1)], recv_sem)


def own_length(lens_ref, me, n_here):
    return lens_ref[lax.axis_index("grp") * n_here + me // HEADS]


def forward_kernel(n_seq, n_here, lens_ref, got_ref, back_ref, kv_ref, q_ref, acc_ref, send_ref, send_sem, recv_sem):
    me = lax.axis_index("seq")
    seq_barrier(me, n_seq)
    length = own_length(lens_ref, me, n_here)
    n_tiles = n_seq * BLOCK // TILE
    per_tile = TILE // BLOCK

    @pl.loop(0, n_seq)
    def _(i):
        rows = pl.ds(pl.multiple_of(i * BLOCK, BLOCK), BLOCK)
        pos = i * BLOCK + lax.broadcasted_iota(jnp.int32, (BLOCK, 2 * HEAD), 0)
        kv = got_ref[i, :BLOCK].astype(F32)
        kv_ref[rows] = jnp.where(pos < length, kv, 0.0).astype(BF16)
        q = got_ref[i, BLOCK:].astype(F32) * 0.5
        low = low_lanes(q.shape)
        q_ref[rows] = jnp.concatenate(
            [jnp.where(low, q, 0.0), jnp.where(low, turned(q), 0.0)], axis=0
        ).astype(BF16)

    inv_len = 1.0 / jnp.full((1, 2 * HEAD), length, jnp.int32).astype(F32)

    def probs(half):
        return (half + half * jnp.tanh(half)).astype(BF16)

    sub = TILE // 2

    @pl.loop(0, n_tiles)
    def _(step):
        c = lax.rem(me // per_tile + step, n_tiles)
        start = pl.multiple_of(c * TILE, TILE)
        q = q_ref[pl.ds(start, TILE)]
        kv_a = kv_ref[pl.ds(start, sub)]
        kv_b = kv_ref[pl.ds(start + sub, sub)]
        seen = lax.broadcasted_iota(jnp.int32, (sub, sub), 1) <= lax.broadcasted_iota(
            jnp.int32, (sub, sub), 0
        )
        acc_ref[:sub] = dot_nn(probs(jnp.where(seen, dot_nt(q[:sub], kv_a), 0.0)), kv_a)
        acc_ref[sub:] = dot_nn(probs(dot_nt(q[sub:], kv_a)), kv_a) + dot_nn(
            probs(jnp.where(seen, dot_nt(q[sub:], kv_b), 0.0)), kv_b
        )

        @pl.loop(0, c)
        def _(other):
            kv = kv_ref[pl.ds(pl.multiple_of(other * TILE, TILE), TILE)]
            acc_ref[...] += dot_nn(probs(dot_nt(q, kv)), kv)

        for u in range(per_tile):
            out = acc_ref[u * BLOCK:(u + 1) * BLOCK] * inv_len
            top, bottom = out[:HEAD], out[HEAD:]
            send_ref[c * per_tile + u] = jnp.where(
                low_lanes(top.shape), turned(top), bottom
            ).astype(BF16)

        @pl.loop(0, per_tile)
        def _(turn):
            i = c * per_tile + lax.rem(me + turn, per_tile)

            @pl.when(i != me)
            def _():
                push(send_ref.at[i], back_ref.at[me], send_sem, recv_sem, {"seq": i})

            @pl.when(i == me)
            def _():
                back_ref[me] = send_ref[me]

    await_bytes(send_ref.at[pl.ds(0, n_seq - 1)], send_sem)
    await_bytes(back_ref.at[pl.ds(0, n_seq - 1)], recv_sem)


def middle_kernel(
    n_seq, lens_ref, back_ref, x_ref, first_ref, id_next_ref, neg_ref, neg_ids_ref, w_out_ref, u_ref,
    slope_ref, got_ref, d_pre_ref, grad_ref, loss_ref, att_ref, exp_ref, send_ref, send_sem, recv_sem,
):
    me = lax.axis_index("seq")
    grp = lax.axis_index("grp")
    seq_barrier(me, n_seq)
    n_here = x_ref.shape[0]
    both = 2
    rows = both * BLOCK
    n_neg = neg_ref.shape[0]
    n_halves = n_here // both

    total = lens_ref[0] - 1
    for at in range(1, lens_ref.shape[0]):
        total = total + (lens_ref[at] - 1)
    weight = 1.0 / jnp.full((rows, 1), total, jnp.int32).astype(F32)
    grad_ref[...] = jnp.zeros_like(grad_ref)
    loss_ref[...] = jnp.zeros_like(loss_ref)

    @pl.loop(0, n_halves)
    def _(step):
        first_b = both * lax.rem(me // (both * HEADS) + step, n_halves)
        for e in range(both):
            for pair in range(PAIRS):
                j = (first_b + e) * HEADS + 2 * pair
                top, bottom = swapped(back_ref[j].astype(F32), back_ref[j + 1].astype(F32))
                cols = slice(pair * 2 * HEAD, (pair + 1) * 2 * HEAD)
                att_ref[e * BLOCK:e * BLOCK + HEAD, cols] = top
                att_ref[e * BLOCK + HEAD:(e + 1) * BLOCK, cols] = bottom

        def joined(make):
            return jnp.concatenate([make(e) for e in range(both)], axis=0)

        att = att_ref[...]
        centered = att - jnp.mean(att, axis=-1, keepdims=True)
        inv_att = lax.rsqrt(jnp.mean(centered * centered, axis=-1, keepdims=True) + eps_norm)
        normed = centered * inv_att
        u = joined(lambda e: u_ref[first_b + e]).astype(F32)
        gated = (normed * u).astype(BF16)
        x = joined(lambda e: x_ref[first_b + e]).astype(F32)
        out_rows = x + dot_nn(gated, w_out_ref[...])
        inv_y = lax.rsqrt(jnp.sum(out_rows * out_rows, axis=-1, keepdims=True) + eps_norm)
        unit_y = out_rows * inv_y
        unit_b = unit_y.astype(BF16)

        def next_rows(e):
            mine = x_ref[first_b + e].astype(F32)
            shifted = pltpu.roll(mine, BLOCK - 1, axis=0)
            is_last = lax.broadcasted_iota(jnp.int32, mine.shape, 0) == BLOCK - 1
            return jnp.where(is_last, first_ref[first_b + e].astype(F32)[:1], shifted)

        x_next = joined(next_rows)
        pos_unit = (
            x_next * lax.rsqrt(jnp.sum(x_next * x_next, axis=-1, keepdims=True) + eps_norm)
        ).astype(BF16).astype(F32)
        pos_logit = logit_scale * jnp.sum(unit_b.astype(F32) * pos_unit, axis=-1, keepdims=True)

        def row_ids(e):
            ids = id_next_ref[first_b + e][:1]
            return jnp.transpose(jnp.broadcast_to(ids, (BLOCK, BLOCK)))

        ids = joined(row_ids)
        lane_sum = jnp.zeros((rows, BLOCK), F32)
        for part in range(n_neg // WIDTH):
            neg_logit = logit_scale * dot_nt(unit_b, neg_ref[part * WIDTH:(part + 1) * WIDTH])
            for sub in range(WIDTH // BLOCK):
                at = part * (WIDTH // BLOCK) + sub
                hit = neg_ids_ref[at:at + 1] == ids
                exps = jnp.where(hit, 0.0, jnp.exp(neg_logit[:, sub * BLOCK:(sub + 1) * BLOCK]))
                exp_ref[:, at * BLOCK:(at + 1) * BLOCK] = exps
                lane_sum = lane_sum + exps
        pos_exp = jnp.exp(pos_logit)
        denom = pos_exp + jnp.sum(lane_sum, axis=-1, keepdims=True)

        def row_valid(e):
            seq_len = lens_ref[grp * n_here + first_b + e]
            pos = me * BLOCK + lax.broadcasted_iota(jnp.int32, (BLOCK, 1), 0)
            return jnp.where(pos + 1 < seq_len, 1.0, 0.0)

        valid = joined(row_valid)
        row_loss = jnp.where(valid > 0.0, jnp.log(denom) - pos_logit, 0.0)
        loss_ref[...] += jnp.broadcast_to(jnp.sum(row_loss, axis=0, keepdims=True), loss_ref.shape)
        row_weight = valid * weight
        d_pos = row_weight * (pos_exp / denom - 1.0)
        scale = row_weight / denom
        neg_back = jnp.zeros((rows, WIDTH), F32)
        for part in range(n_neg // WIDTH):
            d_neg = (scale * exp_ref[:, part * WIDTH:(part + 1) * WIDTH]).astype(BF16)
            neg_back = neg_back + dot_nn(d_neg, neg_ref[part * WIDTH:(part + 1) * WIDTH])
        d_unit = logit_scale * (d_pos * pos_unit + neg_back)
        d_out = (
            (d_unit - unit_y * jnp.sum(unit_y * d_unit, axis=-1, keepdims=True)) * inv_y
        ).astype(BF16)
        d_gate = dot_nt(d_out, w_out_ref[...])
        d_norm = d_gate * u
        d_att = inv_att * (
            d_norm
            - jnp.mean(d_norm, axis=-1, keepdims=True)
            - normed * jnp.mean(d_norm * normed, axis=-1, keepdims=True)
        )
        for e in range(both):
            mine = d_att[e * BLOCK:(e + 1) * BLOCK]
            for pair in range(PAIRS):
                cols = slice(pair * 2 * HEAD, (pair + 1) * 2 * HEAD)
                packed = swapped(mine[:HEAD, cols], mine[HEAD:, cols])
                for odd in range(2):
                    send_ref[(first_b + e) * HEADS + 2 * pair + odd] = packed[odd].astype(BF16)

        @pl.loop(0, both * HEADS)
        def _(turn):
            j = first_b * HEADS + lax.rem(me + turn, both * HEADS)

            @pl.when(j != me)
            def _():
                push(send_ref.at[j], got_ref.at[me], send_sem, recv_sem, {"seq": j})

            @pl.when(j == me)
            def _():
                got_ref[me] = send_ref[me]

        grad_ref[...] += dot_tn(gated, d_out)
        d_u = d_gate * normed
        for e in range(both):
            slope = slope_ref[first_b + e, :, :WIDTH].astype(F32)
            d_pre_ref[first_b + e] = (d_u[e * BLOCK:(e + 1) * BLOCK] * slope).astype(BF16)

    await_bytes(send_ref.at[pl.ds(0, n_seq - 1)], send_sem)
    await_bytes(got_ref.at[pl.ds(0, n_seq - 1)], recv_sem)


def backward_kernel(
    n_seq, n_here, lens_ref, got_ref, datt_ref, back_ref, qa_ref, lhs_ref, kt_ref, dq_ref, dkv_ref,
    send_ref, kv_send_sem, q_send_sem, kv_recv_sem, q_recv_sem,
):
    me = lax.axis_index("seq")
    seq_barrier(me, n_seq)
    length = own_length(lens_ref, me, n_here)
    n_tiles = n_seq * BLOCK // TILE
    per_tile = TILE // BLOCK

    @pl.loop(0, n_seq)
    def _(i):
        rows = pl.ds(pl.multiple_of(i * BLOCK, BLOCK), BLOCK)
        pos = i * BLOCK + lax.broadcasted_iota(jnp.int32, (BLOCK, 2 * HEAD), 0)
        kv = jnp.where(pos < length, got_ref[i, :BLOCK].astype(F32), 0.0)
        low = low_lanes(kv.shape)
        tile = i // per_tile
        at = pl.multiple_of(lax.rem(i, per_tile) * BLOCK, BLOCK)
        lhs_ref[tile, pl.ds(at, BLOCK)] = jnp.where(low, 0.5 * kv, 0.0).astype(BF16)
        lhs_ref[tile, pl.ds(TILE + at, BLOCK)] = jnp.where(low, 0.0, kv).astype(BF16)
        kt_ref[tile, :, pl.ds(at, BLOCK)] = jnp.transpose(kv)[:HEAD].astype(BF16)
        top, bottom = swapped(got_ref[i, BLOCK:].astype(F32), datt_ref[i].astype(F32))
        qa_ref[rows] = jnp.concatenate([top, bottom], axis=0).astype(BF16)

    dq_ref[...] = jnp.zeros_like(dq_ref)
    inv_len = 1.0 / jnp.full((1, 2 * HEAD), length, jnp.int32).astype(F32)
    low_row = low_lanes((1, 2 * HEAD))
    kv_scale = jnp.where(low_row, 0.5 * inv_len, inv_len)
    low = low_lanes((TILE, 2 * HEAD))

    def tile_grads(c, other, masked):
        qa = qa_ref[pl.ds(pl.multiple_of(other * TILE, TILE), TILE)]
        both = dot_nt(lhs_ref[c], qa)
        half, d_probs = both[:TILE], both[TILE:]
        if masked:
            seen = lax.broadcasted_iota(jnp.int32, (TILE, TILE), 0) <= lax.broadcasted_iota(
                jnp.int32, (TILE, TILE), 1
            )
            half = jnp.where(seen, half, 0.0)
            d_probs = jnp.where(seen, d_probs, 0.0)
        up = 1.0 + jnp.tanh(half)
        probs = half * up
        d_scores = (d_probs * up * (1.0 + (half + half) - probs)).astype(BF16)
        dq_ref[other] += dot_nn(kt_ref[c], d_scores)
        return jnp.where(low, dot_nn(d_scores, qa), dot_nn(probs.astype(BF16), qa))

    @pl.loop(0, n_tiles)
    def _(step):
        c = lax.rem(me // per_tile + step, n_tiles)
        dkv_ref[...] = tile_grads(c, c, True)

        @pl.loop(c + 1, n_tiles)
        def _(other):
            dkv_ref[...] += tile_grads(c, other, False)

        for u in range(per_tile):
            send_ref[c * per_tile + u, :BLOCK] = (
                dkv_ref[u * BLOCK:(u + 1) * BLOCK] * kv_scale
            ).astype(BF16)

        @pl.loop(0, per_tile)
        def _(turn):
            i = c * per_tile + lax.rem(me + turn, per_tile)

            @pl.when(i != me)
            def _():
                push(
                    send_ref.at[i, pl.ds(0, BLOCK)], back_ref.at[me, pl.ds(0, BLOCK)],
                    kv_send_sem, kv_recv_sem, {"seq": i},
                )

    @pl.loop(0, n_tiles)
    def _(step):
        c = lax.rem(me // per_tile + step, n_tiles)
        for u in range(per_tile):
            d_q = dq_ref[c, :, u * BLOCK:(u + 1) * BLOCK] * (0.5 * inv_len)
            send_ref[c * per_tile + u, BLOCK:] = d_q.astype(BF16)

        @pl.loop(0, per_tile)
        def _(turn):
            i = c * per_tile + lax.rem(me + turn, per_tile)

            @pl.when(i != me)
            def _():
                push(
                    send_ref.at[i, pl.ds(BLOCK, HEAD)], back_ref.at[me, pl.ds(BLOCK, HEAD)],
                    q_send_sem, q_recv_sem, {"seq": i},
                )

            @pl.when(i == me)
            def _():
                back_ref[me] = send_ref[me]

    others = pl.ds(0, n_seq - 1)
    await_bytes(send_ref.at[others, pl.ds(0, BLOCK)], kv_send_sem)
    await_bytes(send_ref.at[others, pl.ds(BLOCK, HEAD)], q_send_sem)
    await_bytes(back_ref.at[others, pl.ds(0, BLOCK)], kv_recv_sem)
    await_bytes(back_ref.at[others, pl.ds(BLOCK, HEAD)], q_recv_sem)


def gradient_kernel(
    n_seq, back_ref, xn_ref, slope_ref, d_pre_u_ref, grad_out_ref, joined_ref, out_ref,
    d_pre_ref, part_ref, core_ref, sum_ref, got_ref, red_ref, full_ref, send_sem, recv_sem,
):
    me = lax.axis_index("seq")
    grp = lax.axis_index("grp")
    core, z_hi = lax.rem(grp, 2), grp // 2
    n_here = xn_ref.shape[0]
    rows = n_here * BLOCK
    group = part_ref.shape[-1]
    per = BLOCK // HEAD * 8
    mate = {"grp": grp + 1 - 2 * core}

    barrier = pltpu.get_barrier_semaphore()
    pl.semaphore_signal(barrier, inc=1, device_id=mate, device_id_type=MESH)

    @pl.loop(1, 2 * n_seq)
    def _(step):
        slot = lax.rem(z_hi * n_seq + me + step, 2 * n_seq)
        pl.semaphore_signal(
            barrier, inc=1, device_id_type=MESH,
            device_id={"grp": slot // n_seq * 2 + core, "seq": lax.rem(slot, n_seq)},
        )

    for b in range(n_here):
        at = slice(b * BLOCK, (b + 1) * BLOCK)
        d_pre_ref[at, :WIDTH] = d_pre_u_ref[b]
        for pair in range(PAIRS):
            j = b * HEADS + 2 * pair
            d_k, d_v = swapped(back_ref[j, :BLOCK].astype(F32), back_ref[j + 1, :BLOCK].astype(F32))
            d_q = jnp.transpose(
                jnp.concatenate(
                    [back_ref[j, BLOCK:].astype(F32), back_ref[j + 1, BLOCK:].astype(F32)], axis=0
                )
            )
            for part, grad in ((1, d_v), (2, d_q), (3, d_k)):
                low = part * WIDTH + pair * 2 * HEAD
                slope = slope_ref[b, :, low:low + 2 * HEAD].astype(F32)
                d_pre_ref[at, low:low + 2 * HEAD] = (grad * slope).astype(BF16)

    xn = jnp.concatenate([xn_ref[b] for b in range(n_here)], axis=0)
    total_cols = 4 * WIDTH
    for g in range(4):
        low, high = g * group, (g + 1) * group
        if high <= total_cols:
            part = dot_tn(xn, d_pre_ref[:, low:high])
            part_ref[g % 2, g // 2] = part.astype(BF16)
        else:
            split = total_cols - low
            part_ref[g % 2, g // 2, :, :split] = dot_tn(xn, d_pre_ref[:, low:total_cols]).astype(BF16)
            part_ref[g % 2, g // 2, :, split:] = grad_out_ref[...].astype(BF16)

    pl.semaphore_wait(barrier, 2 * n_seq)
    push(part_ref.at[1 - core], core_ref, send_sem.at[0], recv_sem.at[0], mate)
    await_bytes(part_ref.at[0], send_sem.at[0])
    await_bytes(core_ref, recv_sem.at[0])

    @pl.loop(0, n_seq)
    def _(i):
        at = pl.ds(pl.multiple_of(i * per, per), per)
        for z in range(2):
            sum_ref[z * n_seq + i] = (
                part_ref[core, z, at].astype(F32) + core_ref[z, at].astype(F32)
            ).astype(BF16)

    mine = z_hi * n_seq + me

    @pl.loop(1, 2 * n_seq)
    def _(step):
        slot = lax.rem(mine + step, 2 * n_seq)
        push(
            sum_ref.at[slot], got_ref.at[mine], send_sem.at[1], recv_sem.at[1],
            {"grp": slot // n_seq * 2 + core, "seq": lax.rem(slot, n_seq)},
        )

    got_ref[mine] = sum_ref[mine]
    others = pl.ds(0, 2 * n_seq - 1)
    await_bytes(sum_ref.at[others], send_sem.at[1])
    await_bytes(got_ref.at[others], recv_sem.at[1])

    red_ref[...] = lax.fori_loop(
        0, 2 * n_seq, lambda at, total: total + got_ref[at].astype(F32),
        jnp.zeros(red_ref.shape, F32),
    ).astype(BF16)

    @pl.loop(1, 2 * n_seq)
    def _(step):
        slot = lax.rem(mine + step, 2 * n_seq)
        push(
            red_ref, full_ref.at[core, mine], send_sem.at[2], recv_sem.at[2],
            {"grp": slot // n_seq * 2 + core, "seq": lax.rem(slot, n_seq)},
        )

    full_ref[core, mine] = red_ref[...]
    await_bytes(full_ref.at[0, others], send_sem.at[2])
    await_bytes(full_ref.at[0, others], recv_sem.at[2])
    push(full_ref.at[core], full_ref.at[core], send_sem.at[3], recv_sem.at[3], mate)
    await_bytes(full_ref.at[0], send_sem.at[3])
    await_bytes(full_ref.at[0], recv_sem.at[3])

    @pl.loop(0, n_seq)
    def _(i):
        at = pl.ds(pl.multiple_of(i * per, per), per)
        for g in range(4):
            block = full_ref[g % 2, g // 2 * n_seq + i].astype(F32)
            low, high = g * group, (g + 1) * group
            if high <= total_cols:
                joined_ref[at, low:high] = block
            else:
                split = total_cols - low
                joined_ref[at, low:total_cols] = block[:, :split]
                out_ref[at] = block[:, split:]


def call(body, out_shape, in_specs, scratch, collective, cost=None):
    return pl.pallas_call(
        body,
        out_shape=out_shape,
        in_specs=in_specs,
        out_specs=jax.tree.map(lambda _: VMEM, out_shape),
        scratch_shapes=scratch,
        cost_estimate=cost,
        compiler_params=pltpu.CompilerParams(
            collective_id=collective, has_side_effects=True, vmem_limit_bytes=56 * 1024 * 1024
        ),
    )


def shaped(shape, dtype):
    return jax.ShapeDtypeStruct(shape, dtype)


def unit_rows(values):
    return values * lax.rsqrt(jnp.sum(values * values, axis=-1, keepdims=True) + eps_norm)


def local(inputs, history, lengths, w_joined, w_out, neg_emb, neg_ids):
    n_here, block, width = inputs.shape
    n_seq = lax.axis_size("seq")
    length = n_seq * block
    n_tiles = length // TILE
    lanes = 2 * HEAD
    dma = pltpu.SemaphoreType.DMA

    neg_unit = unit_rows(neg_emb.astype(F32)).astype(BF16)
    all_neg = lax.all_gather(neg_unit, "grp", axis=0, tiled=True)
    all_ids = lax.all_gather(neg_ids, "grp", axis=0, tiled=True).reshape(-1, BLOCK)
    passes = [(source, source - 1) for source in range(1, n_seq)]
    next_first = lax.ppermute(inputs[:, :1, :], "seq", passes)
    next_first_id = lax.ppermute(history[:, :1], "seq", passes)
    id_next = jnp.concatenate([history[:, 1:], next_first_id], axis=1)

    rows3 = (n_here, block, width)
    pack3 = (n_seq, BLOCK + HEAD, lanes)
    pack1 = (n_seq, HEAD, lanes)
    xn, u, slope, got = call(
        functools.partial(project_kernel, n_seq),
        [shaped(rows3, BF16), shaped(rows3, BF16), shaped((n_here, block, 4 * width), BF16), shaped(pack3, BF16)],
        [VMEM, VMEM],
        [pltpu.VMEM(pack3, BF16), dma, dma],
        0,
    )(inputs, w_joined)

    back = call(
        functools.partial(forward_kernel, n_seq, n_here),
        [shaped(pack1, BF16)],
        [SMEM, VMEM],
        [
            pltpu.VMEM((length, lanes), BF16), pltpu.VMEM((length, lanes), BF16),
            pltpu.VMEM((TILE, lanes), F32), pltpu.VMEM(pack1, BF16), dma, dma,
        ],
        1,
    )(lengths, got)[0]

    n_neg = all_neg.shape[0]
    d_att, d_pre_u, grad_out, loss = call(
        functools.partial(middle_kernel, n_seq),
        [shaped(pack1, BF16), shaped(rows3, BF16), shaped((width, width), F32), shaped((8, BLOCK), F32)],
        [SMEM] + [VMEM] * 9,
        [
            pltpu.VMEM((2 * BLOCK, width), F32), pltpu.VMEM((2 * BLOCK, n_neg), F32),
            pltpu.VMEM(pack1, BF16), dma, dma,
        ],
        2,
    )(lengths, back, inputs, next_first, id_next[:, None, :], all_neg, all_ids, w_out, u, slope)

    grads = call(
        functools.partial(backward_kernel, n_seq, n_here),
        [shaped(pack3, BF16)],
        [SMEM, VMEM, VMEM],
        [
            pltpu.VMEM((length, lanes), BF16), pltpu.VMEM((n_tiles, 2 * TILE, lanes), BF16),
            pltpu.VMEM((n_tiles, HEAD, TILE), BF16), pltpu.VMEM((n_tiles, HEAD, TILE), F32),
            pltpu.VMEM((TILE, lanes), F32), pltpu.VMEM(pack3, BF16), dma, dma, dma, dma,
        ],
        3,
    )(lengths, got, d_att)[0]

    group = 5 * width // 4
    strip = (2 * n_seq, width // n_seq, group)
    grad_joined, grad_total = call(
        functools.partial(gradient_kernel, n_seq),
        [shaped((width, 4 * width), F32), shaped((width, width), F32)],
        [VMEM] * 5,
        [
            pltpu.VMEM((n_here * block, 4 * width), BF16), pltpu.VMEM((2, 2, width, group), BF16),
            pltpu.VMEM((2, width, group), BF16), pltpu.VMEM(strip, BF16), pltpu.VMEM(strip, BF16),
            pltpu.VMEM(strip[1:], BF16), pltpu.VMEM((2,) + strip, BF16), dma((4,)), dma((4,)),
        ],
        4,
    )(grads, xn, slope, d_pre_u, grad_out)

    target_count = jnp.sum(lengths - 1).astype(F32)
    loss_total = lax.psum(loss[0, 0], ("grp", "seq"))
    return (grad_joined, grad_total, loss_total / target_count)


def solution(mesh):
    placed = (
        P("grp", "seq", None),
        P("grp", "seq"),
        P(),
        P(),
        P(),
        P(("grp", "seq"), None),
        P(("grp", "seq")),
    )
    return jax.shard_map(
        local, mesh=mesh, in_specs=placed, out_specs=(P(), P(), P()), check_vma=False
    )
```

```python
import functools
import types

import jax
import jax.numpy as jnp
from jax import lax
from jax.experimental import pallas as pl
from jax.experimental.pallas import tpu as pltpu
from jax.sharding import PartitionSpec as P

HEADS = 8
HEAD = 64
WIDTH = 512
PAIRS = 4
BLOCK = 128
FQ = 512
FK = 2048
BM = 512
BT = 1024
eps_norm = 1e-06
logit_scale = 64.0

MESH = pl.DeviceIdType.MESH
F32 = jnp.float32
BF16 = jnp.bfloat16
VMEM = pl.BlockSpec(memory_space=pltpu.VMEM)
SMEM = pl.BlockSpec(memory_space=pltpu.SMEM)


def dot_nn(a, b):
    return lax.dot_general(a, b, (((1,), (0,)), ((), ())), preferred_element_type=F32)


def dot_nt(a, b):
    return lax.dot_general(a, b, (((1,), (1,)), ((), ())), preferred_element_type=F32)


def dot_tn(a, b):
    return lax.dot_general(a, b, (((0,), (0,)), ((), ())), preferred_element_type=F32)


def low_lanes(shape):
    return lax.broadcasted_iota(jnp.int32, shape, 1) < HEAD


def turned(a):
    return pltpu.roll(a, HEAD, axis=1)


def swapped(a, b):
    low = low_lanes(a.shape)
    return jnp.where(low, a, turned(b)), jnp.where(low, turned(a), b)


def copy_to(src, dst, send_sem, recv_sem, where):
    pltpu.make_async_remote_copy(
        src_ref=src, dst_ref=dst, send_sem=send_sem, recv_sem=recv_sem,
        device_id=where, device_id_type=MESH,
    ).start()


def await_bytes(ref, sem):
    pltpu.make_async_copy(ref, ref, sem).wait()


def aligned(at, size):
    return pl.ds(pl.multiple_of(at, size), size)


def pair_cols(pair):
    return slice(pair * 2 * HEAD, (pair + 1) * 2 * HEAD)


def kernel(n_seq, names, *refs):
    r = types.SimpleNamespace(**dict(zip(names, refs, strict=True)))
    me = lax.axis_index("seq")
    grp = lax.axis_index("grp")
    core, z_hi = lax.rem(grp, 2), grp // 2
    n_here = r.x.shape[0]
    planes = n_seq // HEADS
    length = n_seq * BLOCK
    n_chips = 2 * n_seq
    mine = z_hi * n_seq + me
    mate = {"grp": grp + 1 - 2 * core}
    other_z = {"grp": (1 - z_hi) * 2 + core}
    others = pl.ds(0, n_seq - 1)

    def chip(slot):
        return {"grp": slot // n_seq * 2 + core, "seq": lax.rem(slot, n_seq)}

    barrier = pltpu.get_barrier_semaphore()
    pl.semaphore_signal(barrier, inc=1, device_id=mate, device_id_type=MESH)

    @pl.loop(1, n_chips)
    def _(step):
        pl.semaphore_signal(
            barrier, inc=1, device_id=chip(lax.rem(mine + step, n_chips)), device_id_type=MESH
        )

    @pl.loop(0, n_here)
    def _(step):
        b = lax.rem(me // HEADS + step, n_here)
        x = r.x[b].astype(F32)
        centered = x - jnp.mean(x, axis=-1, keepdims=True)
        var = jnp.mean(centered * centered, axis=-1, keepdims=True)
        xn = (centered * lax.rsqrt(var + eps_norm)).astype(BF16)
        r.xn[b] = xn
        v, q, k = (activated(r, b, xn, part) for part in (1, 2, 3))
        for pair in range(PAIRS):
            cols = pair_cols(pair)
            kv = swapped(k[:, cols], v[:, cols])
            qs = swapped(q[:HEAD, cols], q[HEAD:, cols])
            for odd in range(2):
                j = b * HEADS + 2 * pair + odd
                r.send[j, :BLOCK] = kv[odd].astype(BF16)
                r.send[j, BLOCK:] = qs[odd].astype(BF16)

        @pl.when(step == 0)
        def _():
            pl.semaphore_wait(barrier, n_chips)

        @pl.loop(0, HEADS)
        def _(turn):
            j = b * HEADS + lax.rem(me + turn, HEADS)

            @pl.when(j != me)
            def _():
                copy_to(r.send.at[j], r.got.at[me], r.send_sem.at[0], r.got_sem.at[me], {"seq": j})

            @pl.when(j == me)
            def _():
                r.got[me] = r.send[me]

    before = {"seq": lax.rem(me + n_seq - 1, n_seq)}
    r.ids[:n_here] = r.history[...]
    r.ids[n_here:] = r.neg_ids[...]
    copy_to(r.x.at[:, pl.ds(0, 16)], r.first, r.send_sem.at[1], r.one_sem.at[0], before)
    copy_to(r.ids, r.next_ids, r.send_sem.at[2], r.one_sem.at[1], before)

    @pl.loop(0, n_here)
    def _(b):
        xn = r.xn[b]
        r.u[b] = activated(r, b, xn, 0).astype(BF16)
        r.xnt[:, aligned(b * BLOCK, BLOCK)] = jnp.transpose(xn.astype(F32)).astype(BF16)
        rows = aligned(b * BLOCK, BLOCK)
        emb = r.neg_emb[rows].astype(F32)
        r.negs[grp, rows] = (
            emb * lax.rsqrt(jnp.sum(emb * emb, axis=-1, keepdims=True) + eps_norm)
        ).astype(BF16)

    r.all_ids[grp] = r.ids[...]
    copy_to(r.negs.at[grp], r.negs.at[grp], r.send_sem.at[3], r.one_sem.at[2], mate)
    copy_to(r.all_ids.at[grp], r.all_ids.at[grp], r.send_sem.at[4], r.one_sem.at[3], mate)
    copy_to(r.negs.at[grp], r.negs.at[grp], r.send_sem.at[5], r.one_sem.at[4], other_z)
    copy_to(r.all_ids.at[grp], r.all_ids.at[grp], r.send_sem.at[6], r.one_sem.at[5], other_z)

    seq_len = r.lens[grp * n_here + me // HEADS]
    low = low_lanes((HEAD, 2 * HEAD))
    low_block = low_lanes((BLOCK, 2 * HEAD))

    @pl.loop(0, planes)
    def _(step):
        first = lax.rem(me // HEADS + planes - step, planes) * HEADS

        @pl.loop(0, HEADS)
        def _(turn):
            i = first + turn

            @pl.when(i != me)
            def _():
                await_bytes(r.got.at[0], r.got_sem.at[i])

        @pl.loop(0, HEADS, unroll=4)
        def _(turn):
            i = first + turn
            rows = aligned(i * BLOCK, BLOCK)
            pos = i * BLOCK + lax.broadcasted_iota(jnp.int32, (BLOCK, 2 * HEAD), 0)
            kv = jnp.where(pos < seq_len, r.got[i, :BLOCK].astype(F32), 0.0)
            r.k0[rows] = jnp.where(low_block, 0.5 * kv, 0.0).astype(BF16)
            r.v0[rows] = jnp.where(low_block, 0.0, kv).astype(BF16)
            r.kt[:, rows] = jnp.transpose(kv)[:HEAD].astype(BF16)
            q = r.got[i, BLOCK:].astype(F32)
            r.qa[rows] = jnp.concatenate(
                [jnp.where(low, q, 0.0), jnp.where(low, turned(q), 0.0)], axis=0
            ).astype(BF16)

    await_bytes(r.send.at[others], r.send_sem.at[0])
    inv_len = 1.0 / jnp.full((1, 2 * HEAD), seq_len, jnp.int32).astype(F32)

    f_tiles = length // FQ
    f_per = FQ // BLOCK

    @pl.loop(0, f_tiles)
    def _(step):
        c = lax.rem(me // f_per + step, f_tiles)
        q = r.qa[aligned(c * FQ, FQ)]
        r.acc[...] = jnp.zeros_like(r.acc)
        n_full = c * FQ // FK

        def piece(at, masked):
            rows = aligned(at * FK, FK)
            half = dot_nt(q, r.k0[rows])
            if masked:
                ahead = at * FK - c * FQ + lax.broadcasted_iota(
                    jnp.int32, (FQ, FK), 1
                ) - lax.broadcasted_iota(jnp.int32, (FQ, FK), 0)
                half = jnp.where(ahead <= 0, half, 0.0)
            probs = (half + half * jnp.tanh(half)).astype(BF16)
            r.acc[...] += dot_nn(probs, r.v0[rows])

        @pl.loop(0, n_full)
        def _(at):
            piece(at, False)

        piece(n_full, True)
        for u in range(f_per):
            out = r.acc[u * BLOCK:(u + 1) * BLOCK] * inv_len
            top, bottom = out[:HEAD], out[HEAD:]
            r.att_send[c * f_per + u] = jnp.where(low, turned(top), bottom).astype(BF16)

        @pl.loop(0, f_per)
        def _(turn):
            i = c * f_per + lax.rem(me + turn, f_per)

            @pl.when(i != me)
            def _():
                copy_to(
                    r.att_send.at[i], r.att_got.at[me], r.send_sem.at[7], r.att_sem.at[me], {"seq": i}
                )

            @pl.when(i == me)
            def _():
                r.att_got[me] = r.att_send[me]

    far = (1 - z_hi) * 2 + core
    await_bytes(r.negs.at[0], r.one_sem.at[4])
    await_bytes(r.all_ids.at[0], r.one_sem.at[5])
    copy_to(r.negs.at[far], r.negs.at[far], r.send_sem.at[8], r.one_sem.at[6], mate)
    copy_to(r.all_ids.at[far], r.all_ids.at[far], r.send_sem.at[9], r.one_sem.at[7], mate)

    total = r.lens[0] - 1
    for at in range(1, r.lens.shape[0]):
        total = total + (r.lens[at] - 1)
    both = 2
    half_rows = both * BLOCK
    weight = 1.0 / jnp.full((half_rows, 1), total, jnp.int32).astype(F32)
    r.grad_out[...] = jnp.zeros_like(r.grad_out)
    r.loss[...] = jnp.zeros_like(r.loss)
    await_bytes(r.first, r.one_sem.at[0])
    await_bytes(r.ids, r.one_sem.at[1])
    await_bytes(r.negs.at[0], r.one_sem.at[2])
    await_bytes(r.all_ids.at[0], r.one_sem.at[3])
    await_bytes(r.negs.at[0], r.one_sem.at[6])
    await_bytes(r.all_ids.at[0], r.one_sem.at[7])
    n_halves = n_here // both

    @pl.loop(0, n_halves)
    def _(step):
        middle(r, n_seq, me, grp, both * lax.rem(me // (both * HEADS) + step, n_halves), weight)

    r.e_part[0, 0] = dot_nn(r.xnt[...], r.d_pre[:, :WIDTH // 2]).astype(BF16)
    r.e_part[1, 0] = dot_nn(r.xnt[...], r.d_pre[:, WIDTH // 2:WIDTH]).astype(BF16)
    r.e_part[0, 1] = r.grad_out[:, :WIDTH // 2].astype(BF16)
    r.e_part[1, 1] = r.grad_out[:, WIDTH // 2:].astype(BF16)

    def reduction(name, sem_at):
        part, got_core, sums, got, red, full = (
            getattr(r, name + tail) for tail in ("_part", "_core", "_sum", "_got", "_red", "_full")
        )
        send = [r.red_send.at[sem_at + k] for k in range(4)]
        recv = [r.red_recv.at[sem_at + k] for k in range(4)]
        rest = pl.ds(0, n_chips - 1)
        height = sums.shape[1]

        def to_core():
            copy_to(part.at[1 - core], got_core, send[0], recv[0], mate)

        def spread():
            await_bytes(got_core, recv[0])

            @pl.loop(0, n_seq, unroll=4)
            def _(i):
                at = aligned(i * height, height)
                for z in range(2):
                    sums[z * n_seq + i] = (
                        part[core, z, at].astype(F32) + got_core[z, at].astype(F32)
                    ).astype(BF16)

            @pl.loop(1, n_chips)
            def _(step):
                slot = lax.rem(mine + step, n_chips)
                copy_to(sums.at[slot], got.at[mine], send[1], recv[1], chip(slot))

            got[mine] = sums[mine]

        def collect():
            await_bytes(got.at[rest], recv[1])
            red[...] = jnp.sum(got[...].astype(F32), axis=0).astype(BF16)

            @pl.loop(1, n_chips)
            def _(step):
                slot = lax.rem(mine + step, n_chips)
                copy_to(red, full.at[core, mine], send[2], recv[2], chip(slot))

            full[core, mine] = red[...]

        def share():
            await_bytes(full.at[0, rest], recv[2])
            copy_to(full.at[core], full.at[core], send[3], recv[3], mate)

        def finish():
            await_bytes(full.at[0], recv[3])
            await_bytes(part.at[0], send[0])
            await_bytes(sums.at[rest], send[1])
            await_bytes(full.at[0, rest], send[2])
            await_bytes(full.at[0], send[3])

        def written(at, ref, col):
            width = full.shape[-1]
            ref[:, col:col + width] = full[
                at % 2, at // 2 * n_seq:(at // 2 + 1) * n_seq
            ].reshape(n_seq * height, width)

        return types.SimpleNamespace(
            to_core=to_core, spread=spread, collect=collect, share=share, finish=finish, written=written
        )

    early = reduction("e", 0)
    early.to_core()
    copy_to(r.loss, r.loss_core, r.loss_sem.at[0], r.loss_sem.at[1], mate)

    @pl.loop(0, n_seq)
    def _(step):
        i = lax.rem(me + step, n_seq)

        @pl.when(i != me)
        def _():
            await_bytes(r.datt_got.at[0], r.datt_sem.at[i])

    @pl.loop(0, n_seq, unroll=4)
    def _(i):
        d_att = r.datt_got[i].astype(F32)
        rows = aligned(i * BLOCK, BLOCK)
        qa = r.qa[rows].astype(F32)
        r.qa[rows] = jnp.where(
            low_block, qa, jnp.concatenate([turned(d_att), d_att], axis=0)
        ).astype(BF16)

    r.dq[...] = jnp.zeros_like(r.dq)
    b_tiles = length // BM
    b_per = BM // BLOCK
    t_tiles = length // BT
    kv_scale = jnp.where(low_lanes((1, 2 * HEAD)), 0.5 * inv_len, inv_len)

    @pl.loop(0, b_tiles)
    def _(step):
        c = lax.rem(me // b_per + step, b_tiles)
        m_rows = aligned(c * BM, BM)
        low_tile = low_lanes((BM, 2 * HEAD))

        def piece(at, masked):
            t_rows = aligned(at * BT, BT)
            qa = r.qa[t_rows]
            half = dot_nt(r.k0[m_rows], qa)
            d_probs = dot_nt(r.v0[m_rows], qa)
            if masked:
                ahead = c * BM - at * BT + lax.broadcasted_iota(
                    jnp.int32, (BM, BT), 0
                ) - lax.broadcasted_iota(jnp.int32, (BM, BT), 1)
                half = jnp.where(ahead <= 0, half, 0.0)
                d_probs = jnp.where(ahead <= 0, d_probs, 0.0)
            up = 1.0 + jnp.tanh(half)
            probs = half * up
            d_scores = (d_probs * up * (1.0 + (half + half) - probs)).astype(BF16)
            r.dq[:, t_rows] += dot_nn(r.kt[:, m_rows], d_scores)
            return jnp.where(low_tile, dot_nn(d_scores, qa), dot_nn(probs.astype(BF16), qa))

        first = c * BM // BT
        r.dkv[...] = piece(first, True)

        @pl.loop(first + 1, t_tiles)
        def _(at):
            r.dkv[...] += piece(at, False)

        for u in range(b_per):
            r.grad_send[c * b_per + u, :BLOCK] = (
                r.dkv[u * BLOCK:(u + 1) * BLOCK] * kv_scale
            ).astype(BF16)

        @pl.loop(0, b_per)
        def _(turn):
            i = c * b_per + lax.rem(me + turn, b_per)

            @pl.when(i != me)
            def _():
                copy_to(
                    r.grad_send.at[i, pl.ds(0, BLOCK)], r.grad_got.at[me, pl.ds(0, BLOCK)],
                    r.send_sem.at[10], r.grad_sem.at[0], {"seq": i},
                )

            @pl.when(i == me)
            def _():
                r.grad_got[me, :BLOCK] = r.grad_send[me, :BLOCK]

        @pl.when(step == 0)
        def _():
            early.spread()
            await_bytes(r.loss_core, r.loss_sem.at[1])
            r.loss_sum[...] = r.loss[...] + r.loss_core[...]
            r.loss_all[mine] = r.loss_sum[...]

            @pl.loop(1, n_chips)
            def _(turn):
                slot = lax.rem(mine + turn, n_chips)
                copy_to(
                    r.loss_sum, r.loss_all.at[mine], r.loss_sem.at[2], r.loss_sem.at[3], chip(slot)
                )

        @pl.when(step == b_tiles // 2)
        def _():
            early.collect()

    @pl.loop(0, b_tiles)
    def _(step):
        c = lax.rem(me // b_per + step, b_tiles)
        for u in range(b_per):
            d_q = r.dq[:, aligned((c * b_per + u) * BLOCK, BLOCK)] * (0.5 * inv_len)
            r.grad_send[c * b_per + u, BLOCK:] = d_q.astype(BF16)

        @pl.loop(0, b_per)
        def _(turn):
            i = c * b_per + lax.rem(me + turn, b_per)

            @pl.when(i != me)
            def _():
                copy_to(
                    r.grad_send.at[i, pl.ds(BLOCK, HEAD)], r.grad_got.at[me, pl.ds(BLOCK, HEAD)],
                    r.send_sem.at[11], r.grad_sem.at[1], {"seq": i},
                )

            @pl.when(i == me)
            def _():
                r.grad_got[me, BLOCK:] = r.grad_send[me, BLOCK:]

    later = reduction("l", 4)
    last = reduction("q", 8)
    await_bytes(r.grad_got.at[others, pl.ds(0, BLOCK)], r.grad_sem.at[0])

    @pl.loop(0, n_here)
    def _(b):
        rows = aligned(b * BLOCK, BLOCK)
        for pair in range(PAIRS):
            j = b * HEADS + 2 * pair
            d_k, d_v = swapped(r.grad_got[j, :BLOCK].astype(F32), r.grad_got[j + 1, :BLOCK].astype(F32))
            for part, grad in ((1, d_v), (3, d_k)):
                at = part * WIDTH + pair * 2 * HEAD
                slope = r.slope[b, :, at:at + 2 * HEAD].astype(F32)
                r.d_pre[rows, at:at + 2 * HEAD] = (grad * slope).astype(BF16)

    for at, low_col in enumerate((1, 1.5, 3, 3.5)):
        col = int(low_col * WIDTH)
        r.l_part[at % 2, at // 2] = dot_nn(r.xnt[...], r.d_pre[:, col:col + WIDTH // 2]).astype(BF16)
    later.to_core()
    await_bytes(r.grad_got.at[others, pl.ds(BLOCK, HEAD)], r.grad_sem.at[1])

    @pl.loop(0, n_here)
    def _(b):
        rows = aligned(b * BLOCK, BLOCK)
        for pair in range(PAIRS):
            j = b * HEADS + 2 * pair
            at = 2 * WIDTH + pair * 2 * HEAD
            grad = jnp.transpose(
                jnp.concatenate([r.grad_got[j + e, BLOCK:].astype(F32) for e in range(2)], axis=0)
            )
            slope = r.slope[b, :, at:at + 2 * HEAD].astype(F32)
            r.d_pre[rows, at:at + 2 * HEAD] = (grad * slope).astype(BF16)

    later.spread()
    q_grad = dot_nn(r.xnt[...], r.d_pre[:, 2 * WIDTH:3 * WIDTH]).astype(BF16)
    for at in range(4):
        r.q_part[at % 2, at // 2] = q_grad[:, at * BLOCK:(at + 1) * BLOCK]
    last.to_core()
    early.share()
    last.spread()
    later.collect()
    last.collect()

    await_bytes(r.loss_all.at[pl.ds(0, n_chips - 1)], r.loss_sem.at[3])
    r.loss_out[...] = jnp.sum(r.loss_all[...], axis=0)
    early.finish()
    for at in range(2):
        early.written(at, r.joined, at * WIDTH // 2)
        early.written(2 + at, r.out, at * WIDTH // 2)
    later.share()
    last.share()
    later.finish()
    for at, low_col in enumerate((1, 1.5, 3, 3.5)):
        later.written(at, r.joined, int(low_col * WIDTH))
    last.finish()
    for at in range(4):
        last.written(at, r.joined, 2 * WIDTH + at * BLOCK)

    await_bytes(r.first, r.send_sem.at[1])
    await_bytes(r.ids, r.send_sem.at[2])
    for at in (3, 5, 8):
        await_bytes(r.negs.at[0], r.send_sem.at[at])
        await_bytes(r.all_ids.at[0], r.send_sem.at[at + 1])
    await_bytes(r.att_send.at[others], r.send_sem.at[7])
    await_bytes(r.datt_send.at[others], r.send_sem.at[12])
    await_bytes(r.grad_send.at[others, pl.ds(0, BLOCK)], r.send_sem.at[10])
    await_bytes(r.grad_send.at[others, pl.ds(BLOCK, HEAD)], r.send_sem.at[11])
    await_bytes(r.loss, r.loss_sem.at[0])
    await_bytes(r.loss_all.at[pl.ds(0, n_chips - 1)], r.loss_sem.at[2])


def activated(r, b, xn, part):
    half = 0.5 * dot_nn(xn, r.w_joined[:, part * WIDTH:(part + 1) * WIDTH])
    th = jnp.tanh(half)
    slope = (0.5 + 0.5 * th) * (1.0 + half * (1.0 - th))
    r.slope[b, :, part * WIDTH:(part + 1) * WIDTH] = slope.astype(BF16)
    return half + half * th


def middle(r, n_seq, me, grp, first_b, weight):
    both = 2
    rows = both * BLOCK
    n_here = r.x.shape[0]
    n_grp, n_neg = r.negs.shape[:2]

    def joined(make):
        return jnp.concatenate([make(e) for e in range(both)], axis=0)

    @pl.loop(0, both * HEADS)
    def _(turn):
        j = first_b * HEADS + turn

        @pl.when(j != me)
        def _():
            await_bytes(r.att_got.at[0], r.att_sem.at[j])

    for e in range(both):
        for pair in range(PAIRS):
            j = (first_b + e) * HEADS + 2 * pair
            top, bottom = swapped(r.att_got[j].astype(F32), r.att_got[j + 1].astype(F32))
            r.att[e * BLOCK:e * BLOCK + HEAD, pair_cols(pair)] = top
            r.att[e * BLOCK + HEAD:(e + 1) * BLOCK, pair_cols(pair)] = bottom

    att = r.att[...]
    centered = att - jnp.mean(att, axis=-1, keepdims=True)
    inv_att = lax.rsqrt(jnp.mean(centered * centered, axis=-1, keepdims=True) + eps_norm)
    normed = centered * inv_att
    u = joined(lambda e: r.u[first_b + e]).astype(F32)
    gated = (normed * u).astype(BF16)
    x = joined(lambda e: r.x[first_b + e]).astype(F32)
    out_rows = x + dot_nn(gated, r.w_out[...])
    inv_y = lax.rsqrt(jnp.sum(out_rows * out_rows, axis=-1, keepdims=True) + eps_norm)
    unit_y = out_rows * inv_y
    unit_b = unit_y.astype(BF16)
    more = jnp.where(me == n_seq - 1, 0, 1)
    last_row = lax.broadcasted_iota(jnp.int32, (BLOCK, WIDTH), 0) == BLOCK - 1
    last_lane = lax.broadcasted_iota(jnp.int32, (1, BLOCK), 1) == BLOCK - 1

    def next_rows(e):
        shifted = pltpu.roll(r.x[first_b + e].astype(F32), BLOCK - 1, axis=0)
        return jnp.where(last_row, r.first[first_b + e].astype(F32)[:1] * more.astype(F32), shifted)

    x_next = joined(next_rows)
    pos_unit = (
        x_next * lax.rsqrt(jnp.sum(x_next * x_next, axis=-1, keepdims=True) + eps_norm)
    ).astype(BF16).astype(F32)
    pos_logit = logit_scale * jnp.sum(unit_b.astype(F32) * pos_unit, axis=-1, keepdims=True)

    def row_ids(e):
        shifted = pltpu.roll(r.ids[pl.ds(first_b + e, 1)], BLOCK - 1, axis=1)
        coming = pltpu.roll(r.next_ids[pl.ds(first_b + e, 1)], BLOCK - 1, axis=1) * more
        return jnp.transpose(jnp.broadcast_to(jnp.where(last_lane, coming, shifted), (BLOCK, BLOCK)))

    ids = joined(row_ids)
    lane_sum = jnp.zeros((rows, BLOCK), F32)
    for g in range(n_grp):
        neg_logit = logit_scale * dot_nt(unit_b, r.negs[g])
        for sub in range(n_neg // BLOCK):
            at = (g * n_neg) + sub * BLOCK
            hit = r.all_ids[g, n_here + sub:n_here + sub + 1] == ids
            exps = jnp.where(hit, 0.0, jnp.exp(neg_logit[:, sub * BLOCK:(sub + 1) * BLOCK]))
            r.exps[:, at:at + BLOCK] = exps
            lane_sum = lane_sum + exps
    pos_exp = jnp.exp(pos_logit)
    denom = pos_exp + jnp.sum(lane_sum, axis=-1, keepdims=True)

    def row_valid(e):
        pos = me * BLOCK + lax.broadcasted_iota(jnp.int32, (BLOCK, 1), 0)
        return jnp.where(pos + 1 < r.lens[grp * n_here + first_b + e], 1.0, 0.0)

    valid = joined(row_valid)
    row_loss = jnp.where(valid > 0.0, jnp.log(denom) - pos_logit, 0.0)
    r.loss[...] += jnp.broadcast_to(jnp.sum(row_loss, axis=0, keepdims=True), r.loss.shape)
    row_weight = valid * weight
    d_pos = row_weight * (pos_exp / denom - 1.0)
    scale = row_weight / denom
    neg_back = jnp.zeros((rows, WIDTH), F32)
    for g in range(n_grp):
        d_neg = (scale * r.exps[:, g * n_neg:(g + 1) * n_neg]).astype(BF16)
        neg_back = neg_back + dot_nn(d_neg, r.negs[g])
    d_unit = logit_scale * (d_pos * pos_unit + neg_back)
    d_out = (
        (d_unit - unit_y * jnp.sum(unit_y * d_unit, axis=-1, keepdims=True)) * inv_y
    ).astype(BF16)
    d_gate = dot_nt(d_out, r.w_out[...])
    d_norm = d_gate * u
    d_att = inv_att * (
        d_norm
        - jnp.mean(d_norm, axis=-1, keepdims=True)
        - normed * jnp.mean(d_norm * normed, axis=-1, keepdims=True)
    )
    for e in range(both):
        rows_e = d_att[e * BLOCK:(e + 1) * BLOCK]
        for pair in range(PAIRS):
            cols = pair_cols(pair)
            packed = swapped(rows_e[:HEAD, cols], rows_e[HEAD:, cols])
            for odd in range(2):
                r.datt_send[(first_b + e) * HEADS + 2 * pair + odd] = packed[odd].astype(BF16)

    @pl.loop(0, both * HEADS)
    def _(turn):
        j = first_b * HEADS + lax.rem(me + turn, both * HEADS)

        @pl.when(j != me)
        def _():
            copy_to(
                r.datt_send.at[j], r.datt_got.at[me], r.send_sem.at[12], r.datt_sem.at[me], {"seq": j}
            )

        @pl.when(j == me)
        def _():
            r.datt_got[me] = r.datt_send[me]

    r.grad_out[...] += dot_tn(gated, d_out)
    d_u = d_gate * normed
    for e in range(both):
        slope = r.slope[first_b + e, :, :WIDTH].astype(F32)
        r.d_pre[aligned((first_b + e) * BLOCK, BLOCK), :WIDTH] = (
            d_u[e * BLOCK:(e + 1) * BLOCK] * slope
        ).astype(BF16)


def local(inputs, history, lengths, w_joined, w_out, neg_emb, neg_ids):
    n_here, block, width = inputs.shape
    n_seq = lax.axis_size("seq")
    length = n_seq * block
    lanes = 2 * HEAD
    rows = n_here * block
    n_neg = neg_emb.shape[0]
    chips = 2 * n_seq
    strip = width // n_seq
    dma = pltpu.SemaphoreType.DMA
    buffers = dict(
        xn=((n_here, block, width), BF16), xnt=((width, rows), BF16), u=((n_here, block, width), BF16),
        slope=((n_here, block, 4 * width), BF16), d_pre=((rows, 4 * width), BF16),
        send=((n_seq, BLOCK + HEAD, lanes), BF16), got=((n_seq, BLOCK + HEAD, lanes), BF16),
        att_send=((n_seq, HEAD, lanes), BF16), att_got=((n_seq, HEAD, lanes), BF16),
        datt_send=((n_seq, HEAD, lanes), BF16), datt_got=((n_seq, HEAD, lanes), BF16),
        grad_send=((n_seq, BLOCK + HEAD, lanes), BF16), grad_got=((n_seq, BLOCK + HEAD, lanes), BF16),
        first=((n_here, 16, width), BF16), ids=((2 * n_here, block), jnp.int32),
        next_ids=((2 * n_here, block), jnp.int32), negs=((4, n_neg, width), BF16),
        all_ids=((4, 2 * n_here, block), jnp.int32),
        k0=((length, lanes), BF16), v0=((length, lanes), BF16), qa=((length, lanes), BF16),
        kt=((HEAD, length), BF16), acc=((FQ, lanes), F32), dq=((HEAD, length), F32), dkv=((BM, lanes), F32),
        att=((2 * block, width), F32), exps=((2 * block, 4 * n_neg), F32), grad_out=((width, width), F32),
        loss=((8, block), F32), loss_core=((8, block), F32), loss_sum=((8, block), F32),
        loss_all=((chips, 8, block), F32),
    )
    for name, cols in (("e", 2 * width // 4), ("l", 2 * width // 4), ("q", width // 4)):
        buffers[name + "_part"] = ((2, 2, width, cols), BF16)
        buffers[name + "_core"] = ((2, width, cols), BF16)
        buffers[name + "_sum"] = ((chips, strip, cols), BF16)
        buffers[name + "_got"] = ((chips, strip, cols), BF16)
        buffers[name + "_red"] = ((strip, cols), BF16)
        buffers[name + "_full"] = ((2, chips, strip, cols), BF16)
    sems = dict(
        send_sem=13, one_sem=8, got_sem=n_seq, att_sem=n_seq, datt_sem=n_seq, grad_sem=2, loss_sem=4,
        red_send=12, red_recv=12,
    )
    takes = ("lens", "x", "history", "neg_ids", "w_joined", "w_out", "neg_emb")
    gives = dict(
        joined=((width, 4 * width), BF16), out=((width, width), BF16), loss_out=((8, block), F32)
    )
    names = takes + tuple(gives) + tuple(buffers) + tuple(sems)
    joined, out, loss = pl.pallas_call(
        functools.partial(kernel, n_seq, names),
        out_shape=[jax.ShapeDtypeStruct(*kind) for kind in gives.values()],
        in_specs=[SMEM] + [VMEM] * (len(takes) - 1),
        out_specs=[VMEM] * len(gives),
        scratch_shapes=[pltpu.VMEM(*kind) for kind in buffers.values()]
        + [dma((count,)) for count in sems.values()],
        compiler_params=pltpu.CompilerParams(
            collective_id=0, has_side_effects=True, vmem_limit_bytes=60 * 1024 * 1024
        ),
    )(lengths, inputs, history, neg_ids.reshape(-1, block), w_joined, w_out, neg_emb)
    target_count = jnp.sum(lengths - 1).astype(F32)
    return (joined.astype(F32), out.astype(F32), loss[0, 0] / target_count)


def solution(mesh):
    placed = (
        P("grp", "seq", None),
        P("grp", "seq"),
        P(),
        P(),
        P(),
        P(("grp", "seq"), None),
        P(("grp", "seq")),
    )
    return jax.shard_map(
        local, mesh=mesh, in_specs=placed, out_specs=(P(), P(), P()), check_vma=False
    )
```

```python
import functools
import types

import jax
import jax.numpy as jnp
from jax import lax
from jax.experimental import pallas as pl
from jax.experimental.pallas import tpu as pltpu
from jax.sharding import PartitionSpec as P

HEADS = 8
HEAD = 64
WIDTH = 512
PAIRS = 4
BLOCK = 128
TILE = 512
FQ = TILE
BM = TILE
eps_norm = 1e-06
logit_scale = 64.0

MESH = pl.DeviceIdType.MESH
F32 = jnp.float32
BF16 = jnp.bfloat16
VMEM = pl.BlockSpec(memory_space=pltpu.VMEM)
SMEM = pl.BlockSpec(memory_space=pltpu.SMEM)


def dot_nn(a, b):
    return lax.dot_general(a, b, (((1,), (0,)), ((), ())), preferred_element_type=F32)


def dot_nt(a, b):
    return lax.dot_general(a, b, (((1,), (1,)), ((), ())), preferred_element_type=F32)


def dot_tn(a, b):
    return lax.dot_general(a, b, (((0,), (0,)), ((), ())), preferred_element_type=F32)


def low_lanes(shape):
    return lax.broadcasted_iota(jnp.int32, shape, 1) < HEAD


def turned(a):
    return pltpu.roll(a, HEAD, axis=1)


def swapped(a, b):
    low = low_lanes(a.shape)
    return jnp.where(low, a, turned(b)), jnp.where(low, turned(a), b)


def copy_to(src, dst, send_sem, recv_sem, where):
    pltpu.make_async_remote_copy(
        src_ref=src, dst_ref=dst, send_sem=send_sem, recv_sem=recv_sem,
        device_id=where, device_id_type=MESH,
    ).start()


def await_bytes(ref, sem):
    pltpu.make_async_copy(ref, ref, sem).wait()


def aligned(at, size):
    return pl.ds(pl.multiple_of(at, size), size)


def pair_cols(pair):
    return slice(pair * 2 * HEAD, (pair + 1) * 2 * HEAD)


def shifts(n_seq):
    side = int((n_seq // 2) ** 0.5)
    steps = [(x, y, z) for x in range(side) for y in range(side) for z in range(2)]
    return sorted(steps[1:], key=lambda at: -(min(at[0], side - at[0]) + min(at[1], side - at[1]) + at[2]))


def peer(me, shift):
    x, y, z = me // HEADS, lax.rem(me // 2, 4), lax.rem(me, 2)
    return (lax.rem(x + shift[0], 4) * 4 + lax.rem(y + shift[1], 4)) * 2 + lax.rem(z + shift[2], 2)


def cover(first, count, body):
    done = 0
    for tiles in (4, 2, 1):
        n = count // tiles if tiles == 4 else lax.rem(count // tiles, 2)

        @pl.loop(0, n)
        def _(at, done=done, tiles=tiles):
            body((first + done + at * tiles) * TILE, tiles * TILE)

        done = done + n * tiles


def kernel(n_seq, names, *refs):
    r = types.SimpleNamespace(**dict(zip(names, refs, strict=True)))
    me = lax.axis_index("seq")
    grp = lax.axis_index("grp")
    core, z_hi = lax.rem(grp, 2), grp // 2
    n_here = r.x.shape[0]
    planes = n_seq // HEADS
    length = n_seq * BLOCK
    n_chips = 2 * n_seq
    mine = z_hi * n_seq + me
    mate = {"grp": grp + 1 - 2 * core}
    other_z = {"grp": (1 - z_hi) * 2 + core}
    others = pl.ds(0, n_seq - 1)

    def chip(slot):
        return {"grp": slot // n_seq * 2 + core, "seq": lax.rem(slot, n_seq)}

    barrier = pltpu.get_barrier_semaphore()
    pl.semaphore_signal(barrier, inc=1, device_id=mate, device_id_type=MESH)

    @pl.loop(1, n_chips)
    def _(step):
        pl.semaphore_signal(
            barrier, inc=1, device_id=chip(lax.rem(mine + step, n_chips)), device_id_type=MESH
        )

    @pl.loop(0, n_here)
    def _(b):
        x = r.x[b].astype(F32)
        centered = x - jnp.mean(x, axis=-1, keepdims=True)
        var = jnp.mean(centered * centered, axis=-1, keepdims=True)
        xn = (centered * lax.rsqrt(var + eps_norm)).astype(BF16)
        r.xn[b] = xn
        v, q, k = (activated(r, b, xn, part) for part in (1, 2, 3))
        for pair in range(PAIRS):
            cols = pair_cols(pair)
            kv = swapped(k[:, cols], v[:, cols])
            qs = swapped(q[:HEAD, cols], q[HEAD:, cols])
            for odd in range(2):
                j = b * HEADS + 2 * pair + odd
                r.send[j, :BLOCK] = kv[odd].astype(BF16)
                r.send[j, BLOCK:] = qs[odd].astype(BF16)

    pl.semaphore_wait(barrier, n_chips)
    for shift in shifts(n_seq):
        j = peer(me, shift)
        copy_to(r.send.at[j], r.got.at[me], r.send_sem.at[0], r.got_sem.at[me], {"seq": j})
    r.got[me] = r.send[me]

    before = {"seq": lax.rem(me + n_seq - 1, n_seq)}
    r.ids[:n_here] = r.history[...]
    r.ids[n_here:] = r.neg_ids[...]
    copy_to(r.x.at[:, pl.ds(0, 16)], r.first, r.send_sem.at[1], r.one_sem.at[0], before)
    copy_to(r.ids, r.next_ids, r.send_sem.at[2], r.one_sem.at[1], before)

    @pl.loop(0, n_here)
    def _(b):
        xn = r.xn[b]
        r.u[b] = activated(r, b, xn, 0).astype(BF16)
        r.xnt[:, aligned(b * BLOCK, BLOCK)] = jnp.transpose(xn.astype(F32)).astype(BF16)
        rows = aligned(b * BLOCK, BLOCK)
        emb = r.neg_emb[rows].astype(F32)
        r.negs[grp, rows] = (
            emb * lax.rsqrt(jnp.sum(emb * emb, axis=-1, keepdims=True) + eps_norm)
        ).astype(BF16)

    r.all_ids[grp] = r.ids[...]

    seq_len = r.lens[grp * n_here + me // HEADS]
    low = low_lanes((HEAD, 2 * HEAD))
    low_block = low_lanes((BLOCK, 2 * HEAD))

    @pl.loop(0, planes)
    def _(step):
        first = lax.rem(me // HEADS + planes // 2 + step, planes) * HEADS

        @pl.loop(0, HEADS)
        def _(turn):
            i = first + turn

            @pl.when(i != me)
            def _():
                await_bytes(r.got.at[0], r.got_sem.at[i])

        @pl.loop(0, HEADS, unroll=4)
        def _(turn):
            i = first + turn
            rows = aligned(i * BLOCK, BLOCK)
            pos = i * BLOCK + lax.broadcasted_iota(jnp.int32, (BLOCK, 2 * HEAD), 0)
            kv = jnp.where(pos < seq_len, r.got[i, :BLOCK].astype(F32), 0.0)
            r.k0[rows] = jnp.where(low_block, 0.5 * kv, 0.0).astype(BF16)
            r.v0[rows] = jnp.where(low_block, 0.0, kv).astype(BF16)
            r.kt[:, rows] = jnp.transpose(kv)[:HEAD].astype(BF16)
            q = r.got[i, BLOCK:].astype(F32)
            r.qa[rows] = jnp.concatenate(
                [jnp.where(low, q, 0.0), jnp.where(low, turned(q), 0.0)], axis=0
            ).astype(BF16)

    copy_to(r.negs.at[grp], r.negs.at[grp], r.send_sem.at[3], r.one_sem.at[2], mate)
    copy_to(r.all_ids.at[grp], r.all_ids.at[grp], r.send_sem.at[4], r.one_sem.at[3], mate)
    copy_to(r.negs.at[grp], r.negs.at[grp], r.send_sem.at[5], r.one_sem.at[4], other_z)
    copy_to(r.all_ids.at[grp], r.all_ids.at[grp], r.send_sem.at[6], r.one_sem.at[5], other_z)
    await_bytes(r.send.at[others], r.send_sem.at[0])
    inv_len = 1.0 / jnp.full((1, 2 * HEAD), seq_len, jnp.int32).astype(F32)

    f_tiles = length // FQ
    f_per = FQ // BLOCK

    @pl.loop(0, f_tiles)
    def _(step):
        c = lax.rem(me // f_per + step, f_tiles)
        q = r.qa[aligned(c * FQ, FQ)]

        def piece(start, size, masked):
            rows = pl.ds(pl.multiple_of(start, TILE), size)
            half = dot_nt(q, r.k0[rows])
            if masked:
                ahead = lax.broadcasted_iota(jnp.int32, (FQ, size), 1) - lax.broadcasted_iota(
                    jnp.int32, (FQ, size), 0
                )
                half = jnp.where(ahead <= 0, half, 0.0)
            probs = (half + half * jnp.tanh(half)).astype(BF16)
            return dot_nn(probs, r.v0[rows])

        r.acc[...] = piece(c * FQ, FQ, True)

        def more(start, size):
            r.acc[...] += piece(start, size, False)

        cover(0, c, more)
        for u in range(f_per):
            out = r.acc[u * BLOCK:(u + 1) * BLOCK] * inv_len
            top, bottom = out[:HEAD], out[HEAD:]
            r.att_send[c * f_per + u] = jnp.where(low, turned(top), bottom).astype(BF16)

        @pl.loop(0, f_per)
        def _(turn):
            i = c * f_per + lax.rem(me + turn, f_per)

            @pl.when(i != me)
            def _():
                copy_to(
                    r.att_send.at[i], r.att_got.at[me], r.send_sem.at[7], r.att_sem.at[me], {"seq": i}
                )

            @pl.when(i == me)
            def _():
                r.att_got[me] = r.att_send[me]

    far = (1 - z_hi) * 2 + core
    await_bytes(r.negs.at[0], r.one_sem.at[4])
    await_bytes(r.all_ids.at[0], r.one_sem.at[5])
    copy_to(r.negs.at[far], r.negs.at[far], r.send_sem.at[8], r.one_sem.at[6], mate)
    copy_to(r.all_ids.at[far], r.all_ids.at[far], r.send_sem.at[9], r.one_sem.at[7], mate)

    total = r.lens[0] - 1
    for at in range(1, r.lens.shape[0]):
        total = total + (r.lens[at] - 1)
    both = 2
    half_rows = both * BLOCK
    weight = 1.0 / jnp.full((half_rows, 1), total, jnp.int32).astype(F32)
    r.grad_out[...] = jnp.zeros_like(r.grad_out)
    r.loss[...] = jnp.zeros_like(r.loss)
    await_bytes(r.first, r.one_sem.at[0])
    await_bytes(r.ids, r.one_sem.at[1])
    await_bytes(r.negs.at[0], r.one_sem.at[2])
    await_bytes(r.all_ids.at[0], r.one_sem.at[3])
    await_bytes(r.negs.at[0], r.one_sem.at[6])
    await_bytes(r.all_ids.at[0], r.one_sem.at[7])
    n_halves = n_here // both

    @pl.loop(0, n_halves)
    def _(step):
        middle(r, n_seq, me, grp, both * lax.rem(me // (both * HEADS) + step, n_halves), weight)

    r.e_part[0, 0] = dot_nn(r.xnt[...], r.d_pre[:, :WIDTH // 2]).astype(BF16)
    r.e_part[1, 0] = dot_nn(r.xnt[...], r.d_pre[:, WIDTH // 2:WIDTH]).astype(BF16)
    r.e_part[0, 1] = r.grad_out[:, :WIDTH // 2].astype(BF16)
    r.e_part[1, 1] = r.grad_out[:, WIDTH // 2:].astype(BF16)

    def reduction(name, sem_at):
        part, got_core, sums, got, red, full = (
            getattr(r, name + tail) for tail in ("_part", "_core", "_sum", "_got", "_red", "_full")
        )
        send = [r.red_send.at[sem_at + k] for k in range(4)]
        recv = [r.red_recv.at[sem_at + k] for k in range(4)]
        rest = pl.ds(0, n_chips - 1)
        height = sums.shape[1]

        def to_core():
            copy_to(part.at[1 - core], got_core, send[0], recv[0], mate)

        def spread():
            await_bytes(got_core, recv[0])

            @pl.loop(0, n_seq, unroll=4)
            def _(i):
                at = aligned(i * height, height)
                for z in range(2):
                    sums[z * n_seq + i] = (
                        part[core, z, at].astype(F32) + got_core[z, at].astype(F32)
                    ).astype(BF16)

            @pl.loop(1, n_chips)
            def _(step):
                slot = lax.rem(mine + step, n_chips)
                copy_to(sums.at[slot], got.at[mine], send[1], recv[1], chip(slot))

            got[mine] = sums[mine]

        def collect():
            await_bytes(got.at[rest], recv[1])
            red[...] = jnp.sum(got[...].astype(F32), axis=0).astype(BF16)

            @pl.loop(1, n_chips)
            def _(step):
                slot = lax.rem(mine + step, n_chips)
                copy_to(red, full.at[core, mine], send[2], recv[2], chip(slot))

            full[core, mine] = red[...]

        def share():
            await_bytes(full.at[0, rest], recv[2])
            copy_to(full.at[core], full.at[core], send[3], recv[3], mate)

        def finish():
            await_bytes(full.at[0], recv[3])
            await_bytes(part.at[0], send[0])
            await_bytes(sums.at[rest], send[1])
            await_bytes(full.at[0, rest], send[2])
            await_bytes(full.at[0], send[3])

        def written(at, ref, col):
            width = full.shape[-1]
            ref[:, col:col + width] = full[
                at % 2, at // 2 * n_seq:(at // 2 + 1) * n_seq
            ].reshape(n_seq * height, width)

        return types.SimpleNamespace(
            to_core=to_core, spread=spread, collect=collect, share=share, finish=finish, written=written
        )

    early = reduction("e", 0)
    early.to_core()
    copy_to(r.loss, r.loss_core, r.loss_sem.at[0], r.loss_sem.at[1], mate)

    @pl.loop(0, n_seq)
    def _(step):
        i = lax.rem(me + step, n_seq)

        @pl.when(i != me)
        def _():
            await_bytes(r.datt_got.at[0], r.datt_sem.at[i])

    @pl.loop(0, n_seq, unroll=4)
    def _(i):
        d_att = r.datt_got[i].astype(F32)
        rows = aligned(i * BLOCK, BLOCK)
        qa = r.qa[rows].astype(F32)
        r.qa[rows] = jnp.where(
            low_block, qa, jnp.concatenate([turned(d_att), d_att], axis=0)
        ).astype(BF16)

    r.dq[...] = jnp.zeros_like(r.dq)
    b_tiles = length // BM
    b_per = BM // BLOCK
    kv_scale = jnp.where(low_lanes((1, 2 * HEAD)), 0.5 * inv_len, inv_len)

    @pl.loop(0, b_tiles)
    def _(step):
        c = lax.rem(me // b_per + step, b_tiles)
        m_rows = aligned(c * BM, BM)
        low_tile = low_lanes((BM, 2 * HEAD))

        def piece(start, size, masked):
            t_rows = pl.ds(pl.multiple_of(start, TILE), size)
            qa = r.qa[t_rows]
            half = dot_nt(r.k0[m_rows], qa)
            d_probs = dot_nt(r.v0[m_rows], qa)
            if masked:
                ahead = lax.broadcasted_iota(jnp.int32, (BM, size), 0) - lax.broadcasted_iota(
                    jnp.int32, (BM, size), 1
                )
                half = jnp.where(ahead <= 0, half, 0.0)
                d_probs = jnp.where(ahead <= 0, d_probs, 0.0)
            up = 1.0 + jnp.tanh(half)
            probs = half * up
            d_scores = (d_probs * up * (1.0 + (half + half) - probs)).astype(BF16)
            r.dq[:, t_rows] += dot_nn(r.kt[:, m_rows], d_scores)
            return jnp.where(low_tile, dot_nn(d_scores, qa), dot_nn(probs.astype(BF16), qa))

        r.dkv[...] = piece(c * BM, BM, True)

        def more(start, size):
            r.dkv[...] += piece(start, size, False)

        cover(c + 1, b_tiles - 1 - c, more)
        for u in range(b_per):
            r.grad_send[c * b_per + u, :BLOCK] = (
                r.dkv[u * BLOCK:(u + 1) * BLOCK] * kv_scale
            ).astype(BF16)

        @pl.loop(0, b_per)
        def _(turn):
            i = c * b_per + lax.rem(me + turn, b_per)

            @pl.when(i != me)
            def _():
                copy_to(
                    r.grad_send.at[i, pl.ds(0, BLOCK)], r.grad_got.at[me, pl.ds(0, BLOCK)],
                    r.send_sem.at[10], r.grad_sem.at[0], {"seq": i},
                )

            @pl.when(i == me)
            def _():
                r.grad_got[me, :BLOCK] = r.grad_send[me, :BLOCK]

        @pl.when(step == 0)
        def _():
            early.spread()
            await_bytes(r.loss_core, r.loss_sem.at[1])
            r.loss_sum[...] = r.loss[...] + r.loss_core[...]
            r.loss_all[mine] = r.loss_sum[...]

            @pl.loop(1, n_chips)
            def _(turn):
                slot = lax.rem(mine + turn, n_chips)
                copy_to(
                    r.loss_sum, r.loss_all.at[mine], r.loss_sem.at[2], r.loss_sem.at[3], chip(slot)
                )

        @pl.when(step == b_tiles // 2)
        def _():
            early.collect()

    @pl.loop(0, b_tiles)
    def _(step):
        c = lax.rem(me // b_per + step, b_tiles)
        for u in range(b_per):
            d_q = r.dq[:, aligned((c * b_per + u) * BLOCK, BLOCK)] * (0.5 * inv_len)
            r.grad_send[c * b_per + u, BLOCK:] = d_q.astype(BF16)

        @pl.loop(0, b_per)
        def _(turn):
            i = c * b_per + lax.rem(me + turn, b_per)

            @pl.when(i != me)
            def _():
                copy_to(
                    r.grad_send.at[i, pl.ds(BLOCK, HEAD)], r.grad_got.at[me, pl.ds(BLOCK, HEAD)],
                    r.send_sem.at[11], r.grad_sem.at[1], {"seq": i},
                )

            @pl.when(i == me)
            def _():
                r.grad_got[me, BLOCK:] = r.grad_send[me, BLOCK:]

    later = reduction("l", 4)
    last = reduction("q", 8)
    await_bytes(r.grad_got.at[others, pl.ds(0, BLOCK)], r.grad_sem.at[0])

    @pl.loop(0, n_here)
    def _(b):
        rows = aligned(b * BLOCK, BLOCK)
        for pair in range(PAIRS):
            j = b * HEADS + 2 * pair
            d_k, d_v = swapped(r.grad_got[j, :BLOCK].astype(F32), r.grad_got[j + 1, :BLOCK].astype(F32))
            for part, grad in ((1, d_v), (3, d_k)):
                at = part * WIDTH + pair * 2 * HEAD
                slope = r.slope[b, :, at:at + 2 * HEAD].astype(F32)
                r.d_pre[rows, at:at + 2 * HEAD] = (grad * slope).astype(BF16)

    for at, low_col in enumerate((1, 1.5, 3, 3.5)):
        col = int(low_col * WIDTH)
        r.l_part[at % 2, at // 2] = dot_nn(r.xnt[...], r.d_pre[:, col:col + WIDTH // 2]).astype(BF16)
    later.to_core()
    await_bytes(r.grad_got.at[others, pl.ds(BLOCK, HEAD)], r.grad_sem.at[1])

    @pl.loop(0, n_here)
    def _(b):
        rows = aligned(b * BLOCK, BLOCK)
        for pair in range(PAIRS):
            j = b * HEADS + 2 * pair
            at = 2 * WIDTH + pair * 2 * HEAD
            grad = jnp.transpose(
                jnp.concatenate([r.grad_got[j + e, BLOCK:].astype(F32) for e in range(2)], axis=0)
            )
            slope = r.slope[b, :, at:at + 2 * HEAD].astype(F32)
            r.d_pre[rows, at:at + 2 * HEAD] = (grad * slope).astype(BF16)

    later.spread()
    q_grad = dot_nn(r.xnt[...], r.d_pre[:, 2 * WIDTH:3 * WIDTH]).astype(BF16)
    for at in range(4):
        r.q_part[at % 2, at // 2] = q_grad[:, at * BLOCK:(at + 1) * BLOCK]
    last.to_core()
    early.share()
    last.spread()
    later.collect()
    last.collect()

    await_bytes(r.loss_all.at[pl.ds(0, n_chips - 1)], r.loss_sem.at[3])
    count = jnp.full((8, BLOCK), total, jnp.int32).astype(F32)
    r.loss_out[0] = (jnp.sum(r.loss_all[...], axis=0) / count)[0, 0]
    early.finish()
    for at in range(2):
        early.written(at, r.joined, at * WIDTH // 2)
        early.written(2 + at, r.out, at * WIDTH // 2)
    later.share()
    last.share()
    later.finish()
    for at, low_col in enumerate((1, 1.5, 3, 3.5)):
        later.written(at, r.joined, int(low_col * WIDTH))
    last.finish()
    for at in range(4):
        last.written(at, r.joined, 2 * WIDTH + at * BLOCK)

    await_bytes(r.first, r.send_sem.at[1])
    await_bytes(r.ids, r.send_sem.at[2])
    for at in (3, 5, 8):
        await_bytes(r.negs.at[0], r.send_sem.at[at])
        await_bytes(r.all_ids.at[0], r.send_sem.at[at + 1])
    await_bytes(r.att_send.at[others], r.send_sem.at[7])
    await_bytes(r.datt_send.at[others], r.send_sem.at[12])
    await_bytes(r.grad_send.at[others, pl.ds(0, BLOCK)], r.send_sem.at[10])
    await_bytes(r.grad_send.at[others, pl.ds(BLOCK, HEAD)], r.send_sem.at[11])
    await_bytes(r.loss, r.loss_sem.at[0])
    await_bytes(r.loss_all.at[pl.ds(0, n_chips - 1)], r.loss_sem.at[2])


def activated(r, b, xn, part):
    half = 0.5 * dot_nn(xn, r.w_joined[:, part * WIDTH:(part + 1) * WIDTH])
    th = jnp.tanh(half)
    slope = (0.5 + 0.5 * th) * (1.0 + half * (1.0 - th))
    r.slope[b, :, part * WIDTH:(part + 1) * WIDTH] = slope.astype(BF16)
    return half + half * th


def middle(r, n_seq, me, grp, first_b, weight):
    both = 2
    rows = both * BLOCK
    n_here = r.x.shape[0]
    n_grp, n_neg = r.negs.shape[:2]

    def joined(make):
        return jnp.concatenate([make(e) for e in range(both)], axis=0)

    @pl.loop(0, both * HEADS)
    def _(turn):
        j = first_b * HEADS + turn

        @pl.when(j != me)
        def _():
            await_bytes(r.att_got.at[0], r.att_sem.at[j])

    for e in range(both):
        for pair in range(PAIRS):
            j = (first_b + e) * HEADS + 2 * pair
            top, bottom = swapped(r.att_got[j].astype(F32), r.att_got[j + 1].astype(F32))
            r.att[e * BLOCK:e * BLOCK + HEAD, pair_cols(pair)] = top
            r.att[e * BLOCK + HEAD:(e + 1) * BLOCK, pair_cols(pair)] = bottom

    att = r.att[...]
    centered = att - jnp.mean(att, axis=-1, keepdims=True)
    inv_att = lax.rsqrt(jnp.mean(centered * centered, axis=-1, keepdims=True) + eps_norm)
    normed = centered * inv_att
    u = joined(lambda e: r.u[first_b + e]).astype(F32)
    gated = (normed * u).astype(BF16)
    x = joined(lambda e: r.x[first_b + e]).astype(F32)
    out_rows = x + dot_nn(gated, r.w_out[...])
    inv_y = lax.rsqrt(jnp.sum(out_rows * out_rows, axis=-1, keepdims=True) + eps_norm)
    unit_y = out_rows * inv_y
    unit_b = unit_y.astype(BF16)
    more = jnp.where(me == n_seq - 1, 0, 1)
    last_row = lax.broadcasted_iota(jnp.int32, (BLOCK, WIDTH), 0) == BLOCK - 1
    last_lane = lax.broadcasted_iota(jnp.int32, (1, BLOCK), 1) == BLOCK - 1

    def next_rows(e):
        shifted = pltpu.roll(r.x[first_b + e].astype(F32), BLOCK - 1, axis=0)
        return jnp.where(last_row, r.first[first_b + e].astype(F32)[:1] * more.astype(F32), shifted)

    x_next = joined(next_rows)
    pos_unit = (
        x_next * lax.rsqrt(jnp.sum(x_next * x_next, axis=-1, keepdims=True) + eps_norm)
    ).astype(BF16).astype(F32)
    pos_logit = logit_scale * jnp.sum(unit_b.astype(F32) * pos_unit, axis=-1, keepdims=True)

    def row_ids(e):
        shifted = pltpu.roll(r.ids[pl.ds(first_b + e, 1)], BLOCK - 1, axis=1)
        coming = pltpu.roll(r.next_ids[pl.ds(first_b + e, 1)], BLOCK - 1, axis=1) * more
        return jnp.transpose(jnp.broadcast_to(jnp.where(last_lane, coming, shifted), (BLOCK, BLOCK)))

    ids = joined(row_ids)
    lane_sum = jnp.zeros((rows, BLOCK), F32)
    for g in range(n_grp):
        neg_logit = logit_scale * dot_nt(unit_b, r.negs[g])
        for sub in range(n_neg // BLOCK):
            at = (g * n_neg) + sub * BLOCK
            hit = r.all_ids[g, n_here + sub:n_here + sub + 1] == ids
            exps = jnp.where(hit, 0.0, jnp.exp(neg_logit[:, sub * BLOCK:(sub + 1) * BLOCK]))
            r.exps[:, at:at + BLOCK] = exps
            lane_sum = lane_sum + exps
    pos_exp = jnp.exp(pos_logit)
    denom = pos_exp + jnp.sum(lane_sum, axis=-1, keepdims=True)

    def row_valid(e):
        pos = me * BLOCK + lax.broadcasted_iota(jnp.int32, (BLOCK, 1), 0)
        return jnp.where(pos + 1 < r.lens[grp * n_here + first_b + e], 1.0, 0.0)

    valid = joined(row_valid)
    row_loss = jnp.where(valid > 0.0, jnp.log(denom) - pos_logit, 0.0)
    r.loss[...] += jnp.broadcast_to(jnp.sum(row_loss, axis=0, keepdims=True), r.loss.shape)
    row_weight = valid * weight
    d_pos = row_weight * (pos_exp / denom - 1.0)
    scale = row_weight / denom
    neg_back = jnp.zeros((rows, WIDTH), F32)
    for g in range(n_grp):
        d_neg = (scale * r.exps[:, g * n_neg:(g + 1) * n_neg]).astype(BF16)
        neg_back = neg_back + dot_nn(d_neg, r.negs[g])
    d_unit = logit_scale * (d_pos * pos_unit + neg_back)
    d_out = (
        (d_unit - unit_y * jnp.sum(unit_y * d_unit, axis=-1, keepdims=True)) * inv_y
    ).astype(BF16)
    d_gate = dot_nt(d_out, r.w_out[...])
    d_norm = d_gate * u
    d_att = inv_att * (
        d_norm
        - jnp.mean(d_norm, axis=-1, keepdims=True)
        - normed * jnp.mean(d_norm * normed, axis=-1, keepdims=True)
    )
    for e in range(both):
        rows_e = d_att[e * BLOCK:(e + 1) * BLOCK]
        for pair in range(PAIRS):
            cols = pair_cols(pair)
            packed = swapped(rows_e[:HEAD, cols], rows_e[HEAD:, cols])
            for odd in range(2):
                r.datt_send[(first_b + e) * HEADS + 2 * pair + odd] = packed[odd].astype(BF16)

    @pl.loop(0, both * HEADS)
    def _(turn):
        j = first_b * HEADS + lax.rem(me + turn, both * HEADS)

        @pl.when(j != me)
        def _():
            copy_to(
                r.datt_send.at[j], r.datt_got.at[me], r.send_sem.at[12], r.datt_sem.at[me], {"seq": j}
            )

        @pl.when(j == me)
        def _():
            r.datt_got[me] = r.datt_send[me]

    r.grad_out[...] += dot_tn(gated, d_out)
    d_u = d_gate * normed
    for e in range(both):
        slope = r.slope[first_b + e, :, :WIDTH].astype(F32)
        r.d_pre[aligned((first_b + e) * BLOCK, BLOCK), :WIDTH] = (
            d_u[e * BLOCK:(e + 1) * BLOCK] * slope
        ).astype(BF16)


def local(inputs, history, lengths, w_joined, w_out, neg_emb, neg_ids):
    n_here, block, width = inputs.shape
    n_seq = lax.axis_size("seq")
    length = n_seq * block
    lanes = 2 * HEAD
    rows = n_here * block
    n_neg = neg_emb.shape[0]
    chips = 2 * n_seq
    strip = width // n_seq
    dma = pltpu.SemaphoreType.DMA
    buffers = dict(
        xn=((n_here, block, width), BF16), xnt=((width, rows), BF16), u=((n_here, block, width), BF16),
        slope=((n_here, block, 4 * width), BF16), d_pre=((rows, 4 * width), BF16),
        send=((n_seq, BLOCK + HEAD, lanes), BF16), got=((n_seq, BLOCK + HEAD, lanes), BF16),
        att_send=((n_seq, HEAD, lanes), BF16), att_got=((n_seq, HEAD, lanes), BF16),
        datt_send=((n_seq, HEAD, lanes), BF16), datt_got=((n_seq, HEAD, lanes), BF16),
        grad_send=((n_seq, BLOCK + HEAD, lanes), BF16), grad_got=((n_seq, BLOCK + HEAD, lanes), BF16),
        first=((n_here, 16, width), BF16), ids=((2 * n_here, block), jnp.int32),
        next_ids=((2 * n_here, block), jnp.int32), negs=((4, n_neg, width), BF16),
        all_ids=((4, 2 * n_here, block), jnp.int32),
        k0=((length, lanes), BF16), v0=((length, lanes), BF16), qa=((length, lanes), BF16),
        kt=((HEAD, length), BF16), acc=((FQ, lanes), F32), dq=((HEAD, length), F32), dkv=((BM, lanes), F32),
        att=((2 * block, width), F32), exps=((2 * block, 4 * n_neg), F32), grad_out=((width, width), F32),
        loss=((8, block), F32), loss_core=((8, block), F32), loss_sum=((8, block), F32),
        loss_all=((chips, 8, block), F32),
    )
    for name, cols in (("e", 2 * width // 4), ("l", 2 * width // 4), ("q", width // 4)):
        buffers[name + "_part"] = ((2, 2, width, cols), BF16)
        buffers[name + "_core"] = ((2, width, cols), BF16)
        buffers[name + "_sum"] = ((chips, strip, cols), BF16)
        buffers[name + "_got"] = ((chips, strip, cols), BF16)
        buffers[name + "_red"] = ((strip, cols), BF16)
        buffers[name + "_full"] = ((2, chips, strip, cols), BF16)
    sems = dict(
        send_sem=13, one_sem=8, got_sem=n_seq, att_sem=n_seq, datt_sem=n_seq, grad_sem=2, loss_sem=4,
        red_send=12, red_recv=12,
    )
    takes = ("lens", "x", "history", "neg_ids", "w_joined", "w_out", "neg_emb")
    gives = dict(
        joined=((width, 4 * width), BF16), out=((width, width), BF16), loss_out=((1,), F32)
    )
    names = takes + tuple(gives) + tuple(buffers) + tuple(sems)
    joined, out, loss = pl.pallas_call(
        functools.partial(kernel, n_seq, names),
        out_shape=[jax.ShapeDtypeStruct(*kind) for kind in gives.values()],
        in_specs=[SMEM] + [VMEM] * (len(takes) - 1),
        out_specs=[VMEM, VMEM, SMEM],
        scratch_shapes=[pltpu.VMEM(*kind) for kind in buffers.values()]
        + [dma((count,)) for count in sems.values()],
        compiler_params=pltpu.CompilerParams(
            collective_id=0, has_side_effects=True, vmem_limit_bytes=60 * 1024 * 1024
        ),
    )(lengths, inputs, history, neg_ids.reshape(-1, block), w_joined, w_out, neg_emb)
    return (joined.astype(F32), out.astype(F32), loss.reshape(()))


def solution(mesh):
    placed = (
        P("grp", "seq", None),
        P("grp", "seq"),
        P(),
        P(),
        P(),
        P(("grp", "seq"), None),
        P(("grp", "seq")),
    )
    return jax.shard_map(
        local, mesh=mesh, in_specs=placed, out_specs=(P(), P(), P()), check_vma=False
    )
```

```python
import functools
import types

import jax
import jax.numpy as jnp
from jax import lax
from jax.experimental import pallas as pl
from jax.experimental.pallas import tpu as pltpu
from jax.sharding import PartitionSpec as P

HEADS = 8
HEAD = 64
WIDTH = 512
PAIRS = 4
BLOCK = 128
TILE = 512
FQ = TILE
BM = TILE
eps_norm = 1e-06
logit_scale = 64.0

MESH = pl.DeviceIdType.MESH
F32 = jnp.float32
BF16 = jnp.bfloat16
VMEM = pl.BlockSpec(memory_space=pltpu.VMEM)
SMEM = pl.BlockSpec(memory_space=pltpu.SMEM)


def dot_nn(a, b):
    return lax.dot_general(a, b, (((1,), (0,)), ((), ())), preferred_element_type=F32)


def dot_nt(a, b):
    return lax.dot_general(a, b, (((1,), (1,)), ((), ())), preferred_element_type=F32)


def dot_tn(a, b):
    return lax.dot_general(a, b, (((0,), (0,)), ((), ())), preferred_element_type=F32)


def low_lanes(shape):
    return lax.broadcasted_iota(jnp.int32, shape, 1) < HEAD


def turned(a):
    return pltpu.roll(a, HEAD, axis=1)


def swapped(a, b):
    low = low_lanes(a.shape)
    return jnp.where(low, a, turned(b)), jnp.where(low, turned(a), b)


def copy_to(src, dst, send_sem, recv_sem, where):
    pltpu.make_async_remote_copy(
        src_ref=src, dst_ref=dst, send_sem=send_sem, recv_sem=recv_sem,
        device_id=where, device_id_type=MESH,
    ).start()


def await_bytes(ref, sem):
    pltpu.make_async_copy(ref, ref, sem).wait()


def aligned(at, size):
    return pl.ds(pl.multiple_of(at, size), size)


def pair_cols(pair):
    return slice(pair * 2 * HEAD, (pair + 1) * 2 * HEAD)


def shifts(n_seq):
    side = int((n_seq // 2) ** 0.5)
    steps = [(x, y, z) for x in range(side) for y in range(side) for z in range(2)]
    return sorted(steps[1:], key=lambda at: -(min(at[0], side - at[0]) + min(at[1], side - at[1]) + at[2]))


def peer(me, shift):
    x, y, z = me // HEADS, lax.rem(me // 2, 4), lax.rem(me, 2)
    return (lax.rem(x + shift[0], 4) * 4 + lax.rem(y + shift[1], 4)) * 2 + lax.rem(z + shift[2], 2)


def cover(first, count, body):
    done = 0
    for tiles in (4, 2, 1):
        n = count // tiles if tiles == 4 else lax.rem(count // tiles, 2)

        @pl.loop(0, n)
        def _(at, done=done, tiles=tiles):
            body((first + done + at * tiles) * TILE, tiles * TILE)

        done = done + n * tiles


def kernel(n_seq, names, *refs):
    r = types.SimpleNamespace(**dict(zip(names, refs, strict=True)))
    me = lax.axis_index("seq")
    grp = lax.axis_index("grp")
    core, z_hi = lax.rem(grp, 2), grp // 2
    loads = [
        pltpu.make_async_copy(getattr(r, name + "_in"), getattr(r, name), r.load_sem.at[at])
        for at, name in enumerate(("x", "w_joined", "history", "neg_ids", "neg_emb", "w_out"))
    ]
    for load in loads:
        load.start()
    n_here = r.x.shape[0]
    planes = n_seq // HEADS
    length = n_seq * BLOCK
    mate = {"grp": grp + 1 - 2 * core}
    other_z = {"grp": (1 - z_hi) * 2 + core}
    others = pl.ds(0, n_seq - 1)
    x_at, y_at, z_at = me // HEADS, lax.rem(me // 2, 4), z_hi * 2 + lax.rem(me, 2)

    barrier = pltpu.get_barrier_semaphore()

    def greet(where):
        pl.semaphore_signal(barrier, inc=1, device_id=where, device_id_type=MESH)

    greet(mate)

    @pl.loop(1, n_seq)
    def _(step):
        greet({"seq": lax.rem(me + step, n_seq)})

    for step in range(4):
        for z in range(2):
            greet(dict(other_z, seq=(x_at * 4 + lax.rem(y_at + step, 4)) * 2 + z))
            if step:
                greet(dict(other_z, seq=(lax.rem(x_at + step, 4) * 4 + y_at) * 2 + z))
    n_peers = n_seq + 14

    loads[0].wait()
    loads[1].wait()

    @pl.loop(0, n_here)
    def _(b):
        x = r.x[b].astype(F32)
        centered = x - jnp.mean(x, axis=-1, keepdims=True)
        var = jnp.mean(centered * centered, axis=-1, keepdims=True)
        xn = (centered * lax.rsqrt(var + eps_norm)).astype(BF16)
        r.xn[b] = xn
        v, q, k = (activated(r, b, xn, part) for part in (1, 2, 3))
        for pair in range(PAIRS):
            cols = pair_cols(pair)
            kv = swapped(k[:, cols], v[:, cols])
            qs = swapped(q[:HEAD, cols], q[HEAD:, cols])
            for odd in range(2):
                j = b * HEADS + 2 * pair + odd
                r.send[j, :BLOCK] = kv[odd].astype(BF16)
                r.send[j, BLOCK:] = qs[odd].astype(BF16)

    pl.semaphore_wait(barrier, n_peers)
    for shift in shifts(n_seq):
        j = peer(me, shift)
        copy_to(r.send.at[j], r.got.at[me], r.send_sem.at[0], r.got_sem.at[me], {"seq": j})
    r.got[me] = r.send[me]

    before = {"seq": lax.rem(me + n_seq - 1, n_seq)}
    loads[2].wait()
    loads[3].wait()
    r.ids[:n_here] = r.history[...]
    r.ids[n_here:] = r.neg_ids[...]
    copy_to(r.x.at[:, pl.ds(0, 16)], r.first, r.send_sem.at[1], r.one_sem.at[0], before)
    copy_to(r.ids, r.next_ids, r.send_sem.at[2], r.one_sem.at[1], before)

    loads[4].wait()
    loads[5].wait()

    @pl.loop(0, n_here)
    def _(b):
        xn = r.xn[b]
        r.u[b] = activated(r, b, xn, 0).astype(BF16)
        r.xnt[:, aligned(b * BLOCK, BLOCK)] = jnp.transpose(xn.astype(F32)).astype(BF16)
        rows = aligned(b * BLOCK, BLOCK)
        emb = r.neg_emb[rows].astype(F32)
        r.negs[grp, rows] = (
            emb * lax.rsqrt(jnp.sum(emb * emb, axis=-1, keepdims=True) + eps_norm)
        ).astype(BF16)

    r.all_ids[grp] = r.ids[...]

    seq_len = r.lens[grp * n_here + me // HEADS]
    low = low_lanes((HEAD, 2 * HEAD))
    low_block = low_lanes((BLOCK, 2 * HEAD))

    @pl.loop(0, planes)
    def _(step):
        first = lax.rem(me // HEADS + planes // 2 + step, planes) * HEADS

        @pl.loop(0, HEADS)
        def _(turn):
            i = first + turn

            @pl.when(i != me)
            def _():
                await_bytes(r.got.at[0], r.got_sem.at[i])

        @pl.loop(0, HEADS, unroll=4)
        def _(turn):
            i = first + turn
            rows = aligned(i * BLOCK, BLOCK)
            pos = i * BLOCK + lax.broadcasted_iota(jnp.int32, (BLOCK, 2 * HEAD), 0)
            kv = jnp.where(pos < seq_len, r.got[i, :BLOCK].astype(F32), 0.0)
            r.k0[rows] = jnp.where(low_block, 0.5 * kv, 0.0).astype(BF16)
            r.v0[rows] = jnp.where(low_block, 0.0, kv).astype(BF16)
            r.kt[:, rows] = jnp.transpose(kv)[:HEAD].astype(BF16)
            q = r.got[i, BLOCK:].astype(F32)
            r.qa[rows] = jnp.concatenate(
                [jnp.where(low, q, 0.0), jnp.where(low, turned(q), 0.0)], axis=0
            ).astype(BF16)

    copy_to(r.negs.at[grp], r.negs.at[grp], r.send_sem.at[3], r.one_sem.at[2], mate)
    copy_to(r.all_ids.at[grp], r.all_ids.at[grp], r.send_sem.at[4], r.one_sem.at[3], mate)
    copy_to(r.negs.at[grp], r.negs.at[grp], r.send_sem.at[5], r.one_sem.at[4], other_z)
    copy_to(r.all_ids.at[grp], r.all_ids.at[grp], r.send_sem.at[6], r.one_sem.at[5], other_z)
    await_bytes(r.send.at[others], r.send_sem.at[0])
    inv_len = 1.0 / jnp.full((1, 2 * HEAD), seq_len, jnp.int32).astype(F32)

    f_tiles = length // FQ
    f_per = FQ // BLOCK

    @pl.loop(0, f_tiles)
    def _(step):
        c = lax.rem(me // f_per + step, f_tiles)
        q = r.qa[aligned(c * FQ, FQ)]

        def piece(start, size, masked):
            rows = pl.ds(pl.multiple_of(start, TILE), size)
            half = dot_nt(q, r.k0[rows])
            if masked:
                ahead = lax.broadcasted_iota(jnp.int32, (FQ, size), 1) - lax.broadcasted_iota(
                    jnp.int32, (FQ, size), 0
                )
                half = jnp.where(ahead <= 0, half, 0.0)
            probs = (half + half * jnp.tanh(half)).astype(BF16)
            return dot_nn(probs, r.v0[rows])

        r.acc[...] = piece(c * FQ, FQ, True)

        def more(start, size):
            r.acc[...] += piece(start, size, False)

        cover(0, c, more)
        for u in range(f_per):
            out = r.acc[u * BLOCK:(u + 1) * BLOCK] * inv_len
            top, bottom = out[:HEAD], out[HEAD:]
            r.att_send[c * f_per + u] = jnp.where(low, turned(top), bottom).astype(BF16)

        @pl.loop(0, f_per)
        def _(turn):
            i = c * f_per + lax.rem(me + turn, f_per)

            @pl.when(i != me)
            def _():
                copy_to(
                    r.att_send.at[i], r.att_got.at[me], r.send_sem.at[7], r.att_sem.at[me], {"seq": i}
                )

            @pl.when(i == me)
            def _():
                r.att_got[me] = r.att_send[me]

    far = (1 - z_hi) * 2 + core
    await_bytes(r.negs.at[0], r.one_sem.at[4])
    await_bytes(r.all_ids.at[0], r.one_sem.at[5])
    copy_to(r.negs.at[far], r.negs.at[far], r.send_sem.at[8], r.one_sem.at[6], mate)
    copy_to(r.all_ids.at[far], r.all_ids.at[far], r.send_sem.at[9], r.one_sem.at[7], mate)

    total = r.lens[0] - 1
    for at in range(1, r.lens.shape[0]):
        total = total + (r.lens[at] - 1)
    both = 2
    half_rows = both * BLOCK
    weight = 1.0 / jnp.full((half_rows, 1), total, jnp.int32).astype(F32)
    r.grad_out[...] = jnp.zeros_like(r.grad_out)
    r.loss[...] = jnp.zeros_like(r.loss)
    await_bytes(r.first, r.one_sem.at[0])
    await_bytes(r.ids, r.one_sem.at[1])
    await_bytes(r.negs.at[0], r.one_sem.at[2])
    await_bytes(r.all_ids.at[0], r.one_sem.at[3])
    await_bytes(r.negs.at[0], r.one_sem.at[6])
    await_bytes(r.all_ids.at[0], r.one_sem.at[7])
    n_halves = n_here // both

    @pl.loop(0, n_halves)
    def _(step):
        middle(r, n_seq, me, grp, both * lax.rem(me // (both * HEADS) + step, n_halves), weight)

    axes = dict(x=x_at, y=y_at, z=z_at)
    plane_at = dict(x=y_at * 4 + z_at, y=x_at * 4 + z_at, z=x_at * 4 + y_at)

    def chip(axis, along, across):
        hi, lo = across // 4, lax.rem(across, 4)
        x, y, z = dict(x=(along, hi, lo), y=(hi, along, lo), z=(hi, lo, along))[axis]
        return {"grp": z // 2 * 2 + core, "seq": (x * 4 + y) * 2 + lax.rem(z, 2)}

    def reduction(name, axis, at):
        part, got_core, sums, got, sums2, got2, red, full = (
            getattr(r, name + tail)
            for tail in ("_part", "_core", "_sum", "_got", "_sum2", "_got2", "_red", "_full")
        )
        send = [r.red_send.at[at * 6 + k] for k in range(6)]
        recv = [r.red_recv.at[at * 6 + k] for k in range(6)]
        along, across = axes[axis], plane_at[axis]
        rest = pl.ds(0, 15)

        def to_core(grad):
            for half in range(4):
                block = grad[:, half * BLOCK:(half + 1) * BLOCK].astype(BF16)
                low = half % 2 * 8
                part[half // 2, :, low:low + 8] = block.reshape(4, 8, 16, BLOCK)
            copy_to(part.at[1 - core], got_core, send[0], recv[0], mate)

        def along_axis(sources, target, sems):
            for step in range(1, 4):
                to = lax.rem(along + step, 4)
                copy_to(sources(to), target, *sems, chip(axis, to, across))

        def over_plane(sources, target, sems):
            @pl.loop(1, 16)
            def _(step):
                to = lax.rem(across + step, 16)
                copy_to(sources(to), target, *sems, chip(axis, along, to))

        def fold():
            await_bytes(got_core, recv[0])
            sums[...] = (part[core].astype(F32) + got_core[...].astype(F32)).astype(BF16)
            along_axis(lambda to: sums.at[to], got.at[along], (send[1], recv[1]))

        def plane():
            got[along] = sums[along]
            await_bytes(got.at[pl.ds(0, 3)], recv[1])
            sums2[...] = jnp.sum(got[...].astype(F32), axis=0).astype(BF16)
            over_plane(lambda to: sums2.at[to], got2.at[across], (send[2], recv[2]))

        def gather():
            got2[across] = sums2[across]
            await_bytes(got2.at[rest], recv[2])
            red[...] = jnp.sum(got2[...].astype(F32), axis=0).astype(BF16)
            full[core, along, across] = red[...]
            over_plane(lambda to: red, full.at[core, along, across], (send[3], recv[3]))

        def spread():
            await_bytes(got2.at[rest], recv[3])
            along_axis(lambda to: full.at[core, along], full.at[core, along], (send[4], recv[4]))

        def share():
            await_bytes(got.at[pl.ds(0, 3)], recv[4])
            copy_to(full.at[core], full.at[core], send[5], recv[5], mate)

        def finish():
            await_bytes(full.at[0], recv[5])
            await_bytes(part.at[0], send[0])
            await_bytes(got.at[pl.ds(0, 3)], send[1])
            for k in (2, 3):
                await_bytes(got2.at[rest], send[k])
            await_bytes(got.at[pl.ds(0, 3)], send[4])
            await_bytes(full.at[0], send[5])

        return types.SimpleNamespace(
            to_core=to_core, fold=fold, plane=plane, gather=gather, spread=spread, share=share, finish=finish
        )

    early = [reduction("u", "x", 0), reduction("o", "y", 1)]
    early[0].to_core(dot_nn(r.xnt[...], r.d_pre[:, :WIDTH]))
    early[1].to_core(r.grad_out[...])
    copy_to(r.loss, r.loss_core, r.loss_sem.at[0], r.loss_sem.at[1], mate)

    def loss_along(axis, value, at):
        r.loss_all[at, axes[axis]] = value
        r.loss_sum[at] = value
        for step in range(1, 4):
            copy_to(
                r.loss_sum.at[at], r.loss_all.at[at, axes[axis]],
                r.loss_sem.at[2 + 2 * at], r.loss_sem.at[3 + 2 * at],
                chip(axis, lax.rem(axes[axis] + step, 4), plane_at[axis]),
            )

    def loss_over(at):
        await_bytes(r.loss_all.at[at, pl.ds(0, 3)], r.loss_sem.at[3 + 2 * at])
        return jnp.sum(r.loss_all[at], axis=0)

    @pl.loop(0, n_seq)
    def _(step):
        i = lax.rem(me + step, n_seq)

        @pl.when(i != me)
        def _():
            await_bytes(r.datt_got.at[0], r.datt_sem.at[i])

    @pl.loop(0, n_seq, unroll=4)
    def _(i):
        d_att = r.datt_got[i].astype(F32)
        rows = aligned(i * BLOCK, BLOCK)
        qa = r.qa[rows].astype(F32)
        r.qa[rows] = jnp.where(
            low_block, qa, jnp.concatenate([turned(d_att), d_att], axis=0)
        ).astype(BF16)

    r.dq[...] = jnp.zeros_like(r.dq)
    b_tiles = length // BM
    b_per = BM // BLOCK
    kv_scale = jnp.where(low_lanes((1, 2 * HEAD)), 0.5 * inv_len, inv_len)

    @pl.loop(0, b_tiles)
    def _(step):
        c = lax.rem(me // b_per + step, b_tiles)
        m_rows = aligned(c * BM, BM)
        low_tile = low_lanes((BM, 2 * HEAD))

        def piece(start, size, masked):
            t_rows = pl.ds(pl.multiple_of(start, TILE), size)
            qa = r.qa[t_rows]
            half = dot_nt(r.k0[m_rows], qa)
            d_probs = dot_nt(r.v0[m_rows], qa)
            if masked:
                ahead = lax.broadcasted_iota(jnp.int32, (BM, size), 0) - lax.broadcasted_iota(
                    jnp.int32, (BM, size), 1
                )
                half = jnp.where(ahead <= 0, half, 0.0)
                d_probs = jnp.where(ahead <= 0, d_probs, 0.0)
            up = 1.0 + jnp.tanh(half)
            probs = half * up
            d_scores = (d_probs * up * (1.0 + (half + half) - probs)).astype(BF16)
            r.dq[:, t_rows] += dot_nn(r.kt[:, m_rows], d_scores)
            return jnp.where(low_tile, dot_nn(d_scores, qa), dot_nn(probs.astype(BF16), qa))

        r.dkv[...] = piece(c * BM, BM, True)

        def more(start, size):
            r.dkv[...] += piece(start, size, False)

        cover(c + 1, b_tiles - 1 - c, more)
        for u in range(b_per):
            r.grad_send[c * b_per + u, :BLOCK] = (
                r.dkv[u * BLOCK:(u + 1) * BLOCK] * kv_scale
            ).astype(BF16)

        @pl.loop(0, b_per)
        def _(turn):
            i = c * b_per + lax.rem(me + turn, b_per)

            @pl.when(i != me)
            def _():
                copy_to(
                    r.grad_send.at[i, pl.ds(0, BLOCK)], r.grad_got.at[me, pl.ds(0, BLOCK)],
                    r.send_sem.at[10], r.grad_sem.at[0], {"seq": i},
                )

            @pl.when(i == me)
            def _():
                r.grad_got[me, :BLOCK] = r.grad_send[me, :BLOCK]

        for at, stage in enumerate(("fold", "plane", "gather", "spread", "share")):
            @pl.when(step == at)
            def _(at=at, stage=stage):
                for one in early:
                    getattr(one, stage)()
                if at == 0:
                    await_bytes(r.loss_core, r.loss_sem.at[1])
                    loss_along("x", r.loss[...] + r.loss_core[...], 0)
                if at == 1:
                    loss_along("y", loss_over(0), 1)
                if at == 2:
                    loss_along("z", loss_over(1), 2)
                if at == 3:
                    count = jnp.full((8, BLOCK), total, jnp.int32).astype(F32)
                    r.loss_out[0] = (loss_over(2) / count)[0, 0]

    @pl.loop(0, b_tiles)
    def _(step):
        c = lax.rem(me // b_per + step, b_tiles)
        for u in range(b_per):
            d_q = r.dq[:, aligned((c * b_per + u) * BLOCK, BLOCK)] * (0.5 * inv_len)
            r.grad_send[c * b_per + u, BLOCK:] = d_q.astype(BF16)

        @pl.loop(0, b_per)
        def _(turn):
            i = c * b_per + lax.rem(me + turn, b_per)

            @pl.when(i != me)
            def _():
                copy_to(
                    r.grad_send.at[i, pl.ds(BLOCK, HEAD)], r.grad_got.at[me, pl.ds(BLOCK, HEAD)],
                    r.send_sem.at[11], r.grad_sem.at[1], {"seq": i},
                )

            @pl.when(i == me)
            def _():
                r.grad_got[me, BLOCK:] = r.grad_send[me, BLOCK:]

    late = [reduction("v", "x", 2), reduction("k", "y", 3), reduction("q", "z", 4)]
    await_bytes(r.grad_got.at[others, pl.ds(0, BLOCK)], r.grad_sem.at[0])

    @pl.loop(0, n_here)
    def _(b):
        rows = aligned(b * BLOCK, BLOCK)
        for pair in range(PAIRS):
            j = b * HEADS + 2 * pair
            d_k, d_v = swapped(r.grad_got[j, :BLOCK].astype(F32), r.grad_got[j + 1, :BLOCK].astype(F32))
            for part, grad in ((1, d_v), (3, d_k)):
                at = part * WIDTH + pair * 2 * HEAD
                slope = r.slope[b, :, at:at + 2 * HEAD].astype(F32)
                r.d_pre[rows, at:at + 2 * HEAD] = (grad * slope).astype(BF16)

    late[0].to_core(dot_nn(r.xnt[...], r.d_pre[:, WIDTH:2 * WIDTH]))
    late[1].to_core(dot_nn(r.xnt[...], r.d_pre[:, 3 * WIDTH:]))
    late[0].fold()
    late[1].fold()
    await_bytes(r.grad_got.at[others, pl.ds(BLOCK, HEAD)], r.grad_sem.at[1])

    @pl.loop(0, n_here)
    def _(b):
        rows = aligned(b * BLOCK, BLOCK)
        for pair in range(PAIRS):
            j = b * HEADS + 2 * pair
            at = 2 * WIDTH + pair * 2 * HEAD
            grad = jnp.transpose(
                jnp.concatenate([r.grad_got[j + e, BLOCK:].astype(F32) for e in range(2)], axis=0)
            )
            slope = r.slope[b, :, at:at + 2 * HEAD].astype(F32)
            r.d_pre[rows, at:at + 2 * HEAD] = (grad * slope).astype(BF16)

    late[2].to_core(dot_nn(r.xnt[...], r.d_pre[:, 2 * WIDTH:3 * WIDTH]))
    late[0].plane()
    late[1].plane()
    late[2].fold()
    late[0].gather()
    late[1].gather()
    late[2].plane()
    late[0].spread()
    late[1].spread()
    late[2].gather()
    late[0].share()
    late[1].share()
    late[2].spread()
    late[2].share()

    for one in early + late:
        one.finish()

    await_bytes(r.first, r.send_sem.at[1])
    await_bytes(r.ids, r.send_sem.at[2])
    for at in (3, 5, 8):
        await_bytes(r.negs.at[0], r.send_sem.at[at])
        await_bytes(r.all_ids.at[0], r.send_sem.at[at + 1])
    await_bytes(r.att_send.at[others], r.send_sem.at[7])
    await_bytes(r.datt_send.at[others], r.send_sem.at[12])
    await_bytes(r.grad_send.at[others, pl.ds(0, BLOCK)], r.send_sem.at[10])
    await_bytes(r.grad_send.at[others, pl.ds(BLOCK, HEAD)], r.send_sem.at[11])
    await_bytes(r.loss, r.loss_sem.at[0])
    for at in range(3):
        await_bytes(r.loss_all.at[at, pl.ds(0, 3)], r.loss_sem.at[2 + 2 * at])


def activated(r, b, xn, part):
    half = 0.5 * dot_nn(xn, r.w_joined[:, part * WIDTH:(part + 1) * WIDTH])
    th = jnp.tanh(half)
    slope = (0.5 + 0.5 * th) * (1.0 + half * (1.0 - th))
    r.slope[b, :, part * WIDTH:(part + 1) * WIDTH] = slope.astype(BF16)
    return half + half * th


def middle(r, n_seq, me, grp, first_b, weight):
    both = 2
    rows = both * BLOCK
    n_here = r.x.shape[0]
    n_grp, n_neg = r.negs.shape[:2]

    def joined(make):
        return jnp.concatenate([make(e) for e in range(both)], axis=0)

    @pl.loop(0, both * HEADS)
    def _(turn):
        j = first_b * HEADS + turn

        @pl.when(j != me)
        def _():
            await_bytes(r.att_got.at[0], r.att_sem.at[j])

    for e in range(both):
        for pair in range(PAIRS):
            j = (first_b + e) * HEADS + 2 * pair
            top, bottom = swapped(r.att_got[j].astype(F32), r.att_got[j + 1].astype(F32))
            r.att[e * BLOCK:e * BLOCK + HEAD, pair_cols(pair)] = top
            r.att[e * BLOCK + HEAD:(e + 1) * BLOCK, pair_cols(pair)] = bottom

    att = r.att[...]
    centered = att - jnp.mean(att, axis=-1, keepdims=True)
    inv_att = lax.rsqrt(jnp.mean(centered * centered, axis=-1, keepdims=True) + eps_norm)
    normed = centered * inv_att
    u = joined(lambda e: r.u[first_b + e]).astype(F32)
    gated = (normed * u).astype(BF16)
    x = joined(lambda e: r.x[first_b + e]).astype(F32)
    out_rows = x + dot_nn(gated, r.w_out[...])
    inv_y = lax.rsqrt(jnp.sum(out_rows * out_rows, axis=-1, keepdims=True) + eps_norm)
    unit_y = out_rows * inv_y
    unit_b = unit_y.astype(BF16)
    more = jnp.where(me == n_seq - 1, 0, 1)
    last_row = lax.broadcasted_iota(jnp.int32, (BLOCK, WIDTH), 0) == BLOCK - 1
    last_lane = lax.broadcasted_iota(jnp.int32, (1, BLOCK), 1) == BLOCK - 1

    def next_rows(e):
        shifted = pltpu.roll(r.x[first_b + e].astype(F32), BLOCK - 1, axis=0)
        return jnp.where(last_row, r.first[first_b + e].astype(F32)[:1] * more.astype(F32), shifted)

    x_next = joined(next_rows)
    pos_unit = (
        x_next * lax.rsqrt(jnp.sum(x_next * x_next, axis=-1, keepdims=True) + eps_norm)
    ).astype(BF16).astype(F32)
    pos_logit = logit_scale * jnp.sum(unit_b.astype(F32) * pos_unit, axis=-1, keepdims=True)

    def row_ids(e):
        shifted = pltpu.roll(r.ids[pl.ds(first_b + e, 1)], BLOCK - 1, axis=1)
        coming = pltpu.roll(r.next_ids[pl.ds(first_b + e, 1)], BLOCK - 1, axis=1) * more
        return jnp.transpose(jnp.broadcast_to(jnp.where(last_lane, coming, shifted), (BLOCK, BLOCK)))

    ids = joined(row_ids)
    lane_sum = jnp.zeros((rows, BLOCK), F32)
    for g in range(n_grp):
        neg_logit = logit_scale * dot_nt(unit_b, r.negs[g])
        for sub in range(n_neg // BLOCK):
            at = (g * n_neg) + sub * BLOCK
            hit = r.all_ids[g, n_here + sub:n_here + sub + 1] == ids
            exps = jnp.where(hit, 0.0, jnp.exp(neg_logit[:, sub * BLOCK:(sub + 1) * BLOCK]))
            r.exps[:, at:at + BLOCK] = exps
            lane_sum = lane_sum + exps
    pos_exp = jnp.exp(pos_logit)
    denom = pos_exp + jnp.sum(lane_sum, axis=-1, keepdims=True)

    def row_valid(e):
        pos = me * BLOCK + lax.broadcasted_iota(jnp.int32, (BLOCK, 1), 0)
        return jnp.where(pos + 1 < r.lens[grp * n_here + first_b + e], 1.0, 0.0)

    valid = joined(row_valid)
    row_loss = jnp.where(valid > 0.0, jnp.log(denom) - pos_logit, 0.0)
    r.loss[...] += jnp.broadcast_to(jnp.sum(row_loss, axis=0, keepdims=True), r.loss.shape)
    row_weight = valid * weight
    d_pos = row_weight * (pos_exp / denom - 1.0)
    scale = row_weight / denom
    neg_back = jnp.zeros((rows, WIDTH), F32)
    for g in range(n_grp):
        d_neg = (scale * r.exps[:, g * n_neg:(g + 1) * n_neg]).astype(BF16)
        neg_back = neg_back + dot_nn(d_neg, r.negs[g])
    d_unit = logit_scale * (d_pos * pos_unit + neg_back)
    d_out = (
        (d_unit - unit_y * jnp.sum(unit_y * d_unit, axis=-1, keepdims=True)) * inv_y
    ).astype(BF16)
    d_gate = dot_nt(d_out, r.w_out[...])
    d_norm = d_gate * u
    d_att = inv_att * (
        d_norm
        - jnp.mean(d_norm, axis=-1, keepdims=True)
        - normed * jnp.mean(d_norm * normed, axis=-1, keepdims=True)
    )
    for e in range(both):
        rows_e = d_att[e * BLOCK:(e + 1) * BLOCK]
        for pair in range(PAIRS):
            cols = pair_cols(pair)
            packed = swapped(rows_e[:HEAD, cols], rows_e[HEAD:, cols])
            for odd in range(2):
                r.datt_send[(first_b + e) * HEADS + 2 * pair + odd] = packed[odd].astype(BF16)

    @pl.loop(0, both * HEADS)
    def _(turn):
        j = first_b * HEADS + lax.rem(me + turn, both * HEADS)

        @pl.when(j != me)
        def _():
            copy_to(
                r.datt_send.at[j], r.datt_got.at[me], r.send_sem.at[12], r.datt_sem.at[me], {"seq": j}
            )

        @pl.when(j == me)
        def _():
            r.datt_got[me] = r.datt_send[me]

    r.grad_out[...] += dot_tn(gated, d_out)
    d_u = d_gate * normed
    for e in range(both):
        slope = r.slope[first_b + e, :, :WIDTH].astype(F32)
        r.d_pre[aligned((first_b + e) * BLOCK, BLOCK), :WIDTH] = (
            d_u[e * BLOCK:(e + 1) * BLOCK] * slope
        ).astype(BF16)


def widen(*refs):
    *blocks, joined, out = refs
    for at, block in enumerate(blocks):
        for half in range(4):
            low = half % 2 * 8
            values = block[half // 2, 0, low:low + 8].reshape(BLOCK, BLOCK).astype(F32)
            if at < 4:
                joined[:, at * WIDTH + half * BLOCK:at * WIDTH + (half + 1) * BLOCK] = values
            else:
                out[:, half * BLOCK:(half + 1) * BLOCK] = values


def local(inputs, history, lengths, w_joined, w_out, neg_emb, neg_ids):
    n_here, block, width = inputs.shape
    n_seq = lax.axis_size("seq")
    length = n_seq * block
    lanes = 2 * HEAD
    rows = n_here * block
    n_neg = neg_emb.shape[0]
    dma = pltpu.SemaphoreType.DMA
    buffers = dict(
        xn=((n_here, block, width), BF16), xnt=((width, rows), BF16), u=((n_here, block, width), BF16),
        slope=((n_here, block, 4 * width), BF16), d_pre=((rows, 4 * width), BF16),
        send=((n_seq, BLOCK + HEAD, lanes), BF16), got=((n_seq, BLOCK + HEAD, lanes), BF16),
        att_send=((n_seq, HEAD, lanes), BF16), att_got=((n_seq, HEAD, lanes), BF16),
        datt_send=((n_seq, HEAD, lanes), BF16), datt_got=((n_seq, HEAD, lanes), BF16),
        grad_send=((n_seq, BLOCK + HEAD, lanes), BF16), grad_got=((n_seq, BLOCK + HEAD, lanes), BF16),
        first=((n_here, 16, width), BF16), ids=((2 * n_here, block), jnp.int32),
        next_ids=((2 * n_here, block), jnp.int32), negs=((4, n_neg, width), BF16),
        all_ids=((4, 2 * n_here, block), jnp.int32),
        k0=((length, lanes), BF16), v0=((length, lanes), BF16), qa=((length, lanes), BF16),
        kt=((HEAD, length), BF16), acc=((FQ, lanes), F32), dq=((HEAD, length), F32), dkv=((BM, lanes), F32),
        att=((2 * block, width), F32), exps=((2 * block, 4 * n_neg), F32), grad_out=((width, width), F32),
        loss=((8, block), F32), loss_core=((8, block), F32), loss_sum=((3, 8, block), F32),
        loss_all=((3, 4, 8, block), F32), x=((n_here, block, width), BF16),
        w_joined=((width, 4 * width), BF16), w_out=((width, width), BF16), neg_emb=((n_neg, width), BF16),
        history=((n_here, block), jnp.int32), neg_ids=((n_here, block), jnp.int32),
    )
    wide = (4, 16, 16, block)
    for name in "uovkq":
        buffers[name + "_part"] = ((2,) + wide, BF16)
        for tail in ("_core", "_sum", "_got"):
            buffers[name + tail] = (wide, BF16)
        for tail in ("_sum2", "_got2"):
            buffers[name + tail] = (wide[1:], BF16)
        buffers[name + "_red"] = (wide[2:], BF16)
    sems = dict(
        send_sem=13, one_sem=8, got_sem=n_seq, att_sem=n_seq, datt_sem=n_seq, grad_sem=2, loss_sem=8,
        red_send=30, red_recv=30, load_sem=6,
    )
    takes = ("lens", "x_in", "history_in", "neg_ids_in", "w_joined_in", "w_out_in", "neg_emb_in")
    gives = {name + "_full": ((2,) + wide, BF16) for name in "uvqko"}
    gives["loss_out"] = ((1,), F32)
    names = takes + tuple(gives) + tuple(buffers) + tuple(sems)
    *grads, loss = pl.pallas_call(
        functools.partial(kernel, n_seq, names),
        out_shape=[jax.ShapeDtypeStruct(*kind) for kind in gives.values()],
        in_specs=[SMEM] + [pl.BlockSpec(memory_space=pl.ANY)] * (len(takes) - 1),
        out_specs=[VMEM] * 5 + [SMEM],
        scratch_shapes=[pltpu.VMEM(*kind) for kind in buffers.values()]
        + [dma((count,)) for count in sems.values()],
        compiler_params=pltpu.CompilerParams(
            collective_id=0, has_side_effects=True, vmem_limit_bytes=60 * 1024 * 1024
        ),
    )(lengths, inputs, history, neg_ids.reshape(-1, block), w_joined, w_out, neg_emb)
    taken = pl.BlockSpec((2, 1) + wide[1:], lambda at: (0, at, 0, 0, 0))
    joined, out = pl.pallas_call(
        widen,
        grid=(4,),
        out_shape=[
            jax.ShapeDtypeStruct((width, 4 * width), F32), jax.ShapeDtypeStruct((width, width), F32)
        ],
        in_specs=[taken] * 5,
        out_specs=[
            pl.BlockSpec((width // 4, 4 * width), lambda at: (at, 0)),
            pl.BlockSpec((width // 4, width), lambda at: (at, 0)),
        ],
        compiler_params=pltpu.CompilerParams(vmem_limit_bytes=32 * 1024 * 1024),
    )(*grads)
    return (joined, out, loss.reshape(()))


def solution(mesh):
    placed = (
        P("grp", "seq", None),
        P("grp", "seq"),
        P(),
        P(),
        P(),
        P(("grp", "seq"), None),
        P(("grp", "seq")),
    )
    return jax.shard_map(
        local, mesh=mesh, in_specs=placed, out_specs=(P(), P(), P()), check_vma=False
    )
```

```python
import functools
import types

import jax
import jax.numpy as jnp
from jax import lax
from jax.experimental import pallas as pl
from jax.experimental.pallas import tpu as pltpu
from jax.sharding import PartitionSpec as P

HEADS = 8
HEAD = 64
WIDTH = 512
PAIRS = 4
BLOCK = 128
TILE = 512
FQ = TILE
BM = TILE
eps_norm = 1e-06
logit_scale = 64.0

MESH = pl.DeviceIdType.MESH
F32 = jnp.float32
BF16 = jnp.bfloat16
VMEM = pl.BlockSpec(memory_space=pltpu.VMEM)
SMEM = pl.BlockSpec(memory_space=pltpu.SMEM)


def dot_nn(a, b):
    return lax.dot_general(a, b, (((1,), (0,)), ((), ())), preferred_element_type=F32)


def dot_nt(a, b):
    return lax.dot_general(a, b, (((1,), (1,)), ((), ())), preferred_element_type=F32)


def dot_tn(a, b):
    return lax.dot_general(a, b, (((0,), (0,)), ((), ())), preferred_element_type=F32)


def low_lanes(shape):
    return lax.broadcasted_iota(jnp.int32, shape, 1) < HEAD


def turned(a):
    return pltpu.roll(a, HEAD, axis=1)


def swapped(a, b):
    low = low_lanes(a.shape)
    return jnp.where(low, a, turned(b)), jnp.where(low, turned(a), b)


def copy_to(src, dst, send_sem, recv_sem, where):
    pltpu.make_async_remote_copy(
        src_ref=src, dst_ref=dst, send_sem=send_sem, recv_sem=recv_sem,
        device_id=where, device_id_type=MESH,
    ).start()


def await_bytes(ref, sem):
    pltpu.make_async_copy(ref, ref, sem).wait()


def aligned(at, size):
    return pl.ds(pl.multiple_of(at, size), size)


def pair_cols(pair):
    return slice(pair * 2 * HEAD, (pair + 1) * 2 * HEAD)


def shifts(n_seq):
    side = int((n_seq // 2) ** 0.5)
    steps = [(x, y, z) for x in range(side) for y in range(side) for z in range(2)]
    return sorted(steps[1:], key=lambda at: -(min(at[0], side - at[0]) + min(at[1], side - at[1]) + at[2]))


def peer(me, shift):
    x, y, z = me // HEADS, lax.rem(me // 2, 4), lax.rem(me, 2)
    return (lax.rem(x + shift[0], 4) * 4 + lax.rem(y + shift[1], 4)) * 2 + lax.rem(z + shift[2], 2)


def cover(first, count, body):
    done = 0
    for tiles in (4, 2, 1):
        n = count // tiles if tiles == 4 else lax.rem(count // tiles, 2)

        @pl.loop(0, n)
        def _(at, done=done, tiles=tiles):
            body((first + done + at * tiles) * TILE, tiles * TILE)

        done = done + n * tiles


def tile_at(first, step, tiles):
    low = lax.rem(first + step // 2, tiles // 2)
    odd = lax.rem(step, 2)
    return low + odd * (tiles - 1 - 2 * low)


def kernel(n_seq, names, *refs):
    r = types.SimpleNamespace(**dict(zip(names, refs, strict=True)))
    me = lax.axis_index("seq")
    grp = lax.axis_index("grp")
    core, z_hi = lax.rem(grp, 2), grp // 2
    loads = [
        pltpu.make_async_copy(getattr(r, name + "_in"), getattr(r, name), r.load_sem.at[at])
        for at, name in enumerate(("x", "w_joined", "history", "neg_ids", "neg_emb", "w_out"))
    ]
    for load in loads:
        load.start()
    n_here = r.x.shape[0]
    planes = n_seq // HEADS
    length = n_seq * BLOCK
    mate = {"grp": grp + 1 - 2 * core}
    other_z = {"grp": (1 - z_hi) * 2 + core}
    others = pl.ds(0, n_seq - 1)
    x_at, y_at, z_at = me // HEADS, lax.rem(me // 2, 4), z_hi * 2 + lax.rem(me, 2)

    barrier = pltpu.get_barrier_semaphore()

    def greet(where):
        pl.semaphore_signal(barrier, inc=1, device_id=where, device_id_type=MESH)

    greet(mate)

    @pl.loop(1, n_seq)
    def _(step):
        greet({"seq": lax.rem(me + step, n_seq)})

    for step in range(4):
        for z in range(2):
            greet(dict(other_z, seq=(x_at * 4 + lax.rem(y_at + step, 4)) * 2 + z))
            if step:
                greet(dict(other_z, seq=(lax.rem(x_at + step, 4) * 4 + y_at) * 2 + z))

    def lane(axis, along):
        x, y, z = (along if axis == name else at for name, at in (("x", x_at), ("y", y_at), ("z", z_at)))
        return {"grp": z // 2 * 2 + 1 - core, "seq": (x * 4 + y) * 2 + lax.rem(z, 2)}

    for axis, at in (("x", x_at), ("y", y_at), ("z", z_at)):
        for step in range(1, 4):
            greet(lane(axis, lax.rem(at + step, 4)))
    n_peers = n_seq + 14 + 9

    loads[0].wait()
    loads[1].wait()

    @pl.loop(0, n_here)
    def _(b):
        x = r.x[b].astype(F32)
        centered = x - jnp.mean(x, axis=-1, keepdims=True)
        var = jnp.mean(centered * centered, axis=-1, keepdims=True)
        xn = (centered * lax.rsqrt(var + eps_norm)).astype(BF16)
        r.xn[b] = xn
        v, q, k = (activated(r, b, xn, part) for part in (1, 2, 3))
        for pair in range(PAIRS):
            cols = pair_cols(pair)
            kv = swapped(k[:, cols], v[:, cols])
            qs = swapped(q[:HEAD, cols], q[HEAD:, cols])
            for odd in range(2):
                j = b * HEADS + 2 * pair + odd
                r.send[j, :BLOCK] = kv[odd].astype(BF16)
                r.send[j, BLOCK:] = qs[odd].astype(BF16)

    pl.semaphore_wait(barrier, n_peers)
    for shift in shifts(n_seq):
        j = peer(me, shift)
        copy_to(r.send.at[j], r.got.at[me], r.send_sem.at[0], r.got_sem.at[me], {"seq": j})
    r.got[me] = r.send[me]

    before = {"seq": lax.rem(me + n_seq - 1, n_seq)}
    loads[2].wait()
    loads[3].wait()
    r.ids[:n_here] = r.history[...]
    r.ids[n_here:] = r.neg_ids[...]
    copy_to(r.x.at[:, pl.ds(0, 16)], r.first, r.send_sem.at[1], r.one_sem.at[0], before)
    copy_to(r.ids, r.next_ids, r.send_sem.at[2], r.one_sem.at[1], before)

    loads[4].wait()
    loads[5].wait()

    @pl.loop(0, n_here)
    def _(b):
        xn = r.xn[b]
        r.u[b] = activated(r, b, xn, 0).astype(BF16)
        r.xnt[:, aligned(b * BLOCK, BLOCK)] = jnp.transpose(xn.astype(F32)).astype(BF16)
        rows = aligned(b * BLOCK, BLOCK)
        emb = r.neg_emb[rows].astype(F32)
        r.negs[grp, rows] = (
            emb * lax.rsqrt(jnp.sum(emb * emb, axis=-1, keepdims=True) + eps_norm)
        ).astype(BF16)

    r.all_ids[grp] = r.ids[...]

    seq_len = r.lens[grp * n_here + me // HEADS]
    low = low_lanes((HEAD, 2 * HEAD))
    low_block = low_lanes((BLOCK, 2 * HEAD))

    @pl.loop(0, planes)
    def _(step):
        first = lax.rem(me // HEADS + planes // 2 + step, planes) * HEADS

        @pl.loop(0, HEADS)
        def _(turn):
            i = first + turn

            @pl.when(i != me)
            def _():
                await_bytes(r.got.at[0], r.got_sem.at[i])

        @pl.loop(0, HEADS, unroll=4)
        def _(turn):
            i = first + turn
            rows = aligned(i * BLOCK, BLOCK)
            pos = i * BLOCK + lax.broadcasted_iota(jnp.int32, (BLOCK, 2 * HEAD), 0)
            kv = jnp.where(pos < seq_len, r.got[i, :BLOCK].astype(F32), 0.0)
            r.k0[rows] = jnp.where(low_block, 0.5 * kv, 0.0).astype(BF16)
            r.v0[rows] = jnp.where(low_block, 0.0, kv).astype(BF16)
            r.kt[:, rows] = jnp.transpose(kv)[:HEAD].astype(BF16)
            q = r.got[i, BLOCK:].astype(F32)
            r.qa[rows] = jnp.concatenate(
                [jnp.where(low, q, 0.0), jnp.where(low, turned(q), 0.0)], axis=0
            ).astype(BF16)

    copy_to(r.negs.at[grp], r.negs.at[grp], r.send_sem.at[3], r.one_sem.at[2], mate)
    copy_to(r.all_ids.at[grp], r.all_ids.at[grp], r.send_sem.at[4], r.one_sem.at[3], mate)
    copy_to(r.negs.at[grp], r.negs.at[grp], r.send_sem.at[5], r.one_sem.at[4], other_z)
    copy_to(r.all_ids.at[grp], r.all_ids.at[grp], r.send_sem.at[6], r.one_sem.at[5], other_z)
    await_bytes(r.send.at[others], r.send_sem.at[0])
    inv_len = 1.0 / jnp.full((1, 2 * HEAD), seq_len, jnp.int32).astype(F32)

    f_tiles = length // FQ
    f_per = FQ // BLOCK

    @pl.loop(0, f_tiles)
    def _(step):
        c = tile_at(me // f_per, f_tiles - 1 - step, f_tiles)
        q = r.qa[aligned(c * FQ, FQ)]

        def piece(start, size, masked):
            rows = pl.ds(pl.multiple_of(start, TILE), size)
            half = dot_nt(q, r.k0[rows])
            if masked:
                ahead = lax.broadcasted_iota(jnp.int32, (FQ, size), 1) - lax.broadcasted_iota(
                    jnp.int32, (FQ, size), 0
                )
                half = jnp.where(ahead <= 0, half, 0.0)
            probs = (half + half * jnp.tanh(half)).astype(BF16)
            return dot_nn(probs, r.v0[rows])

        r.acc[...] = piece(c * FQ, FQ, True)

        def more(start, size):
            r.acc[...] += piece(start, size, False)

        cover(0, c, more)
        for u in range(f_per):
            out = r.acc[u * BLOCK:(u + 1) * BLOCK] * inv_len
            top, bottom = out[:HEAD], out[HEAD:]
            r.att_send[c * f_per + u] = jnp.where(low, turned(top), bottom).astype(BF16)

        @pl.loop(0, f_per)
        def _(turn):
            i = c * f_per + lax.rem(me + turn, f_per)

            @pl.when(i != me)
            def _():
                copy_to(
                    r.att_send.at[i], r.att_got.at[me], r.send_sem.at[7], r.att_sem.at[me], {"seq": i}
                )

            @pl.when(i == me)
            def _():
                r.att_got[me] = r.att_send[me]

    far = (1 - z_hi) * 2 + core
    await_bytes(r.negs.at[0], r.one_sem.at[4])
    await_bytes(r.all_ids.at[0], r.one_sem.at[5])
    copy_to(r.negs.at[far], r.negs.at[far], r.send_sem.at[8], r.one_sem.at[6], mate)
    copy_to(r.all_ids.at[far], r.all_ids.at[far], r.send_sem.at[9], r.one_sem.at[7], mate)

    total = r.lens[0] - 1
    for at in range(1, r.lens.shape[0]):
        total = total + (r.lens[at] - 1)
    both = 2
    half_rows = both * BLOCK
    weight = 1.0 / jnp.full((half_rows, 1), total, jnp.int32).astype(F32)
    r.grad_out[...] = jnp.zeros_like(r.grad_out)
    r.loss[...] = jnp.zeros_like(r.loss)
    await_bytes(r.first, r.one_sem.at[0])
    await_bytes(r.ids, r.one_sem.at[1])
    await_bytes(r.negs.at[0], r.one_sem.at[2])
    await_bytes(r.all_ids.at[0], r.one_sem.at[3])
    await_bytes(r.negs.at[0], r.one_sem.at[6])
    await_bytes(r.all_ids.at[0], r.one_sem.at[7])
    n_halves = n_here // both

    @pl.loop(0, n_halves)
    def _(step):
        middle(r, n_seq, me, grp, both * lax.rem(me // (both * HEADS) + step, n_halves), weight)

    axes = dict(x=x_at, y=y_at, z=z_at)
    plane_at = dict(x=y_at * 4 + z_at, y=x_at * 4 + z_at, z=x_at * 4 + y_at)

    def chip(axis, along, across, of_core=core):
        hi, lo = across // 4, lax.rem(across, 4)
        x, y, z = dict(x=(along, hi, lo), y=(hi, along, lo), z=(hi, lo, along))[axis]
        return {"grp": z // 2 * 2 + of_core, "seq": (x * 4 + y) * 2 + lax.rem(z, 2)}

    def reduction(name, axis, at):
        part, got, sums, got2, red, full = (
            getattr(r, name + tail) for tail in ("_part", "_got", "_sum", "_got2", "_red", "_full")
        )
        send = [r.red_send.at[at * 4 + k] for k in range(4)]
        recv = [r.red_recv.at[at * 4 + k] for k in range(4)]
        along, across = axes[axis], plane_at[axis]
        mine = core * 4 + along
        seven, fifteen = pl.ds(0, 7), pl.ds(0, 15)

        def along_axis(source, target, sems):
            @pl.loop(1, 8)
            def _(step):
                to = lax.rem(mine + step, 8)
                copy_to(source(to), target, *sems, chip(axis, lax.rem(to, 4), across, to // 4))

        def over_plane(source, target, sems):
            @pl.loop(1, 16)
            def _(step):
                to = lax.rem(across + step, 16)
                copy_to(source(to), target, *sems, chip(axis, along, to))

        def scatter(grad):
            for half in range(4):
                block = grad[:, half * BLOCK:(half + 1) * BLOCK].astype(BF16)
                low, first = half % 2 * 8, half // 2 * 4
                part[first:first + 4, low:low + 8] = block.reshape(4, 8, 16, BLOCK)
            along_axis(lambda to: part.at[to], got.at[mine], (send[0], recv[0]))

        def plane():
            got[mine] = part[mine]
            await_bytes(got.at[seven], recv[0])
            sums[...] = jnp.sum(got[...].astype(F32), axis=0).astype(BF16)
            over_plane(lambda to: sums.at[to], got2.at[across], (send[1], recv[1]))

        def gather():
            got2[across] = sums[across]
            await_bytes(got2.at[fifteen], recv[1])
            red[...] = jnp.sum(got2[...].astype(F32), axis=0).astype(BF16)
            full[mine, across] = red[...]
            over_plane(lambda to: red, full.at[mine, across], (send[2], recv[2]))

        def spread():
            await_bytes(got2.at[fifteen], recv[2])
            along_axis(lambda to: full.at[mine], full.at[mine], (send[3], recv[3]))

        def finish():
            await_bytes(got.at[seven], recv[3])
            await_bytes(got.at[seven], send[0])
            await_bytes(got2.at[fifteen], send[1])
            await_bytes(got2.at[fifteen], send[2])
            await_bytes(got.at[seven], send[3])

        return types.SimpleNamespace(scatter=scatter, plane=plane, gather=gather, spread=spread, finish=finish)

    early = [reduction("u", "x", 0), reduction("o", "y", 1)]
    early[0].scatter(dot_nn(r.xnt[...], r.d_pre[:, :WIDTH]))
    early[1].scatter(r.grad_out[...])
    copy_to(r.loss, r.loss_core, r.loss_sem.at[0], r.loss_sem.at[1], mate)

    def loss_along(axis, value, at):
        r.loss_all[at, axes[axis]] = value
        r.loss_sum[at] = value
        for step in range(1, 4):
            copy_to(
                r.loss_sum.at[at], r.loss_all.at[at, axes[axis]],
                r.loss_sem.at[2 + 2 * at], r.loss_sem.at[3 + 2 * at],
                chip(axis, lax.rem(axes[axis] + step, 4), plane_at[axis]),
            )

    def loss_over(at):
        await_bytes(r.loss_all.at[at, pl.ds(0, 3)], r.loss_sem.at[3 + 2 * at])
        return jnp.sum(r.loss_all[at], axis=0)

    @pl.loop(0, n_seq)
    def _(step):
        i = lax.rem(me + step, n_seq)

        @pl.when(i != me)
        def _():
            await_bytes(r.datt_got.at[0], r.datt_sem.at[i])

    @pl.loop(0, n_seq, unroll=4)
    def _(i):
        d_att = r.datt_got[i].astype(F32)
        rows = aligned(i * BLOCK, BLOCK)
        qa = r.qa[rows].astype(F32)
        r.qa[rows] = jnp.where(
            low_block, qa, jnp.concatenate([turned(d_att), d_att], axis=0)
        ).astype(BF16)

    r.dq[...] = jnp.zeros_like(r.dq)
    b_tiles = length // BM
    b_per = BM // BLOCK
    kv_scale = jnp.where(low_lanes((1, 2 * HEAD)), 0.5 * inv_len, inv_len)

    def send_d_q(low, high):
        @pl.loop(low, high)
        def _(c):
            for u in range(b_per):
                d_q = r.dq[:, aligned((c * b_per + u) * BLOCK, BLOCK)] * (0.5 * inv_len)
                r.grad_send[c * b_per + u, BLOCK:] = d_q.astype(BF16)

            @pl.loop(0, b_per)
            def _(turn):
                i = c * b_per + lax.rem(me + turn, b_per)

                @pl.when(i != me)
                def _():
                    copy_to(
                        r.grad_send.at[i, pl.ds(BLOCK, HEAD)], r.grad_got.at[me, pl.ds(BLOCK, HEAD)],
                        r.send_sem.at[11], r.grad_sem.at[1], {"seq": i},
                    )

                @pl.when(i == me)
                def _():
                    r.grad_got[me, BLOCK:] = r.grad_send[me, BLOCK:]

    @pl.loop(0, b_tiles)
    def _(step):
        c = tile_at(me // b_per, step, b_tiles)
        m_rows = aligned(c * BM, BM)
        low_tile = low_lanes((BM, 2 * HEAD))

        def piece(start, size, masked):
            t_rows = pl.ds(pl.multiple_of(start, TILE), size)
            qa = r.qa[t_rows]
            half = dot_nt(r.k0[m_rows], qa)
            d_probs = dot_nt(r.v0[m_rows], qa)
            if masked:
                ahead = lax.broadcasted_iota(jnp.int32, (BM, size), 0) - lax.broadcasted_iota(
                    jnp.int32, (BM, size), 1
                )
                half = jnp.where(ahead <= 0, half, 0.0)
                d_probs = jnp.where(ahead <= 0, d_probs, 0.0)
            up = 1.0 + jnp.tanh(half)
            probs = half * up
            d_scores = (d_probs * up * (1.0 + (half + half) - probs)).astype(BF16)
            r.dq[:, t_rows] += dot_nn(r.kt[:, m_rows], d_scores)
            return jnp.where(low_tile, dot_nn(d_scores, qa), dot_nn(probs.astype(BF16), qa))

        r.dkv[...] = piece(c * BM, BM, True)

        def more(start, size):
            r.dkv[...] += piece(start, size, False)

        cover(c + 1, b_tiles - 1 - c, more)
        for u in range(b_per):
            r.grad_send[c * b_per + u, :BLOCK] = (
                r.dkv[u * BLOCK:(u + 1) * BLOCK] * kv_scale
            ).astype(BF16)

        @pl.loop(0, b_per)
        def _(turn):
            i = c * b_per + lax.rem(me + turn, b_per)

            @pl.when(i != me)
            def _():
                copy_to(
                    r.grad_send.at[i, pl.ds(0, BLOCK)], r.grad_got.at[me, pl.ds(0, BLOCK)],
                    r.send_sem.at[10], r.grad_sem.at[0], {"seq": i},
                )

            @pl.when(i == me)
            def _():
                r.grad_got[me, :BLOCK] = r.grad_send[me, :BLOCK]

        for at, stage in enumerate(("plane", "gather", "spread", "")):
            @pl.when(step == 2 * at + 1)
            def _(at=at, stage=stage):
                if stage:
                    for one in early:
                        getattr(one, stage)()
                if at == 0:
                    await_bytes(r.loss_core, r.loss_sem.at[1])
                    loss_along("x", r.loss[...] + r.loss_core[...], 0)
                if at == 1:
                    loss_along("y", loss_over(0), 1)
                if at == 2:
                    loss_along("z", loss_over(1), 2)
                if at == 3:
                    count = jnp.full((8, BLOCK), total, jnp.int32).astype(F32)
                    r.loss_out[0] = (loss_over(2) / count)[0, 0]

        end = tile_at(me // b_per, b_tiles - 1, b_tiles)

        @pl.when(step == b_tiles - 2)
        def _():
            send_d_q(0, end)

        @pl.when(step == b_tiles - 1)
        def _():
            send_d_q(end, b_tiles)

    late = [reduction("v", "x", 2), reduction("k", "y", 3), reduction("q", "z", 4)]
    await_bytes(r.grad_got.at[others, pl.ds(0, BLOCK)], r.grad_sem.at[0])

    @pl.loop(0, n_here)
    def _(b):
        rows = aligned(b * BLOCK, BLOCK)
        for pair in range(PAIRS):
            j = b * HEADS + 2 * pair
            d_k, d_v = swapped(r.grad_got[j, :BLOCK].astype(F32), r.grad_got[j + 1, :BLOCK].astype(F32))
            for part, grad in ((1, d_v), (3, d_k)):
                at = part * WIDTH + pair * 2 * HEAD
                slope = r.slope[b, :, at:at + 2 * HEAD].astype(F32)
                r.d_pre[rows, at:at + 2 * HEAD] = (grad * slope).astype(BF16)

    late[0].scatter(dot_nn(r.xnt[...], r.d_pre[:, WIDTH:2 * WIDTH]))
    late[1].scatter(dot_nn(r.xnt[...], r.d_pre[:, 3 * WIDTH:]))
    await_bytes(r.grad_got.at[others, pl.ds(BLOCK, HEAD)], r.grad_sem.at[1])

    @pl.loop(0, n_here)
    def _(b):
        rows = aligned(b * BLOCK, BLOCK)
        for pair in range(PAIRS):
            j = b * HEADS + 2 * pair
            at = 2 * WIDTH + pair * 2 * HEAD
            grad = jnp.transpose(
                jnp.concatenate([r.grad_got[j + e, BLOCK:].astype(F32) for e in range(2)], axis=0)
            )
            slope = r.slope[b, :, at:at + 2 * HEAD].astype(F32)
            r.d_pre[rows, at:at + 2 * HEAD] = (grad * slope).astype(BF16)

    late[2].scatter(dot_nn(r.xnt[...], r.d_pre[:, 2 * WIDTH:3 * WIDTH]))
    for stage in ("plane", "gather", "spread"):
        for one in late:
            getattr(one, stage)()

    for one in early + late:
        one.finish()

    await_bytes(r.first, r.send_sem.at[1])
    await_bytes(r.ids, r.send_sem.at[2])
    for at in (3, 5, 8):
        await_bytes(r.negs.at[0], r.send_sem.at[at])
        await_bytes(r.all_ids.at[0], r.send_sem.at[at + 1])
    await_bytes(r.att_send.at[others], r.send_sem.at[7])
    await_bytes(r.datt_send.at[others], r.send_sem.at[12])
    await_bytes(r.grad_send.at[others, pl.ds(0, BLOCK)], r.send_sem.at[10])
    await_bytes(r.grad_send.at[others, pl.ds(BLOCK, HEAD)], r.send_sem.at[11])
    await_bytes(r.loss, r.loss_sem.at[0])
    for at in range(3):
        await_bytes(r.loss_all.at[at, pl.ds(0, 3)], r.loss_sem.at[2 + 2 * at])


def activated(r, b, xn, part):
    half = 0.5 * dot_nn(xn, r.w_joined[:, part * WIDTH:(part + 1) * WIDTH])
    th = jnp.tanh(half)
    slope = (0.5 + 0.5 * th) * (1.0 + half * (1.0 - th))
    r.slope[b, :, part * WIDTH:(part + 1) * WIDTH] = slope.astype(BF16)
    return half + half * th


def middle(r, n_seq, me, grp, first_b, weight):
    both = 2
    rows = both * BLOCK
    n_here = r.x.shape[0]
    n_grp, n_neg = r.negs.shape[:2]

    def joined(make):
        return jnp.concatenate([make(e) for e in range(both)], axis=0)

    @pl.loop(0, both * HEADS)
    def _(turn):
        j = first_b * HEADS + turn

        @pl.when(j != me)
        def _():
            await_bytes(r.att_got.at[0], r.att_sem.at[j])

    for e in range(both):
        for pair in range(PAIRS):
            j = (first_b + e) * HEADS + 2 * pair
            top, bottom = swapped(r.att_got[j].astype(F32), r.att_got[j + 1].astype(F32))
            r.att[e * BLOCK:e * BLOCK + HEAD, pair_cols(pair)] = top
            r.att[e * BLOCK + HEAD:(e + 1) * BLOCK, pair_cols(pair)] = bottom

    att = r.att[...]
    centered = att - jnp.mean(att, axis=-1, keepdims=True)
    inv_att = lax.rsqrt(jnp.mean(centered * centered, axis=-1, keepdims=True) + eps_norm)
    normed = centered * inv_att
    u = joined(lambda e: r.u[first_b + e]).astype(F32)
    gated = (normed * u).astype(BF16)
    x = joined(lambda e: r.x[first_b + e]).astype(F32)
    out_rows = x + dot_nn(gated, r.w_out[...])
    inv_y = lax.rsqrt(jnp.sum(out_rows * out_rows, axis=-1, keepdims=True) + eps_norm)
    unit_y = out_rows * inv_y
    unit_b = unit_y.astype(BF16)
    more = jnp.where(me == n_seq - 1, 0, 1)
    last_row = lax.broadcasted_iota(jnp.int32, (BLOCK, WIDTH), 0) == BLOCK - 1
    last_lane = lax.broadcasted_iota(jnp.int32, (1, BLOCK), 1) == BLOCK - 1

    def next_rows(e):
        shifted = pltpu.roll(r.x[first_b + e].astype(F32), BLOCK - 1, axis=0)
        return jnp.where(last_row, r.first[first_b + e].astype(F32)[:1] * more.astype(F32), shifted)

    x_next = joined(next_rows)
    pos_unit = (
        x_next * lax.rsqrt(jnp.sum(x_next * x_next, axis=-1, keepdims=True) + eps_norm)
    ).astype(BF16).astype(F32)
    pos_logit = logit_scale * jnp.sum(unit_b.astype(F32) * pos_unit, axis=-1, keepdims=True)

    def row_ids(e):
        shifted = pltpu.roll(r.ids[pl.ds(first_b + e, 1)], BLOCK - 1, axis=1)
        coming = pltpu.roll(r.next_ids[pl.ds(first_b + e, 1)], BLOCK - 1, axis=1) * more
        return jnp.transpose(jnp.broadcast_to(jnp.where(last_lane, coming, shifted), (BLOCK, BLOCK)))

    ids = joined(row_ids)
    lane_sum = jnp.zeros((rows, BLOCK), F32)
    for g in range(n_grp):
        neg_logit = logit_scale * dot_nt(unit_b, r.negs[g])
        for sub in range(n_neg // BLOCK):
            at = (g * n_neg) + sub * BLOCK
            hit = r.all_ids[g, n_here + sub:n_here + sub + 1] == ids
            exps = jnp.where(hit, 0.0, jnp.exp(neg_logit[:, sub * BLOCK:(sub + 1) * BLOCK]))
            r.exps[:, at:at + BLOCK] = exps
            lane_sum = lane_sum + exps
    pos_exp = jnp.exp(pos_logit)
    denom = pos_exp + jnp.sum(lane_sum, axis=-1, keepdims=True)

    def row_valid(e):
        pos = me * BLOCK + lax.broadcasted_iota(jnp.int32, (BLOCK, 1), 0)
        return jnp.where(pos + 1 < r.lens[grp * n_here + first_b + e], 1.0, 0.0)

    valid = joined(row_valid)
    row_loss = jnp.where(valid > 0.0, jnp.log(denom) - pos_logit, 0.0)
    r.loss[...] += jnp.broadcast_to(jnp.sum(row_loss, axis=0, keepdims=True), r.loss.shape)
    row_weight = valid * weight
    d_pos = row_weight * (pos_exp / denom - 1.0)
    scale = row_weight / denom
    neg_back = jnp.zeros((rows, WIDTH), F32)
    for g in range(n_grp):
        d_neg = (scale * r.exps[:, g * n_neg:(g + 1) * n_neg]).astype(BF16)
        neg_back = neg_back + dot_nn(d_neg, r.negs[g])
    d_unit = logit_scale * (d_pos * pos_unit + neg_back)
    d_out = (
        (d_unit - unit_y * jnp.sum(unit_y * d_unit, axis=-1, keepdims=True)) * inv_y
    ).astype(BF16)
    d_gate = dot_nt(d_out, r.w_out[...])
    d_norm = d_gate * u
    d_att = inv_att * (
        d_norm
        - jnp.mean(d_norm, axis=-1, keepdims=True)
        - normed * jnp.mean(d_norm * normed, axis=-1, keepdims=True)
    )
    for e in range(both):
        rows_e = d_att[e * BLOCK:(e + 1) * BLOCK]
        for pair in range(PAIRS):
            cols = pair_cols(pair)
            packed = swapped(rows_e[:HEAD, cols], rows_e[HEAD:, cols])
            for odd in range(2):
                r.datt_send[(first_b + e) * HEADS + 2 * pair + odd] = packed[odd].astype(BF16)

    @pl.loop(0, both * HEADS)
    def _(turn):
        j = first_b * HEADS + lax.rem(me + turn, both * HEADS)

        @pl.when(j != me)
        def _():
            copy_to(
                r.datt_send.at[j], r.datt_got.at[me], r.send_sem.at[12], r.datt_sem.at[me], {"seq": j}
            )

        @pl.when(j == me)
        def _():
            r.datt_got[me] = r.datt_send[me]

    r.grad_out[...] += dot_tn(gated, d_out)
    d_u = d_gate * normed
    for e in range(both):
        slope = r.slope[first_b + e, :, :WIDTH].astype(F32)
        r.d_pre[aligned((first_b + e) * BLOCK, BLOCK), :WIDTH] = (
            d_u[e * BLOCK:(e + 1) * BLOCK] * slope
        ).astype(BF16)


def widen(*refs):
    *blocks, joined, out = refs
    for at, block in enumerate(blocks):
        for half in range(4):
            low = half % 2 * 8
            values = block[half // 2, 0, low:low + 8].reshape(BLOCK, BLOCK).astype(F32)
            if at < 4:
                joined[:, at * WIDTH + half * BLOCK:at * WIDTH + (half + 1) * BLOCK] = values
            else:
                out[:, half * BLOCK:(half + 1) * BLOCK] = values


def local(inputs, history, lengths, w_joined, w_out, neg_emb, neg_ids):
    n_here, block, width = inputs.shape
    n_seq = lax.axis_size("seq")
    length = n_seq * block
    lanes = 2 * HEAD
    rows = n_here * block
    n_neg = neg_emb.shape[0]
    dma = pltpu.SemaphoreType.DMA
    buffers = dict(
        xn=((n_here, block, width), BF16), xnt=((width, rows), BF16), u=((n_here, block, width), BF16),
        slope=((n_here, block, 4 * width), BF16), d_pre=((rows, 4 * width), BF16),
        send=((n_seq, BLOCK + HEAD, lanes), BF16), got=((n_seq, BLOCK + HEAD, lanes), BF16),
        att_send=((n_seq, HEAD, lanes), BF16), att_got=((n_seq, HEAD, lanes), BF16),
        datt_send=((n_seq, HEAD, lanes), BF16), datt_got=((n_seq, HEAD, lanes), BF16),
        grad_send=((n_seq, BLOCK + HEAD, lanes), BF16), grad_got=((n_seq, BLOCK + HEAD, lanes), BF16),
        first=((n_here, 16, width), BF16), ids=((2 * n_here, block), jnp.int32),
        next_ids=((2 * n_here, block), jnp.int32), negs=((4, n_neg, width), BF16),
        all_ids=((4, 2 * n_here, block), jnp.int32),
        k0=((length, lanes), BF16), v0=((length, lanes), BF16), qa=((length, lanes), BF16),
        kt=((HEAD, length), BF16), acc=((FQ, lanes), F32), dq=((HEAD, length), F32), dkv=((BM, lanes), F32),
        att=((2 * block, width), F32), exps=((2 * block, 4 * n_neg), F32), grad_out=((width, width), F32),
        loss=((8, block), F32), loss_core=((8, block), F32), loss_sum=((3, 8, block), F32),
        loss_all=((3, 4, 8, block), F32), x=((n_here, block, width), BF16),
        w_joined=((width, 4 * width), BF16), w_out=((width, width), BF16), neg_emb=((n_neg, width), BF16),
        history=((n_here, block), jnp.int32), neg_ids=((n_here, block), jnp.int32),
    )
    wide = (8, 16, 16, block)
    for name in "uovkq":
        buffers[name + "_part"] = buffers[name + "_got"] = (wide, BF16)
        buffers[name + "_sum"] = buffers[name + "_got2"] = (wide[1:], BF16)
        buffers[name + "_red"] = (wide[2:], BF16)
    sems = dict(
        send_sem=13, one_sem=8, got_sem=n_seq, att_sem=n_seq, datt_sem=n_seq, grad_sem=2, loss_sem=8,
        red_send=20, red_recv=20, load_sem=6,
    )
    takes = ("lens", "x_in", "history_in", "neg_ids_in", "w_joined_in", "w_out_in", "neg_emb_in")
    gives = {name + "_full": (wide, BF16) for name in "uvqko"}
    gives["loss_out"] = ((1,), F32)
    names = takes + tuple(gives) + tuple(buffers) + tuple(sems)
    *grads, loss = pl.pallas_call(
        functools.partial(kernel, n_seq, names),
        out_shape=[jax.ShapeDtypeStruct(*kind) for kind in gives.values()],
        in_specs=[SMEM] + [pl.BlockSpec(memory_space=pl.ANY)] * (len(takes) - 1),
        out_specs=[VMEM] * 5 + [SMEM],
        scratch_shapes=[pltpu.VMEM(*kind) for kind in buffers.values()]
        + [dma((count,)) for count in sems.values()],
        compiler_params=pltpu.CompilerParams(
            collective_id=0, has_side_effects=True, vmem_limit_bytes=60 * 1024 * 1024
        ),
    )(lengths, inputs, history, neg_ids.reshape(-1, block), w_joined, w_out, neg_emb)
    taken = pl.BlockSpec((2, 1) + wide[1:], lambda at: (0, at, 0, 0, 0))
    joined, out = pl.pallas_call(
        widen,
        grid=(4,),
        out_shape=[
            jax.ShapeDtypeStruct((width, 4 * width), F32), jax.ShapeDtypeStruct((width, width), F32)
        ],
        in_specs=[taken] * 5,
        out_specs=[
            pl.BlockSpec((width // 4, 4 * width), lambda at: (at, 0)),
            pl.BlockSpec((width // 4, width), lambda at: (at, 0)),
        ],
        compiler_params=pltpu.CompilerParams(vmem_limit_bytes=60 * 1024 * 1024),
    )(*(grad.reshape((2, 4) + wide[1:]) for grad in grads))
    return (joined, out, loss.reshape(()))


def solution(mesh):
    placed = (
        P("grp", "seq", None),
        P("grp", "seq"),
        P(),
        P(),
        P(),
        P(("grp", "seq"), None),
        P(("grp", "seq")),
    )
    return jax.shard_map(
        local, mesh=mesh, in_specs=placed, out_specs=(P(), P(), P()), check_vma=False
    )
```

```python
import functools
import types

import jax
import jax.numpy as jnp
from jax import lax
from jax.experimental import pallas as pl
from jax.experimental.pallas import tpu as pltpu
from jax.sharding import PartitionSpec as P

HEADS = 8
HEAD = 64
WIDTH = 512
PAIRS = 4
BLOCK = 128
TILE = 512
FQ = TILE
BM = TILE
eps_norm = 1e-06
logit_scale = 64.0

MESH = pl.DeviceIdType.MESH
F32 = jnp.float32
BF16 = jnp.bfloat16
VMEM = pl.BlockSpec(memory_space=pltpu.VMEM)
SMEM = pl.BlockSpec(memory_space=pltpu.SMEM)


def dot_nn(a, b):
    return lax.dot_general(a, b, (((1,), (0,)), ((), ())), preferred_element_type=F32)


def dot_nt(a, b):
    return lax.dot_general(a, b, (((1,), (1,)), ((), ())), preferred_element_type=F32)


def dot_tn(a, b):
    return lax.dot_general(a, b, (((0,), (0,)), ((), ())), preferred_element_type=F32)


def low_lanes(shape):
    return lax.broadcasted_iota(jnp.int32, shape, 1) < HEAD


def turned(a):
    return pltpu.roll(a, HEAD, axis=1)


def swapped(a, b):
    low = low_lanes(a.shape)
    return jnp.where(low, a, turned(b)), jnp.where(low, turned(a), b)


def copy_to(src, dst, send_sem, recv_sem, where):
    pltpu.make_async_remote_copy(
        src_ref=src, dst_ref=dst, send_sem=send_sem, recv_sem=recv_sem,
        device_id=where, device_id_type=MESH,
    ).start()


def await_bytes(ref, sem):
    pltpu.make_async_copy(ref, ref, sem).wait()


def aligned(at, size):
    return pl.ds(pl.multiple_of(at, size), size)


def pair_cols(pair):
    return slice(pair * 2 * HEAD, (pair + 1) * 2 * HEAD)


def shifts(n_seq):
    side = int((n_seq // 2) ** 0.5)
    steps = [(x, y, z) for x in range(side) for y in range(side) for z in range(2)]
    return sorted(steps[1:], key=lambda at: -(min(at[0], side - at[0]) + min(at[1], side - at[1]) + at[2]))


def peer(me, shift):
    x, y, z = me // HEADS, lax.rem(me // 2, 4), lax.rem(me, 2)
    return (lax.rem(x + shift[0], 4) * 4 + lax.rem(y + shift[1], 4)) * 2 + lax.rem(z + shift[2], 2)


def cover(first, count, body):
    done = 0
    for tiles in (4, 2):
        n = count // tiles if tiles == 4 else lax.rem(count // tiles, 2)

        @pl.loop(0, n)
        def _(at, done=done, tiles=tiles):
            body(first + done + at * tiles, tiles)

        done = done + n * tiles


def tile_at(first, step, tiles):
    low = lax.rem(first + step // 2, tiles // 2)
    odd = lax.rem(step, 2)
    return low + odd * (tiles - 1 - 2 * low)


def kernel(n_seq, names, *refs):
    r = types.SimpleNamespace(**dict(zip(names, refs, strict=True)))
    me = lax.axis_index("seq")
    grp = lax.axis_index("grp")
    core, z_hi = lax.rem(grp, 2), grp // 2
    loads = [
        pltpu.make_async_copy(getattr(r, name + "_in"), getattr(r, name), r.load_sem.at[at])
        for at, name in enumerate(("x", "w_joined", "history", "neg_ids", "neg_emb", "w_out"))
    ]
    for load in loads:
        load.start()
    n_here = r.x.shape[0]
    planes = n_seq // HEADS
    length = n_seq * BLOCK
    mate = {"grp": grp + 1 - 2 * core}
    other_z = {"grp": (1 - z_hi) * 2 + core}
    others = pl.ds(0, n_seq - 1)
    x_at, y_at, z_at = me // HEADS, lax.rem(me // 2, 4), z_hi * 2 + lax.rem(me, 2)

    barrier = pltpu.get_barrier_semaphore()

    def greet(where):
        pl.semaphore_signal(barrier, inc=1, device_id=where, device_id_type=MESH)

    greet(mate)

    @pl.loop(1, n_seq)
    def _(step):
        greet({"seq": lax.rem(me + step, n_seq)})

    for step in range(4):
        for z in range(2):
            greet(dict(other_z, seq=(x_at * 4 + lax.rem(y_at + step, 4)) * 2 + z))
            if step:
                greet(dict(other_z, seq=(lax.rem(x_at + step, 4) * 4 + y_at) * 2 + z))

    def lane(axis, along):
        x, y, z = (along if axis == name else at for name, at in (("x", x_at), ("y", y_at), ("z", z_at)))
        return {"grp": z // 2 * 2 + 1 - core, "seq": (x * 4 + y) * 2 + lax.rem(z, 2)}

    for axis, at in (("x", x_at), ("y", y_at), ("z", z_at)):
        for step in range(1, 4):
            greet(lane(axis, lax.rem(at + step, 4)))
    n_peers = n_seq + 14 + 9

    loads[0].wait()
    loads[1].wait()

    @pl.loop(0, n_here)
    def _(b):
        x = r.x[b].astype(F32)
        centered = x - jnp.mean(x, axis=-1, keepdims=True)
        var = jnp.mean(centered * centered, axis=-1, keepdims=True)
        xn = (centered * lax.rsqrt(var + eps_norm)).astype(BF16)
        r.xn[b] = xn
        v, q, k = (activated(r, b, xn, part) for part in (1, 2, 3))
        for pair in range(PAIRS):
            cols = pair_cols(pair)
            kv = swapped(k[:, cols], v[:, cols])
            qs = swapped(q[:HEAD, cols], q[HEAD:, cols])
            for odd in range(2):
                j = b * HEADS + 2 * pair + odd
                r.send[j, :BLOCK] = kv[odd].astype(BF16)
                r.send[j, BLOCK:] = qs[odd].astype(BF16)

    pl.semaphore_wait(barrier, n_peers)
    for shift in shifts(n_seq):
        j = peer(me, shift)
        copy_to(r.send.at[j], r.got.at[me], r.send_sem.at[0], r.got_sem.at[me], {"seq": j})
    r.got[me] = r.send[me]

    before = {"seq": lax.rem(me + n_seq - 1, n_seq)}
    loads[2].wait()
    loads[3].wait()
    r.ids[:n_here] = r.history[...]
    r.ids[n_here:] = r.neg_ids[...]
    copy_to(r.x.at[:, pl.ds(0, 16)], r.first, r.send_sem.at[1], r.one_sem.at[0], before)
    copy_to(r.ids, r.next_ids, r.send_sem.at[2], r.one_sem.at[1], before)

    loads[4].wait()
    loads[5].wait()

    @pl.loop(0, n_here)
    def _(b):
        xn = r.xn[b]
        r.u[b] = activated(r, b, xn, 0).astype(BF16)
        r.xnt[:, aligned(b * BLOCK, BLOCK)] = jnp.transpose(xn.astype(F32)).astype(BF16)
        rows = aligned(b * BLOCK, BLOCK)
        emb = r.neg_emb[rows].astype(F32)
        r.negs[grp, rows] = (
            emb * lax.rsqrt(jnp.sum(emb * emb, axis=-1, keepdims=True) + eps_norm)
        ).astype(BF16)

    r.all_ids[grp] = r.ids[...]

    seq_len = r.lens[grp * n_here + me // HEADS]
    low = low_lanes((HEAD, 2 * HEAD))
    low_block = low_lanes((BLOCK, 2 * HEAD))

    @pl.loop(0, planes)
    def _(step):
        first = lax.rem(me // HEADS + planes // 2 + step, planes) * HEADS

        @pl.loop(0, HEADS)
        def _(turn):
            i = first + turn

            @pl.when(i != me)
            def _():
                await_bytes(r.got.at[0], r.got_sem.at[i])

        @pl.loop(0, HEADS, unroll=4)
        def _(turn):
            i = first + turn
            rows = aligned(i * BLOCK, BLOCK)
            pos = i * BLOCK + lax.broadcasted_iota(jnp.int32, (BLOCK, 2 * HEAD), 0)
            kv = jnp.where(pos < seq_len, r.got[i, :BLOCK].astype(F32), 0.0)
            tile, at = i // (TILE // BLOCK), lax.rem(i, TILE // BLOCK) * BLOCK
            r.kv0[tile, aligned(at, BLOCK)] = jnp.where(low_block, 0.5 * kv, 0.0).astype(BF16)
            r.kv0[tile, aligned(TILE + at, BLOCK)] = jnp.where(low_block, 0.0, kv).astype(BF16)
            r.kt[:, rows] = jnp.transpose(kv)[:HEAD].astype(BF16)
            q = r.got[i, BLOCK:].astype(F32)
            r.qa[rows] = jnp.concatenate(
                [jnp.where(low, q, 0.0), jnp.where(low, turned(q), 0.0)], axis=0
            ).astype(BF16)

    copy_to(r.negs.at[grp], r.negs.at[grp], r.send_sem.at[3], r.one_sem.at[2], mate)
    copy_to(r.all_ids.at[grp], r.all_ids.at[grp], r.send_sem.at[4], r.one_sem.at[3], mate)
    copy_to(r.negs.at[grp], r.negs.at[grp], r.send_sem.at[5], r.one_sem.at[4], other_z)
    copy_to(r.all_ids.at[grp], r.all_ids.at[grp], r.send_sem.at[6], r.one_sem.at[5], other_z)
    await_bytes(r.send.at[others], r.send_sem.at[0])
    inv_len = 1.0 / jnp.full((1, 2 * HEAD), seq_len, jnp.int32).astype(F32)

    f_tiles = length // FQ
    f_per = FQ // BLOCK

    @pl.loop(0, f_tiles)
    def _(step):
        c = tile_at(me // f_per, f_tiles - 1 - step, f_tiles)
        q = r.qa[aligned(c * FQ, FQ)]

        def piece(start, size, masked):
            rows = pl.ds(start, size)
            size = size * TILE
            half = dot_nt(q, r.kv0[rows, :TILE].reshape(size, 2 * HEAD))
            if masked:
                ahead = lax.broadcasted_iota(jnp.int32, (FQ, size), 1) - lax.broadcasted_iota(
                    jnp.int32, (FQ, size), 0
                )
                half = jnp.where(ahead <= size - FQ, half, 0.0)
            probs = (half + half * jnp.tanh(half)).astype(BF16)
            return dot_nn(probs, r.kv0[rows, TILE:].reshape(size, 2 * HEAD))

        odd = lax.rem(c, 2)

        @pl.when(odd == 0)
        def _():
            r.acc[...] = piece(c, 1, True)

        @pl.when(odd == 1)
        def _():
            r.acc[...] = piece(c - 1, 2, True)

        def more(start, size):
            r.acc[...] += piece(start, size, False)

        cover(0, c - odd, more)
        for u in range(f_per):
            out = r.acc[u * BLOCK:(u + 1) * BLOCK] * inv_len
            top, bottom = out[:HEAD], out[HEAD:]
            r.att_send[c * f_per + u] = jnp.where(low, turned(top), bottom).astype(BF16)

        @pl.loop(0, f_per)
        def _(turn):
            i = c * f_per + lax.rem(me + turn, f_per)

            @pl.when(i != me)
            def _():
                copy_to(
                    r.att_send.at[i], r.att_got.at[me], r.send_sem.at[7], r.att_sem.at[me], {"seq": i}
                )

            @pl.when(i == me)
            def _():
                r.att_got[me] = r.att_send[me]

    far = (1 - z_hi) * 2 + core
    await_bytes(r.negs.at[0], r.one_sem.at[4])
    await_bytes(r.all_ids.at[0], r.one_sem.at[5])
    copy_to(r.negs.at[far], r.negs.at[far], r.send_sem.at[8], r.one_sem.at[6], mate)
    copy_to(r.all_ids.at[far], r.all_ids.at[far], r.send_sem.at[9], r.one_sem.at[7], mate)

    total = r.lens[0] - 1
    for at in range(1, r.lens.shape[0]):
        total = total + (r.lens[at] - 1)
    both = 2
    half_rows = both * BLOCK
    weight = 1.0 / jnp.full((half_rows, 1), total, jnp.int32).astype(F32)
    r.grad_out[...] = jnp.zeros_like(r.grad_out)
    r.loss[...] = jnp.zeros_like(r.loss)
    await_bytes(r.first, r.one_sem.at[0])
    await_bytes(r.ids, r.one_sem.at[1])
    await_bytes(r.negs.at[0], r.one_sem.at[2])
    await_bytes(r.all_ids.at[0], r.one_sem.at[3])
    await_bytes(r.negs.at[0], r.one_sem.at[6])
    await_bytes(r.all_ids.at[0], r.one_sem.at[7])
    n_halves = n_here // both

    @pl.loop(0, n_halves)
    def _(step):
        middle(r, n_seq, me, grp, both * lax.rem(me // (both * HEADS) + step, n_halves), weight)

    axes = dict(x=x_at, y=y_at, z=z_at)
    plane_at = dict(x=y_at * 4 + z_at, y=x_at * 4 + z_at, z=x_at * 4 + y_at)

    def chip(axis, along, across, of_core=core):
        hi, lo = across // 4, lax.rem(across, 4)
        x, y, z = dict(x=(along, hi, lo), y=(hi, along, lo), z=(hi, lo, along))[axis]
        return {"grp": z // 2 * 2 + of_core, "seq": (x * 4 + y) * 2 + lax.rem(z, 2)}

    def reduction(name, axis, at):
        part, got, sums, got2, red, full = (
            getattr(r, name + tail) for tail in ("_part", "_got", "_sum", "_got2", "_red", "_full")
        )
        send = [r.red_send.at[at * 4 + k] for k in range(4)]
        recv = [r.red_recv.at[at * 4 + k] for k in range(4)]
        along, across = axes[axis], plane_at[axis]
        mine = core * 4 + along
        seven, fifteen = pl.ds(0, 7), pl.ds(0, 15)

        def along_axis(source, target, sems):
            @pl.loop(1, 8)
            def _(step):
                to = lax.rem(mine + step, 8)
                copy_to(source(to), target, *sems, chip(axis, lax.rem(to, 4), across, to // 4))

        def over_plane(source, target, sems):
            @pl.loop(1, 16)
            def _(step):
                to = lax.rem(across + step, 16)
                copy_to(source(to), target, *sems, chip(axis, along, to))

        def scatter(*grads):
            for which, grad in enumerate(grads):
                for half in range(4):
                    block = grad[:, half * BLOCK:(half + 1) * BLOCK].astype(BF16)
                    low, first = half % 2 * 8, half // 2 * 4
                    part[first:first + 4, low:low + 8, which * 16:which * 16 + 16] = block.reshape(
                        4, 8, 16, BLOCK
                    )
            along_axis(lambda to: part.at[to], got.at[mine], (send[0], recv[0]))

        def plane():
            got[mine] = part[mine]
            await_bytes(got.at[seven], recv[0])
            sums[...] = jnp.sum(got[...].astype(F32), axis=0).astype(BF16)
            over_plane(lambda to: sums.at[to], got2.at[across], (send[1], recv[1]))

        def gather():
            got2[across] = sums[across]
            await_bytes(got2.at[fifteen], recv[1])
            red[...] = jnp.sum(got2[...].astype(F32), axis=0).astype(BF16)
            full[mine, across] = red[...]
            over_plane(lambda to: red, full.at[mine, across], (send[2], recv[2]))

        def spread():
            await_bytes(got2.at[fifteen], recv[2])
            along_axis(lambda to: full.at[mine], full.at[mine], (send[3], recv[3]))

        def finish():
            await_bytes(got.at[seven], recv[3])
            await_bytes(got.at[seven], send[0])
            await_bytes(got2.at[fifteen], send[1])
            await_bytes(got2.at[fifteen], send[2])
            await_bytes(got.at[seven], send[3])

        return types.SimpleNamespace(scatter=scatter, plane=plane, gather=gather, spread=spread, finish=finish)

    early = reduction("e", "x", 0)
    early.scatter(dot_nn(r.xnt[...], r.d_pre[:, :WIDTH]), r.grad_out[...])
    copy_to(r.loss, r.loss_core, r.loss_sem.at[0], r.loss_sem.at[1], mate)

    def loss_along(axis, value, at):
        r.loss_all[at, axes[axis]] = value
        r.loss_sum[at] = value
        for step in range(1, 4):
            copy_to(
                r.loss_sum.at[at], r.loss_all.at[at, axes[axis]],
                r.loss_sem.at[2 + 2 * at], r.loss_sem.at[3 + 2 * at],
                chip(axis, lax.rem(axes[axis] + step, 4), plane_at[axis]),
            )

    def loss_over(at):
        await_bytes(r.loss_all.at[at, pl.ds(0, 3)], r.loss_sem.at[3 + 2 * at])
        return jnp.sum(r.loss_all[at], axis=0)

    @pl.loop(0, n_seq)
    def _(step):
        i = lax.rem(me + step, n_seq)

        @pl.when(i != me)
        def _():
            await_bytes(r.datt_got.at[0], r.datt_sem.at[i])

    @pl.loop(0, n_seq, unroll=4)
    def _(i):
        d_att = r.datt_got[i].astype(F32)
        rows = aligned(i * BLOCK, BLOCK)
        qa = r.qa[rows].astype(F32)
        r.qa[rows] = jnp.where(
            low_block, qa, jnp.concatenate([turned(d_att), d_att], axis=0)
        ).astype(BF16)

    r.dq[...] = jnp.zeros_like(r.dq)
    b_tiles = length // BM
    b_per = BM // BLOCK
    kv_scale = jnp.where(low_lanes((1, 2 * HEAD)), 0.5 * inv_len, inv_len)

    def send_d_q(low, high):
        @pl.loop(low, high)
        def _(c):
            for u in range(b_per):
                d_q = r.dq[:, aligned((c * b_per + u) * BLOCK, BLOCK)] * (0.5 * inv_len)
                r.grad_send[c * b_per + u, BLOCK:] = d_q.astype(BF16)

            @pl.loop(0, b_per)
            def _(turn):
                i = c * b_per + lax.rem(me + turn, b_per)

                @pl.when(i != me)
                def _():
                    copy_to(
                        r.grad_send.at[i, pl.ds(BLOCK, HEAD)], r.grad_got.at[me, pl.ds(BLOCK, HEAD)],
                        r.send_sem.at[11], r.grad_sem.at[1], {"seq": i},
                    )

                @pl.when(i == me)
                def _():
                    r.grad_got[me, BLOCK:] = r.grad_send[me, BLOCK:]

    @pl.loop(0, b_tiles)
    def _(step):
        c = tile_at(me // b_per, step, b_tiles)
        m_rows = aligned(c * BM, BM)
        low_tile = low_lanes((BM, 2 * HEAD))

        def piece(start, size, masked):
            size = size * TILE
            t_rows = pl.ds(pl.multiple_of(start * TILE, TILE), size)
            qa = r.qa[t_rows]
            products = dot_nt(r.kv0[c], qa)
            half, d_probs = products[:TILE], products[TILE:]
            if masked:
                ahead = lax.broadcasted_iota(jnp.int32, (BM, size), 0) - lax.broadcasted_iota(
                    jnp.int32, (BM, size), 1
                )
                half = jnp.where(ahead <= 0, half, 0.0)
                d_probs = jnp.where(ahead <= 0, d_probs, 0.0)
            up = 1.0 + jnp.tanh(half)
            probs = half * up
            d_scores = (d_probs * up * (1.0 + (half + half) - probs)).astype(BF16)
            r.dq[:, t_rows] += dot_nn(r.kt[:, m_rows], d_scores)
            return jnp.where(low_tile, dot_nn(d_scores, qa), dot_nn(probs.astype(BF16), qa))

        odd = lax.rem(b_tiles - 1 - c, 2)

        @pl.when(odd == 0)
        def _():
            r.dkv[...] = piece(c, 1, True)

        @pl.when(odd == 1)
        def _():
            r.dkv[...] = piece(c, 2, True)

        def more(start, size):
            r.dkv[...] += piece(start, size, False)

        cover(c + 1 + odd, b_tiles - 1 - c - odd, more)
        for u in range(b_per):
            r.grad_send[c * b_per + u, :BLOCK] = (
                r.dkv[u * BLOCK:(u + 1) * BLOCK] * kv_scale
            ).astype(BF16)

        @pl.loop(0, b_per)
        def _(turn):
            i = c * b_per + lax.rem(me + turn, b_per)

            @pl.when(i != me)
            def _():
                copy_to(
                    r.grad_send.at[i, pl.ds(0, BLOCK)], r.grad_got.at[me, pl.ds(0, BLOCK)],
                    r.send_sem.at[10], r.grad_sem.at[0], {"seq": i},
                )

            @pl.when(i == me)
            def _():
                r.grad_got[me, :BLOCK] = r.grad_send[me, :BLOCK]

        for at, stage in enumerate(("plane", "gather", "spread", "")):
            @pl.when(step == 2 * at + 1)
            def _(at=at, stage=stage):
                if stage:
                    getattr(early, stage)()
                if at == 0:
                    await_bytes(r.loss_core, r.loss_sem.at[1])
                    loss_along("x", r.loss[...] + r.loss_core[...], 0)
                if at == 1:
                    loss_along("y", loss_over(0), 1)
                if at == 2:
                    loss_along("z", loss_over(1), 2)
                if at == 3:
                    count = jnp.full((8, BLOCK), total, jnp.int32).astype(F32)
                    r.loss_out[0] = (loss_over(2) / count)[0, 0]

        end = tile_at(me // b_per, b_tiles - 1, b_tiles)

        @pl.when(step == b_tiles - 2)
        def _():
            send_d_q(0, end)

        @pl.when(step == b_tiles - 1)
        def _():
            send_d_q(end, b_tiles)

    late = [reduction("v", "x", 1), reduction("k", "y", 2), reduction("q", "z", 3)]
    await_bytes(r.grad_got.at[others, pl.ds(0, BLOCK)], r.grad_sem.at[0])

    @pl.loop(0, n_here)
    def _(b):
        rows = aligned(b * BLOCK, BLOCK)
        for pair in range(PAIRS):
            j = b * HEADS + 2 * pair
            d_k, d_v = swapped(r.grad_got[j, :BLOCK].astype(F32), r.grad_got[j + 1, :BLOCK].astype(F32))
            for part, grad in ((1, d_v), (3, d_k)):
                at = part * WIDTH + pair * 2 * HEAD
                slope = r.slope[b, :, at:at + 2 * HEAD].astype(F32)
                r.d_pre[rows, at:at + 2 * HEAD] = (grad * slope).astype(BF16)

    late[0].scatter(dot_nn(r.xnt[...], r.d_pre[:, WIDTH:2 * WIDTH]))
    late[1].scatter(dot_nn(r.xnt[...], r.d_pre[:, 3 * WIDTH:]))
    await_bytes(r.grad_got.at[others, pl.ds(BLOCK, HEAD)], r.grad_sem.at[1])

    @pl.loop(0, n_here)
    def _(b):
        rows = aligned(b * BLOCK, BLOCK)
        for pair in range(PAIRS):
            j = b * HEADS + 2 * pair
            at = 2 * WIDTH + pair * 2 * HEAD
            grad = jnp.transpose(
                jnp.concatenate([r.grad_got[j + e, BLOCK:].astype(F32) for e in range(2)], axis=0)
            )
            slope = r.slope[b, :, at:at + 2 * HEAD].astype(F32)
            r.d_pre[rows, at:at + 2 * HEAD] = (grad * slope).astype(BF16)

    late[2].scatter(dot_nn(r.xnt[...], r.d_pre[:, 2 * WIDTH:3 * WIDTH]))
    for stage in ("plane", "gather", "spread"):
        for one in late:
            getattr(one, stage)()

    for one in [early] + late:
        one.finish()

    await_bytes(r.first, r.send_sem.at[1])
    await_bytes(r.ids, r.send_sem.at[2])
    for at in (3, 5, 8):
        await_bytes(r.negs.at[0], r.send_sem.at[at])
        await_bytes(r.all_ids.at[0], r.send_sem.at[at + 1])
    await_bytes(r.att_send.at[others], r.send_sem.at[7])
    await_bytes(r.datt_send.at[others], r.send_sem.at[12])
    await_bytes(r.grad_send.at[others, pl.ds(0, BLOCK)], r.send_sem.at[10])
    await_bytes(r.grad_send.at[others, pl.ds(BLOCK, HEAD)], r.send_sem.at[11])
    await_bytes(r.loss, r.loss_sem.at[0])
    for at in range(3):
        await_bytes(r.loss_all.at[at, pl.ds(0, 3)], r.loss_sem.at[2 + 2 * at])


def activated(r, b, xn, part):
    half = 0.5 * dot_nn(xn, r.w_joined[:, part * WIDTH:(part + 1) * WIDTH])
    th = jnp.tanh(half)
    slope = (0.5 + 0.5 * th) * (1.0 + half * (1.0 - th))
    r.slope[b, :, part * WIDTH:(part + 1) * WIDTH] = slope.astype(BF16)
    return half + half * th


def middle(r, n_seq, me, grp, first_b, weight):
    both = 2
    rows = both * BLOCK
    n_here = r.x.shape[0]
    n_grp, n_neg = r.negs.shape[:2]

    def joined(make):
        return jnp.concatenate([make(e) for e in range(both)], axis=0)

    @pl.loop(0, both * HEADS)
    def _(turn):
        j = first_b * HEADS + turn

        @pl.when(j != me)
        def _():
            await_bytes(r.att_got.at[0], r.att_sem.at[j])

    for e in range(both):
        for pair in range(PAIRS):
            j = (first_b + e) * HEADS + 2 * pair
            top, bottom = swapped(r.att_got[j].astype(F32), r.att_got[j + 1].astype(F32))
            r.att[e * BLOCK:e * BLOCK + HEAD, pair_cols(pair)] = top
            r.att[e * BLOCK + HEAD:(e + 1) * BLOCK, pair_cols(pair)] = bottom

    att = r.att[...]
    centered = att - jnp.mean(att, axis=-1, keepdims=True)
    inv_att = lax.rsqrt(jnp.mean(centered * centered, axis=-1, keepdims=True) + eps_norm)
    normed = centered * inv_att
    u = joined(lambda e: r.u[first_b + e]).astype(F32)
    gated = (normed * u).astype(BF16)
    x = joined(lambda e: r.x[first_b + e]).astype(F32)
    out_rows = x + dot_nn(gated, r.w_out[...])
    inv_y = lax.rsqrt(jnp.sum(out_rows * out_rows, axis=-1, keepdims=True) + eps_norm)
    unit_y = out_rows * inv_y
    unit_b = unit_y.astype(BF16)
    more = jnp.where(me == n_seq - 1, 0, 1)
    last_row = lax.broadcasted_iota(jnp.int32, (BLOCK, WIDTH), 0) == BLOCK - 1
    last_lane = lax.broadcasted_iota(jnp.int32, (1, BLOCK), 1) == BLOCK - 1

    def next_rows(e):
        shifted = pltpu.roll(r.x[first_b + e].astype(F32), BLOCK - 1, axis=0)
        return jnp.where(last_row, r.first[first_b + e].astype(F32)[:1] * more.astype(F32), shifted)

    x_next = joined(next_rows)
    pos_unit = (
        x_next * lax.rsqrt(jnp.sum(x_next * x_next, axis=-1, keepdims=True) + eps_norm)
    ).astype(BF16).astype(F32)
    pos_logit = logit_scale * jnp.sum(unit_b.astype(F32) * pos_unit, axis=-1, keepdims=True)

    def row_ids(e):
        shifted = pltpu.roll(r.ids[pl.ds(first_b + e, 1)], BLOCK - 1, axis=1)
        coming = pltpu.roll(r.next_ids[pl.ds(first_b + e, 1)], BLOCK - 1, axis=1) * more
        return jnp.transpose(jnp.broadcast_to(jnp.where(last_lane, coming, shifted), (BLOCK, BLOCK)))

    ids = joined(row_ids)
    lane_sum = jnp.zeros((rows, BLOCK), F32)
    for g in range(n_grp):
        neg_logit = logit_scale * dot_nt(unit_b, r.negs[g])
        for sub in range(n_neg // BLOCK):
            at = (g * n_neg) + sub * BLOCK
            hit = r.all_ids[g, n_here + sub:n_here + sub + 1] == ids
            exps = jnp.where(hit, 0.0, jnp.exp(neg_logit[:, sub * BLOCK:(sub + 1) * BLOCK]))
            r.exps[:, at:at + BLOCK] = exps
            lane_sum = lane_sum + exps
    pos_exp = jnp.exp(pos_logit)
    denom = pos_exp + jnp.sum(lane_sum, axis=-1, keepdims=True)

    def row_valid(e):
        pos = me * BLOCK + lax.broadcasted_iota(jnp.int32, (BLOCK, 1), 0)
        return jnp.where(pos + 1 < r.lens[grp * n_here + first_b + e], 1.0, 0.0)

    valid = joined(row_valid)
    row_loss = jnp.where(valid > 0.0, jnp.log(denom) - pos_logit, 0.0)
    r.loss[...] += jnp.broadcast_to(jnp.sum(row_loss, axis=0, keepdims=True), r.loss.shape)
    row_weight = valid * weight
    d_pos = row_weight * (pos_exp / denom - 1.0)
    scale = row_weight / denom
    neg_back = jnp.zeros((rows, WIDTH), F32)
    for g in range(n_grp):
        d_neg = (scale * r.exps[:, g * n_neg:(g + 1) * n_neg]).astype(BF16)
        neg_back = neg_back + dot_nn(d_neg, r.negs[g])
    d_unit = logit_scale * (d_pos * pos_unit + neg_back)
    d_out = (
        (d_unit - unit_y * jnp.sum(unit_y * d_unit, axis=-1, keepdims=True)) * inv_y
    ).astype(BF16)
    d_gate = dot_nt(d_out, r.w_out[...])
    d_norm = d_gate * u
    d_att = inv_att * (
        d_norm
        - jnp.mean(d_norm, axis=-1, keepdims=True)
        - normed * jnp.mean(d_norm * normed, axis=-1, keepdims=True)
    )
    for e in range(both):
        rows_e = d_att[e * BLOCK:(e + 1) * BLOCK]
        for pair in range(PAIRS):
            cols = pair_cols(pair)
            packed = swapped(rows_e[:HEAD, cols], rows_e[HEAD:, cols])
            for odd in range(2):
                r.datt_send[(first_b + e) * HEADS + 2 * pair + odd] = packed[odd].astype(BF16)

    @pl.loop(0, both * HEADS)
    def _(turn):
        j = first_b * HEADS + lax.rem(me + turn, both * HEADS)

        @pl.when(j != me)
        def _():
            copy_to(
                r.datt_send.at[j], r.datt_got.at[me], r.send_sem.at[12], r.datt_sem.at[me], {"seq": j}
            )

        @pl.when(j == me)
        def _():
            r.datt_got[me] = r.datt_send[me]

    r.grad_out[...] += dot_tn(gated, d_out)
    d_u = d_gate * normed
    for e in range(both):
        slope = r.slope[first_b + e, :, :WIDTH].astype(F32)
        r.d_pre[aligned((first_b + e) * BLOCK, BLOCK), :WIDTH] = (
            d_u[e * BLOCK:(e + 1) * BLOCK] * slope
        ).astype(BF16)


def widen(*refs):
    *blocks, joined, out = refs
    for half in range(4):
        low = half % 2 * 8

        def taken(block, first):
            return block[half // 2, 0, low:low + 8, first:first + 16].reshape(BLOCK, BLOCK).astype(F32)

        for at, block in enumerate(blocks):
            joined[:, at * WIDTH + half * BLOCK:at * WIDTH + (half + 1) * BLOCK] = taken(block, 0)
        out[:, half * BLOCK:(half + 1) * BLOCK] = taken(blocks[0], 16)


def local(inputs, history, lengths, w_joined, w_out, neg_emb, neg_ids):
    n_here, block, width = inputs.shape
    n_seq = lax.axis_size("seq")
    length = n_seq * block
    lanes = 2 * HEAD
    rows = n_here * block
    n_neg = neg_emb.shape[0]
    dma = pltpu.SemaphoreType.DMA
    buffers = dict(
        xn=((n_here, block, width), BF16), xnt=((width, rows), BF16), u=((n_here, block, width), BF16),
        slope=((n_here, block, 4 * width), BF16), d_pre=((rows, 4 * width), BF16),
        send=((n_seq, BLOCK + HEAD, lanes), BF16), got=((n_seq, BLOCK + HEAD, lanes), BF16),
        att_send=((n_seq, HEAD, lanes), BF16), att_got=((n_seq, HEAD, lanes), BF16),
        datt_send=((n_seq, HEAD, lanes), BF16), datt_got=((n_seq, HEAD, lanes), BF16),
        grad_send=((n_seq, BLOCK + HEAD, lanes), BF16), grad_got=((n_seq, BLOCK + HEAD, lanes), BF16),
        first=((n_here, 16, width), BF16), ids=((2 * n_here, block), jnp.int32),
        next_ids=((2 * n_here, block), jnp.int32), negs=((4, n_neg, width), BF16),
        all_ids=((4, 2 * n_here, block), jnp.int32),
        kv0=((length // TILE, 2 * TILE, lanes), BF16), qa=((length, lanes), BF16),
        kt=((HEAD, length), BF16), acc=((FQ, lanes), F32), dq=((HEAD, length), F32), dkv=((BM, lanes), F32),
        att=((2 * block, width), F32), exps=((2 * block, 4 * n_neg), F32), grad_out=((width, width), F32),
        loss=((8, block), F32), loss_core=((8, block), F32), loss_sum=((3, 8, block), F32),
        loss_all=((3, 4, 8, block), F32), x=((n_here, block, width), BF16),
        w_joined=((width, 4 * width), BF16), w_out=((width, width), BF16), neg_emb=((n_neg, width), BF16),
        history=((n_here, block), jnp.int32), neg_ids=((n_here, block), jnp.int32),
    )
    wide = (8, 16, 16, block)
    shapes = dict(e=(8, 16, 32, block), v=wide, k=wide, q=wide)
    for name, shape in shapes.items():
        buffers[name + "_part"] = buffers[name + "_got"] = (shape, BF16)
        buffers[name + "_sum"] = buffers[name + "_got2"] = (shape[1:], BF16)
        buffers[name + "_red"] = (shape[2:], BF16)
    sems = dict(
        send_sem=13, one_sem=8, got_sem=n_seq, att_sem=n_seq, datt_sem=n_seq, grad_sem=2, loss_sem=8,
        red_send=16, red_recv=16, load_sem=6,
    )
    takes = ("lens", "x_in", "history_in", "neg_ids_in", "w_joined_in", "w_out_in", "neg_emb_in")
    gives = {name + "_full": (shapes[name], BF16) for name in "evqk"}
    gives["loss_out"] = ((1,), F32)
    names = takes + tuple(gives) + tuple(buffers) + tuple(sems)
    *grads, loss = pl.pallas_call(
        functools.partial(kernel, n_seq, names),
        out_shape=[jax.ShapeDtypeStruct(*kind) for kind in gives.values()],
        in_specs=[SMEM] + [pl.BlockSpec(memory_space=pl.ANY)] * (len(takes) - 1),
        out_specs=[VMEM] * 4 + [SMEM],
        scratch_shapes=[pltpu.VMEM(*kind) for kind in buffers.values()]
        + [dma((count,)) for count in sems.values()],
        compiler_params=pltpu.CompilerParams(
            collective_id=0, has_side_effects=True, vmem_limit_bytes=60 * 1024 * 1024
        ),
    )(lengths, inputs, history, neg_ids.reshape(-1, block), w_joined, w_out, neg_emb)
    grads = [grad.reshape((2, 4) + grad.shape[1:]) for grad in grads]
    taken = [
        pl.BlockSpec((2, 1) + grad.shape[2:], lambda at: (0, at, 0, 0, 0)) for grad in grads
    ]
    joined, out = pl.pallas_call(
        widen,
        grid=(4,),
        out_shape=[
            jax.ShapeDtypeStruct((width, 4 * width), F32), jax.ShapeDtypeStruct((width, width), F32)
        ],
        in_specs=taken,
        out_specs=[
            pl.BlockSpec((width // 4, 4 * width), lambda at: (at, 0)),
            pl.BlockSpec((width // 4, width), lambda at: (at, 0)),
        ],
        compiler_params=pltpu.CompilerParams(vmem_limit_bytes=60 * 1024 * 1024),
    )(*grads)
    return (joined, out, loss.reshape(()))


def solution(mesh):
    placed = (
        P("grp", "seq", None),
        P("grp", "seq"),
        P(),
        P(),
        P(),
        P(("grp", "seq"), None),
        P(("grp", "seq")),
    )
    return jax.shard_map(
        local, mesh=mesh, in_specs=placed, out_specs=(P(), P(), P()), check_vma=False
    )
```

```python
import functools
import types

import jax
import jax.numpy as jnp
from jax import lax
from jax.experimental import pallas as pl
from jax.experimental.pallas import tpu as pltpu
from jax.sharding import PartitionSpec as P

HEADS = 8
HEAD = 64
WIDTH = 512
PAIRS = 4
BLOCK = 128
TILE = 512
FQ = TILE
BM = TILE
eps_norm = 1e-06
logit_scale = 64.0

MESH = pl.DeviceIdType.MESH
F32 = jnp.float32
BF16 = jnp.bfloat16
VMEM = pl.BlockSpec(memory_space=pltpu.VMEM)
SMEM = pl.BlockSpec(memory_space=pltpu.SMEM)


def dot_nn(a, b):
    return lax.dot_general(a, b, (((1,), (0,)), ((), ())), preferred_element_type=F32)


def dot_nt(a, b):
    return lax.dot_general(a, b, (((1,), (1,)), ((), ())), preferred_element_type=F32)


def dot_tn(a, b):
    return lax.dot_general(a, b, (((0,), (0,)), ((), ())), preferred_element_type=F32)


def low_lanes(shape):
    return lax.broadcasted_iota(jnp.int32, shape, 1) < HEAD


def turned(a):
    return pltpu.roll(a, HEAD, axis=1)


def swapped(a, b):
    low = low_lanes(a.shape)
    return jnp.where(low, a, turned(b)), jnp.where(low, turned(a), b)


def copy_to(src, dst, send_sem, recv_sem, where):
    pltpu.make_async_remote_copy(
        src_ref=src, dst_ref=dst, send_sem=send_sem, recv_sem=recv_sem,
        device_id=where, device_id_type=MESH,
    ).start()


def await_bytes(ref, sem):
    pltpu.make_async_copy(ref, ref, sem).wait()


def aligned(at, size):
    return pl.ds(pl.multiple_of(at, size), size)


def pair_cols(pair):
    return slice(pair * 2 * HEAD, (pair + 1) * 2 * HEAD)


def shifts(n_seq):
    side = int((n_seq // 2) ** 0.5)
    steps = [(x, y, z) for x in range(side) for y in range(side) for z in range(2)]
    return sorted(steps[1:], key=lambda at: -(min(at[0], side - at[0]) + min(at[1], side - at[1]) + at[2]))


def peer(me, shift):
    x, y, z = me // HEADS, lax.rem(me // 2, 4), lax.rem(me, 2)
    return (lax.rem(x + shift[0], 4) * 4 + lax.rem(y + shift[1], 4)) * 2 + lax.rem(z + shift[2], 2)


def cover(first, count, body):
    done = 0
    for tiles in (4, 2):
        n = count // tiles if tiles == 4 else lax.rem(count // tiles, 2)

        @pl.loop(0, n)
        def _(at, done=done, tiles=tiles):
            body(first + done + at * tiles, tiles)

        done = done + n * tiles


def tile_at(first, step, tiles):
    low = lax.rem(first + step // 2, tiles // 2)
    odd = lax.rem(step, 2)
    return low + odd * (tiles - 1 - 2 * low)


def kernel(n_seq, names, *refs):
    r = types.SimpleNamespace(**dict(zip(names, refs, strict=True)))
    me = lax.axis_index("seq")
    grp = lax.axis_index("grp")
    core, z_hi = lax.rem(grp, 2), grp // 2
    loads = [
        pltpu.make_async_copy(getattr(r, name + "_in"), getattr(r, name), r.load_sem.at[at])
        for at, name in enumerate(("x", "w_joined", "history", "neg_ids", "neg_emb", "w_out"))
    ]
    for load in loads:
        load.start()
    n_here = r.x.shape[0]
    planes = n_seq // HEADS
    length = n_seq * BLOCK
    mate = {"grp": grp + 1 - 2 * core}
    other_z = {"grp": (1 - z_hi) * 2 + core}
    others = pl.ds(0, n_seq - 1)
    x_at, y_at, z_at = me // HEADS, lax.rem(me // 2, 4), z_hi * 2 + lax.rem(me, 2)

    barrier = pltpu.get_barrier_semaphore()

    def greet(where):
        pl.semaphore_signal(barrier, inc=1, device_id=where, device_id_type=MESH)

    greet(mate)

    @pl.loop(1, n_seq)
    def _(step):
        greet({"seq": lax.rem(me + step, n_seq)})

    for step in range(4):
        for z in range(2):
            greet(dict(other_z, seq=(x_at * 4 + lax.rem(y_at + step, 4)) * 2 + z))
            if step:
                greet(dict(other_z, seq=(lax.rem(x_at + step, 4) * 4 + y_at) * 2 + z))

    def lane(axis, along):
        x, y, z = (along if axis == name else at for name, at in (("x", x_at), ("y", y_at), ("z", z_at)))
        return {"grp": z // 2 * 2 + 1 - core, "seq": (x * 4 + y) * 2 + lax.rem(z, 2)}

    for axis, at in (("x", x_at), ("y", y_at), ("z", z_at)):
        for step in range(1, 4):
            greet(lane(axis, lax.rem(at + step, 4)))
    n_peers = n_seq + 14 + 9

    loads[0].wait()
    loads[1].wait()

    @pl.loop(0, n_here)
    def _(b):
        x = r.x[b].astype(F32)
        centered = x - jnp.mean(x, axis=-1, keepdims=True)
        var = jnp.mean(centered * centered, axis=-1, keepdims=True)
        xn = (centered * lax.rsqrt(var + eps_norm)).astype(BF16)
        r.xn[b] = xn
        v, q, k = (activated(r, b, xn, part) for part in (1, 2, 3))
        for pair in range(PAIRS):
            cols = pair_cols(pair)
            kv = swapped(k[:, cols], v[:, cols])
            qs = swapped(q[:HEAD, cols], q[HEAD:, cols])
            for odd in range(2):
                j = b * HEADS + 2 * pair + odd
                r.send[j, :BLOCK] = kv[odd].astype(BF16)
                r.send[j, BLOCK:] = qs[odd].astype(BF16)

    pl.semaphore_wait(barrier, n_peers)
    for shift in shifts(n_seq):
        j = peer(me, shift)
        copy_to(r.send.at[j], r.got.at[me], r.send_sem.at[0], r.got_sem.at[me], {"seq": j})
    r.got[me] = r.send[me]

    before = {"seq": lax.rem(me + n_seq - 1, n_seq)}
    loads[2].wait()
    loads[3].wait()
    r.ids[:n_here] = r.history[...]
    r.ids[n_here:] = r.neg_ids[...]
    copy_to(r.x.at[:, pl.ds(0, 16)], r.first, r.send_sem.at[1], r.one_sem.at[0], before)
    copy_to(r.ids, r.next_ids, r.send_sem.at[2], r.one_sem.at[1], before)

    loads[4].wait()
    loads[5].wait()

    @pl.loop(0, n_here)
    def _(b):
        xn = r.xn[b]
        r.u[b] = activated(r, b, xn, 0).astype(BF16)
        r.xnt[:, aligned(b * BLOCK, BLOCK)] = jnp.transpose(xn.astype(F32)).astype(BF16)
        rows = aligned(b * BLOCK, BLOCK)
        emb = r.neg_emb[rows].astype(F32)
        r.negs[grp, rows] = (
            emb * lax.rsqrt(jnp.sum(emb * emb, axis=-1, keepdims=True) + eps_norm)
        ).astype(BF16)

    r.all_ids[grp] = r.ids[...]

    seq_len = r.lens[grp * n_here + me // HEADS]
    low = low_lanes((HEAD, 2 * HEAD))
    low_block = low_lanes((BLOCK, 2 * HEAD))

    @pl.loop(0, planes)
    def _(step):
        first = lax.rem(me // HEADS + planes // 2 + step, planes) * HEADS

        @pl.loop(0, HEADS)
        def _(turn):
            i = first + turn

            @pl.when(i != me)
            def _():
                await_bytes(r.got.at[0], r.got_sem.at[i])

        @pl.loop(0, HEADS, unroll=4)
        def _(turn):
            i = first + turn
            rows = aligned(i * BLOCK, BLOCK)
            pos = i * BLOCK + lax.broadcasted_iota(jnp.int32, (BLOCK, 2 * HEAD), 0)
            kv = jnp.where(pos < seq_len, r.got[i, :BLOCK].astype(F32), 0.0)
            tile, at = i // (TILE // BLOCK), lax.rem(i, TILE // BLOCK) * BLOCK
            r.kv0[tile, aligned(at, BLOCK)] = jnp.where(low_block, 0.5 * kv, 0.0).astype(BF16)
            r.kv0[tile, aligned(TILE + at, BLOCK)] = jnp.where(low_block, 0.0, kv).astype(BF16)
            r.kt[:, rows] = jnp.transpose(kv)[:HEAD].astype(BF16)
            q = r.got[i, BLOCK:].astype(F32)
            r.qa[rows] = jnp.concatenate(
                [jnp.where(low, q, 0.0), jnp.where(low, turned(q), 0.0)], axis=0
            ).astype(BF16)

    copy_to(r.negs.at[grp], r.negs.at[grp], r.send_sem.at[3], r.one_sem.at[2], mate)
    copy_to(r.all_ids.at[grp], r.all_ids.at[grp], r.send_sem.at[4], r.one_sem.at[3], mate)
    copy_to(r.negs.at[grp], r.negs.at[grp], r.send_sem.at[5], r.one_sem.at[4], other_z)
    copy_to(r.all_ids.at[grp], r.all_ids.at[grp], r.send_sem.at[6], r.one_sem.at[5], other_z)
    await_bytes(r.send.at[others], r.send_sem.at[0])
    inv_len = 1.0 / jnp.full((1, 2 * HEAD), seq_len, jnp.int32).astype(F32)

    f_tiles = length // FQ
    f_per = FQ // BLOCK

    @pl.loop(0, f_tiles)
    def _(step):
        c = tile_at(me // f_per, f_tiles - 1 - step, f_tiles)
        q = r.qa[aligned(c * FQ, FQ)]

        def piece(start, size, masked):
            rows = pl.ds(start, size)
            size = size * TILE
            half = dot_nt(q, r.kv0[rows, :TILE].reshape(size, 2 * HEAD))
            if masked:
                ahead = lax.broadcasted_iota(jnp.int32, (FQ, size), 1) - lax.broadcasted_iota(
                    jnp.int32, (FQ, size), 0
                )
                half = jnp.where(ahead <= size - FQ, half, 0.0)
            probs = (half + half * jnp.tanh(half)).astype(BF16)
            return dot_nn(probs, r.kv0[rows, TILE:].reshape(size, 2 * HEAD))

        odd = lax.rem(c, 2)

        @pl.when(odd == 0)
        def _():
            r.acc[...] = piece(c, 1, True)

        @pl.when(odd == 1)
        def _():
            r.acc[...] = piece(c - 1, 2, True)

        def more(start, size):
            r.acc[...] += piece(start, size, False)

        cover(0, c - odd, more)
        for u in range(f_per):
            out = r.acc[u * BLOCK:(u + 1) * BLOCK] * inv_len
            top, bottom = out[:HEAD], out[HEAD:]
            r.att_send[c * f_per + u] = jnp.where(low, turned(top), bottom).astype(BF16)

        @pl.loop(0, f_per)
        def _(turn):
            i = c * f_per + lax.rem(me + turn, f_per)

            @pl.when(i != me)
            def _():
                copy_to(
                    r.att_send.at[i], r.att_got.at[me], r.send_sem.at[7], r.att_sem.at[me], {"seq": i}
                )

            @pl.when(i == me)
            def _():
                r.att_got[me] = r.att_send[me]

    far = (1 - z_hi) * 2 + core
    await_bytes(r.negs.at[0], r.one_sem.at[4])
    await_bytes(r.all_ids.at[0], r.one_sem.at[5])
    copy_to(r.negs.at[far], r.negs.at[far], r.send_sem.at[8], r.one_sem.at[6], mate)
    copy_to(r.all_ids.at[far], r.all_ids.at[far], r.send_sem.at[9], r.one_sem.at[7], mate)

    total = r.lens[0] - 1
    for at in range(1, r.lens.shape[0]):
        total = total + (r.lens[at] - 1)
    both = 2
    half_rows = both * BLOCK
    weight = 1.0 / jnp.full((half_rows, 1), total, jnp.int32).astype(F32)
    r.grad_out[...] = jnp.zeros_like(r.grad_out)
    r.loss[...] = jnp.zeros_like(r.loss)
    await_bytes(r.first, r.one_sem.at[0])
    await_bytes(r.ids, r.one_sem.at[1])
    await_bytes(r.negs.at[0], r.one_sem.at[2])
    await_bytes(r.all_ids.at[0], r.one_sem.at[3])
    await_bytes(r.negs.at[0], r.one_sem.at[6])
    await_bytes(r.all_ids.at[0], r.one_sem.at[7])
    n_halves = n_here // both

    @pl.loop(0, n_halves)
    def _(step):
        middle(r, n_seq, me, grp, both * lax.rem(me // (both * HEADS) + step, n_halves), weight)

    axes = dict(x=x_at, y=y_at, z=z_at)
    plane_at = dict(x=y_at * 4 + z_at, y=x_at * 4 + z_at, z=x_at * 4 + y_at)

    def chip(axis, along, across, of_core=core):
        hi, lo = across // 4, lax.rem(across, 4)
        x, y, z = dict(x=(along, hi, lo), y=(hi, along, lo), z=(hi, lo, along))[axis]
        return {"grp": z // 2 * 2 + of_core, "seq": (x * 4 + y) * 2 + lax.rem(z, 2)}

    def reduction(name, axis, at):
        part, got, sums, got2, red, full = (
            getattr(r, name + tail) for tail in ("_part", "_got", "_sum", "_got2", "_red", "_full")
        )
        send = [r.red_send.at[at * 4 + k] for k in range(4)]
        recv = [r.red_recv.at[at * 4 + k] for k in range(4)]
        along, across = axes[axis], plane_at[axis]
        mine = core * 4 + along
        seven, fifteen = pl.ds(0, 7), pl.ds(0, 15)

        def along_axis(source, target, sems):
            @pl.loop(1, 8)
            def _(step):
                to = lax.rem(mine + step, 8)
                copy_to(source(to), target, *sems, chip(axis, lax.rem(to, 4), across, to // 4))

        def over_plane(source, target, sems):
            @pl.loop(1, 16)
            def _(step):
                to = lax.rem(across + step, 16)
                copy_to(source(to), target, *sems, chip(axis, along, to))

        def scatter(grad):
            for half in range(4):
                block = grad[:, half * BLOCK:(half + 1) * BLOCK].astype(BF16)
                low, first = half % 2 * 8, half // 2 * 4
                part[first:first + 4, low:low + 8] = block.reshape(4, 8, 16, BLOCK)
            along_axis(lambda to: part.at[to], got.at[mine], (send[0], recv[0]))

        def plane():
            got[mine] = part[mine]
            await_bytes(got.at[seven], recv[0])
            sums[...] = jnp.sum(got[...].astype(F32), axis=0).astype(BF16)
            over_plane(lambda to: sums.at[to], got2.at[across], (send[1], recv[1]))

        def gather():
            got2[across] = sums[across]
            await_bytes(got2.at[fifteen], recv[1])
            red[...] = jnp.sum(got2[...].astype(F32), axis=0).astype(BF16)
            full[mine, across] = red[...]
            over_plane(lambda to: red, full.at[mine, across], (send[2], recv[2]))

        def spread():
            await_bytes(got2.at[fifteen], recv[2])
            along_axis(lambda to: full.at[mine], full.at[mine], (send[3], recv[3]))

        def finish():
            await_bytes(got.at[seven], recv[3])
            await_bytes(got.at[seven], send[0])
            await_bytes(got2.at[fifteen], send[1])
            await_bytes(got2.at[fifteen], send[2])
            await_bytes(got.at[seven], send[3])

        return types.SimpleNamespace(scatter=scatter, plane=plane, gather=gather, spread=spread, finish=finish)

    early = [reduction("u", "x", 0), reduction("o", "y", 1)]
    copy_to(r.loss, r.loss_core, r.loss_sem.at[0], r.loss_sem.at[1], mate)

    def loss_along(axis, value, at):
        r.loss_all[at, axes[axis]] = value
        r.loss_sum[at] = value
        for step in range(1, 4):
            copy_to(
                r.loss_sum.at[at], r.loss_all.at[at, axes[axis]],
                r.loss_sem.at[2 + 2 * at], r.loss_sem.at[3 + 2 * at],
                chip(axis, lax.rem(axes[axis] + step, 4), plane_at[axis]),
            )

    def loss_over(at):
        await_bytes(r.loss_all.at[at, pl.ds(0, 3)], r.loss_sem.at[3 + 2 * at])
        return jnp.sum(r.loss_all[at], axis=0)

    @pl.loop(0, n_seq)
    def _(step):
        i = lax.rem(me + step, n_seq)

        @pl.when(i != me)
        def _():
            await_bytes(r.datt_got.at[0], r.datt_sem.at[i])

    @pl.loop(0, n_seq, unroll=4)
    def _(i):
        d_att = r.datt_got[i].astype(F32)
        rows = aligned(i * BLOCK, BLOCK)
        qa = r.qa[rows].astype(F32)
        r.qa[rows] = jnp.where(
            low_block, qa, jnp.concatenate([turned(d_att), d_att], axis=0)
        ).astype(BF16)

    early[0].scatter(dot_nn(r.xnt[...], r.d_pre[:, :WIDTH]))
    early[1].scatter(r.grad_out[...])

    r.dq[...] = jnp.zeros_like(r.dq)
    b_tiles = length // BM
    b_per = BM // BLOCK
    kv_scale = jnp.where(low_lanes((1, 2 * HEAD)), 0.5 * inv_len, inv_len)

    def send_d_q(low, high):
        @pl.loop(low, high)
        def _(c):
            for u in range(b_per):
                d_q = r.dq[:, aligned((c * b_per + u) * BLOCK, BLOCK)] * (0.5 * inv_len)
                r.grad_send[c * b_per + u, BLOCK:] = d_q.astype(BF16)

            @pl.loop(0, b_per)
            def _(turn):
                i = c * b_per + lax.rem(me + turn, b_per)

                @pl.when(i != me)
                def _():
                    copy_to(
                        r.grad_send.at[i, pl.ds(BLOCK, HEAD)], r.grad_got.at[me, pl.ds(BLOCK, HEAD)],
                        r.send_sem.at[11], r.grad_sem.at[1], {"seq": i},
                    )

                @pl.when(i == me)
                def _():
                    r.grad_got[me, BLOCK:] = r.grad_send[me, BLOCK:]

    @pl.loop(0, b_tiles)
    def _(step):
        c = tile_at(me // b_per, step, b_tiles)
        m_rows = aligned(c * BM, BM)
        low_tile = low_lanes((BM, 2 * HEAD))

        def piece(start, size, masked):
            size = size * TILE
            t_rows = pl.ds(pl.multiple_of(start * TILE, TILE), size)
            qa = r.qa[t_rows]
            products = dot_nt(r.kv0[c], qa)
            half, d_probs = products[:TILE], products[TILE:]
            if masked:
                ahead = lax.broadcasted_iota(jnp.int32, (BM, size), 0) - lax.broadcasted_iota(
                    jnp.int32, (BM, size), 1
                )
                half = jnp.where(ahead <= 0, half, 0.0)
                d_probs = jnp.where(ahead <= 0, d_probs, 0.0)
            up = 1.0 + jnp.tanh(half)
            probs = half * up
            d_scores = (d_probs * up * (1.0 + (half + half) - probs)).astype(BF16)
            r.dq[:, t_rows] += dot_nn(r.kt[:, m_rows], d_scores)
            return jnp.where(low_tile, dot_nn(d_scores, qa), dot_nn(probs.astype(BF16), qa))

        odd = lax.rem(b_tiles - 1 - c, 2)

        @pl.when(odd == 0)
        def _():
            r.dkv[...] = piece(c, 1, True)

        @pl.when(odd == 1)
        def _():
            r.dkv[...] = piece(c, 2, True)

        def more(start, size):
            r.dkv[...] += piece(start, size, False)

        cover(c + 1 + odd, b_tiles - 1 - c - odd, more)
        for u in range(b_per):
            r.grad_send[c * b_per + u, :BLOCK] = (
                r.dkv[u * BLOCK:(u + 1) * BLOCK] * kv_scale
            ).astype(BF16)

        @pl.loop(0, b_per)
        def _(turn):
            i = c * b_per + lax.rem(me + turn, b_per)

            @pl.when(i != me)
            def _():
                copy_to(
                    r.grad_send.at[i, pl.ds(0, BLOCK)], r.grad_got.at[me, pl.ds(0, BLOCK)],
                    r.send_sem.at[10], r.grad_sem.at[0], {"seq": i},
                )

            @pl.when(i == me)
            def _():
                r.grad_got[me, :BLOCK] = r.grad_send[me, :BLOCK]

        for at, stage in enumerate(("plane", "gather", "spread", "")):
            @pl.when(step == 2 * at + 1)
            def _(at=at, stage=stage):
                if stage:
                    for one in early:
                        getattr(one, stage)()
                if at == 0:
                    await_bytes(r.loss_core, r.loss_sem.at[1])
                    loss_along("x", r.loss[...] + r.loss_core[...], 0)
                if at == 1:
                    loss_along("y", loss_over(0), 1)
                if at == 2:
                    loss_along("z", loss_over(1), 2)
                if at == 3:
                    count = jnp.full((8, BLOCK), total, jnp.int32).astype(F32)
                    r.loss_out[0] = (loss_over(2) / count)[0, 0]

        end = tile_at(me // b_per, b_tiles - 1, b_tiles)

        @pl.when(step == b_tiles - 2)
        def _():
            send_d_q(0, end)

        @pl.when(step == b_tiles - 1)
        def _():
            send_d_q(end, b_tiles)

    late = [reduction("v", "x", 2), reduction("k", "y", 3), reduction("q", "z", 4)]
    await_bytes(r.grad_got.at[others, pl.ds(0, BLOCK)], r.grad_sem.at[0])

    @pl.loop(0, n_here)
    def _(b):
        rows = aligned(b * BLOCK, BLOCK)
        for pair in range(PAIRS):
            j = b * HEADS + 2 * pair
            d_k, d_v = swapped(r.grad_got[j, :BLOCK].astype(F32), r.grad_got[j + 1, :BLOCK].astype(F32))
            for part, grad in ((1, d_v), (3, d_k)):
                at = part * WIDTH + pair * 2 * HEAD
                slope = r.slope[b, :, at:at + 2 * HEAD].astype(F32)
                r.d_pre[rows, at:at + 2 * HEAD] = (grad * slope).astype(BF16)

    late[0].scatter(dot_nn(r.xnt[...], r.d_pre[:, WIDTH:2 * WIDTH]))
    late[1].scatter(dot_nn(r.xnt[...], r.d_pre[:, 3 * WIDTH:]))
    await_bytes(r.grad_got.at[others, pl.ds(BLOCK, HEAD)], r.grad_sem.at[1])

    @pl.loop(0, n_here)
    def _(b):
        rows = aligned(b * BLOCK, BLOCK)
        for pair in range(PAIRS):
            j = b * HEADS + 2 * pair
            at = 2 * WIDTH + pair * 2 * HEAD
            grad = jnp.transpose(
                jnp.concatenate([r.grad_got[j + e, BLOCK:].astype(F32) for e in range(2)], axis=0)
            )
            slope = r.slope[b, :, at:at + 2 * HEAD].astype(F32)
            r.d_pre[rows, at:at + 2 * HEAD] = (grad * slope).astype(BF16)

    late[2].scatter(dot_nn(r.xnt[...], r.d_pre[:, 2 * WIDTH:3 * WIDTH]))
    for stage in ("plane", "gather", "spread"):
        for one in late:
            getattr(one, stage)()

    for one in early + late:
        one.finish()

    await_bytes(r.first, r.send_sem.at[1])
    await_bytes(r.ids, r.send_sem.at[2])
    for at in (3, 5, 8):
        await_bytes(r.negs.at[0], r.send_sem.at[at])
        await_bytes(r.all_ids.at[0], r.send_sem.at[at + 1])
    await_bytes(r.att_send.at[others], r.send_sem.at[7])
    await_bytes(r.datt_send.at[others], r.send_sem.at[12])
    await_bytes(r.grad_send.at[others, pl.ds(0, BLOCK)], r.send_sem.at[10])
    await_bytes(r.grad_send.at[others, pl.ds(BLOCK, HEAD)], r.send_sem.at[11])
    await_bytes(r.loss, r.loss_sem.at[0])
    for at in range(3):
        await_bytes(r.loss_all.at[at, pl.ds(0, 3)], r.loss_sem.at[2 + 2 * at])


def activated(r, b, xn, part):
    half = 0.5 * dot_nn(xn, r.w_joined[:, part * WIDTH:(part + 1) * WIDTH])
    th = jnp.tanh(half)
    slope = (0.5 + 0.5 * th) * (1.0 + half * (1.0 - th))
    r.slope[b, :, part * WIDTH:(part + 1) * WIDTH] = slope.astype(BF16)
    return half + half * th


def middle(r, n_seq, me, grp, first_b, weight):
    both = 2
    rows = both * BLOCK
    n_here = r.x.shape[0]
    n_grp, n_neg = r.negs.shape[:2]

    def joined(make):
        return jnp.concatenate([make(e) for e in range(both)], axis=0)

    @pl.loop(0, both * HEADS)
    def _(turn):
        j = first_b * HEADS + turn

        @pl.when(j != me)
        def _():
            await_bytes(r.att_got.at[0], r.att_sem.at[j])

    for e in range(both):
        for pair in range(PAIRS):
            j = (first_b + e) * HEADS + 2 * pair
            top, bottom = swapped(r.att_got[j].astype(F32), r.att_got[j + 1].astype(F32))
            r.att[e * BLOCK:e * BLOCK + HEAD, pair_cols(pair)] = top
            r.att[e * BLOCK + HEAD:(e + 1) * BLOCK, pair_cols(pair)] = bottom

    att = r.att[...]
    centered = att - jnp.mean(att, axis=-1, keepdims=True)
    inv_att = lax.rsqrt(jnp.mean(centered * centered, axis=-1, keepdims=True) + eps_norm)
    normed = centered * inv_att
    u = joined(lambda e: r.u[first_b + e]).astype(F32)
    gated = (normed * u).astype(BF16)
    x = joined(lambda e: r.x[first_b + e]).astype(F32)
    out_rows = x + dot_nn(gated, r.w_out[...])
    inv_y = lax.rsqrt(jnp.sum(out_rows * out_rows, axis=-1, keepdims=True) + eps_norm)
    unit_y = out_rows * inv_y
    unit_b = unit_y.astype(BF16)
    more = jnp.where(me == n_seq - 1, 0, 1)
    last_row = lax.broadcasted_iota(jnp.int32, (BLOCK, WIDTH), 0) == BLOCK - 1
    last_lane = lax.broadcasted_iota(jnp.int32, (1, BLOCK), 1) == BLOCK - 1

    def next_rows(e):
        shifted = pltpu.roll(r.x[first_b + e].astype(F32), BLOCK - 1, axis=0)
        return jnp.where(last_row, r.first[first_b + e].astype(F32)[:1] * more.astype(F32), shifted)

    x_next = joined(next_rows)
    pos_unit = (
        x_next * lax.rsqrt(jnp.sum(x_next * x_next, axis=-1, keepdims=True) + eps_norm)
    ).astype(BF16).astype(F32)
    pos_logit = logit_scale * jnp.sum(unit_b.astype(F32) * pos_unit, axis=-1, keepdims=True)

    def row_ids(e):
        shifted = pltpu.roll(r.ids[pl.ds(first_b + e, 1)], BLOCK - 1, axis=1)
        coming = pltpu.roll(r.next_ids[pl.ds(first_b + e, 1)], BLOCK - 1, axis=1) * more
        return jnp.transpose(jnp.broadcast_to(jnp.where(last_lane, coming, shifted), (BLOCK, BLOCK)))

    ids = joined(row_ids)
    lane_sum = jnp.zeros((rows, BLOCK), F32)
    for g in range(n_grp):
        neg_logit = logit_scale * dot_nt(unit_b, r.negs[g])
        for sub in range(n_neg // BLOCK):
            at = (g * n_neg) + sub * BLOCK
            hit = r.all_ids[g, n_here + sub:n_here + sub + 1] == ids
            exps = jnp.where(hit, 0.0, jnp.exp(neg_logit[:, sub * BLOCK:(sub + 1) * BLOCK]))
            r.exps[:, at:at + BLOCK] = exps
            lane_sum = lane_sum + exps
    pos_exp = jnp.exp(pos_logit)
    denom = pos_exp + jnp.sum(lane_sum, axis=-1, keepdims=True)

    def row_valid(e):
        pos = me * BLOCK + lax.broadcasted_iota(jnp.int32, (BLOCK, 1), 0)
        return jnp.where(pos + 1 < r.lens[grp * n_here + first_b + e], 1.0, 0.0)

    valid = joined(row_valid)
    row_loss = jnp.where(valid > 0.0, jnp.log(denom) - pos_logit, 0.0)
    r.loss[...] += jnp.broadcast_to(jnp.sum(row_loss, axis=0, keepdims=True), r.loss.shape)
    row_weight = valid * weight
    d_pos = row_weight * (pos_exp / denom - 1.0)
    scale = row_weight / denom
    neg_back = jnp.zeros((rows, WIDTH), F32)
    for g in range(n_grp):
        d_neg = (scale * r.exps[:, g * n_neg:(g + 1) * n_neg]).astype(BF16)
        neg_back = neg_back + dot_nn(d_neg, r.negs[g])
    d_unit = logit_scale * (d_pos * pos_unit + neg_back)
    d_out = (
        (d_unit - unit_y * jnp.sum(unit_y * d_unit, axis=-1, keepdims=True)) * inv_y
    ).astype(BF16)
    d_gate = dot_nt(d_out, r.w_out[...])
    d_norm = d_gate * u
    d_att = inv_att * (
        d_norm
        - jnp.mean(d_norm, axis=-1, keepdims=True)
        - normed * jnp.mean(d_norm * normed, axis=-1, keepdims=True)
    )
    for e in range(both):
        rows_e = d_att[e * BLOCK:(e + 1) * BLOCK]
        for pair in range(PAIRS):
            cols = pair_cols(pair)
            packed = swapped(rows_e[:HEAD, cols], rows_e[HEAD:, cols])
            for odd in range(2):
                r.datt_send[(first_b + e) * HEADS + 2 * pair + odd] = packed[odd].astype(BF16)

    @pl.loop(0, both * HEADS)
    def _(turn):
        j = first_b * HEADS + lax.rem(me + turn, both * HEADS)

        @pl.when(j != me)
        def _():
            copy_to(
                r.datt_send.at[j], r.datt_got.at[me], r.send_sem.at[12], r.datt_sem.at[me], {"seq": j}
            )

        @pl.when(j == me)
        def _():
            r.datt_got[me] = r.datt_send[me]

    r.grad_out[...] += dot_tn(gated, d_out)
    d_u = d_gate * normed
    for e in range(both):
        slope = r.slope[first_b + e, :, :WIDTH].astype(F32)
        r.d_pre[aligned((first_b + e) * BLOCK, BLOCK), :WIDTH] = (
            d_u[e * BLOCK:(e + 1) * BLOCK] * slope
        ).astype(BF16)


def widen(*refs):
    *blocks, joined, out = refs
    for at, block in enumerate(blocks):
        for half in range(4):
            low = half % 2 * 8
            values = block[half // 2, 0, low:low + 8].reshape(BLOCK, BLOCK).astype(F32)
            if at < 4:
                joined[:, at * WIDTH + half * BLOCK:at * WIDTH + (half + 1) * BLOCK] = values
            else:
                out[:, half * BLOCK:(half + 1) * BLOCK] = values


def local(inputs, history, lengths, w_joined, w_out, neg_emb, neg_ids):
    n_here, block, width = inputs.shape
    n_seq = lax.axis_size("seq")
    length = n_seq * block
    lanes = 2 * HEAD
    rows = n_here * block
    n_neg = neg_emb.shape[0]
    dma = pltpu.SemaphoreType.DMA
    buffers = dict(
        xn=((n_here, block, width), BF16), xnt=((width, rows), BF16), u=((n_here, block, width), BF16),
        slope=((n_here, block, 4 * width), BF16), d_pre=((rows, 4 * width), BF16),
        send=((n_seq, BLOCK + HEAD, lanes), BF16), got=((n_seq, BLOCK + HEAD, lanes), BF16),
        att_send=((n_seq, HEAD, lanes), BF16), att_got=((n_seq, HEAD, lanes), BF16),
        datt_send=((n_seq, HEAD, lanes), BF16), datt_got=((n_seq, HEAD, lanes), BF16),
        grad_send=((n_seq, BLOCK + HEAD, lanes), BF16), grad_got=((n_seq, BLOCK + HEAD, lanes), BF16),
        first=((n_here, 16, width), BF16), ids=((2 * n_here, block), jnp.int32),
        next_ids=((2 * n_here, block), jnp.int32), negs=((4, n_neg, width), BF16),
        all_ids=((4, 2 * n_here, block), jnp.int32),
        kv0=((length // TILE, 2 * TILE, lanes), BF16), qa=((length, lanes), BF16),
        kt=((HEAD, length), BF16), acc=((FQ, lanes), F32), dq=((HEAD, length), F32), dkv=((BM, lanes), F32),
        att=((2 * block, width), F32), exps=((2 * block, 4 * n_neg), F32), grad_out=((width, width), F32),
        loss=((8, block), F32), loss_core=((8, block), F32), loss_sum=((3, 8, block), F32),
        loss_all=((3, 4, 8, block), F32), x=((n_here, block, width), BF16),
        w_joined=((width, 4 * width), BF16), w_out=((width, width), BF16), neg_emb=((n_neg, width), BF16),
        history=((n_here, block), jnp.int32), neg_ids=((n_here, block), jnp.int32),
    )
    wide = (8, 16, 16, block)
    for name in "uovkq":
        buffers[name + "_part"] = buffers[name + "_got"] = (wide, BF16)
        buffers[name + "_sum"] = buffers[name + "_got2"] = (wide[1:], BF16)
        buffers[name + "_red"] = (wide[2:], BF16)
    sems = dict(
        send_sem=13, one_sem=8, got_sem=n_seq, att_sem=n_seq, datt_sem=n_seq, grad_sem=2, loss_sem=8,
        red_send=20, red_recv=20, load_sem=6,
    )
    takes = ("lens", "x_in", "history_in", "neg_ids_in", "w_joined_in", "w_out_in", "neg_emb_in")
    gives = {name + "_full": (wide, BF16) for name in "uvqko"}
    gives["loss_out"] = ((1,), F32)
    names = takes + tuple(gives) + tuple(buffers) + tuple(sems)
    *grads, loss = pl.pallas_call(
        functools.partial(kernel, n_seq, names),
        out_shape=[jax.ShapeDtypeStruct(*kind) for kind in gives.values()],
        in_specs=[SMEM] + [pl.BlockSpec(memory_space=pl.ANY)] * (len(takes) - 1),
        out_specs=[VMEM] * 5 + [SMEM],
        scratch_shapes=[pltpu.VMEM(*kind) for kind in buffers.values()]
        + [dma((count,)) for count in sems.values()],
        compiler_params=pltpu.CompilerParams(
            collective_id=0, has_side_effects=True, vmem_limit_bytes=60 * 1024 * 1024
        ),
    )(lengths, inputs, history, neg_ids.reshape(-1, block), w_joined, w_out, neg_emb)
    taken = pl.BlockSpec((2, 1) + wide[1:], lambda at: (0, at, 0, 0, 0))
    joined, out = pl.pallas_call(
        widen,
        grid=(4,),
        out_shape=[
            jax.ShapeDtypeStruct((width, 4 * width), F32), jax.ShapeDtypeStruct((width, width), F32)
        ],
        in_specs=[taken] * 5,
        out_specs=[
            pl.BlockSpec((width // 4, 4 * width), lambda at: (at, 0)),
            pl.BlockSpec((width // 4, width), lambda at: (at, 0)),
        ],
        compiler_params=pltpu.CompilerParams(vmem_limit_bytes=60 * 1024 * 1024),
    )(*(grad.reshape((2, 4) + wide[1:]) for grad in grads))
    return (joined, out, loss.reshape(()))


def solution(mesh):
    placed = (
        P("grp", "seq", None),
        P("grp", "seq"),
        P(),
        P(),
        P(),
        P(("grp", "seq"), None),
        P(("grp", "seq")),
    )
    return jax.shard_map(
        local, mesh=mesh, in_specs=placed, out_specs=(P(), P(), P()), check_vma=False
    )
```

```python
import functools
import types

import jax
import jax.numpy as jnp
from jax import lax
from jax.experimental import pallas as pl
from jax.experimental.pallas import tpu as pltpu
from jax.sharding import PartitionSpec as P

HEADS = 8
HEAD = 64
WIDTH = 512
PAIRS = 4
BLOCK = 128
TILE = 512
FQ = TILE
BM = TILE
eps_norm = 1e-06
logit_scale = 64.0

MESH = pl.DeviceIdType.MESH
F32 = jnp.float32
BF16 = jnp.bfloat16
VMEM = pl.BlockSpec(memory_space=pltpu.VMEM)
SMEM = pl.BlockSpec(memory_space=pltpu.SMEM)


def dot_nn(a, b):
    return lax.dot_general(a, b, (((1,), (0,)), ((), ())), preferred_element_type=F32)


def dot_nt(a, b):
    return lax.dot_general(a, b, (((1,), (1,)), ((), ())), preferred_element_type=F32)


def dot_tn(a, b):
    return lax.dot_general(a, b, (((0,), (0,)), ((), ())), preferred_element_type=F32)


def low_lanes(shape):
    return lax.broadcasted_iota(jnp.int32, shape, 1) < HEAD


def turned(a):
    return pltpu.roll(a, HEAD, axis=1)


def swapped(a, b):
    low = low_lanes(a.shape)
    return jnp.where(low, a, turned(b)), jnp.where(low, turned(a), b)


def copy_to(src, dst, send_sem, recv_sem, where):
    pltpu.make_async_remote_copy(
        src_ref=src, dst_ref=dst, send_sem=send_sem, recv_sem=recv_sem,
        device_id=where, device_id_type=MESH,
    ).start()


def await_bytes(ref, sem):
    pltpu.make_async_copy(ref, ref, sem).wait()


def aligned(at, size):
    return pl.ds(pl.multiple_of(at, size), size)


def pair_cols(pair):
    return slice(pair * 2 * HEAD, (pair + 1) * 2 * HEAD)


def shifts(n_seq):
    side = int((n_seq // 2) ** 0.5)
    steps = [(x, y, z) for x in range(side) for y in range(side) for z in range(2)]
    return sorted(steps[1:], key=lambda at: -(min(at[0], side - at[0]) + min(at[1], side - at[1]) + at[2]))


def peer(me, shift):
    x, y, z = me // HEADS, lax.rem(me // 2, 4), lax.rem(me, 2)
    return (lax.rem(x + shift[0], 4) * 4 + lax.rem(y + shift[1], 4)) * 2 + lax.rem(z + shift[2], 2)


def cover(first, count, body):
    done = 0
    for tiles in (4, 2):
        n = count // tiles if tiles == 4 else lax.rem(count // tiles, 2)

        @pl.loop(0, n)
        def _(at, done=done, tiles=tiles):
            body(first + done + at * tiles, tiles)

        done = done + n * tiles


def tile_at(first, step, tiles):
    low = lax.rem(first + step // 2, tiles // 2)
    odd = lax.rem(step, 2)
    return low + odd * (tiles - 1 - 2 * low)


def kernel(n_seq, names, *refs):
    r = types.SimpleNamespace(**dict(zip(names, refs, strict=True)))
    me = lax.axis_index("seq")
    grp = lax.axis_index("grp")
    core, z_hi = lax.rem(grp, 2), grp // 2
    loads = [
        pltpu.make_async_copy(getattr(r, name + "_in"), getattr(r, name), r.load_sem.at[at])
        for at, name in enumerate(("x", "w_joined", "history", "neg_ids", "neg_emb", "w_out"))
    ]
    for load in loads:
        load.start()
    n_here = r.x.shape[0]
    planes = n_seq // HEADS
    length = n_seq * BLOCK
    mate = {"grp": grp + 1 - 2 * core}
    other_z = {"grp": (1 - z_hi) * 2 + core}
    others = pl.ds(0, n_seq - 1)
    x_at, y_at, z_at = me // HEADS, lax.rem(me // 2, 4), z_hi * 2 + lax.rem(me, 2)

    barrier = pltpu.get_barrier_semaphore()

    def greet(where):
        pl.semaphore_signal(barrier, inc=1, device_id=where, device_id_type=MESH)

    greet(mate)

    @pl.loop(1, n_seq)
    def _(step):
        greet({"seq": lax.rem(me + step, n_seq)})

    for step in range(4):
        for z in range(2):
            greet(dict(other_z, seq=(x_at * 4 + lax.rem(y_at + step, 4)) * 2 + z))
            if step:
                greet(dict(other_z, seq=(lax.rem(x_at + step, 4) * 4 + y_at) * 2 + z))

    def lane(axis, along):
        x, y, z = (along if axis == name else at for name, at in (("x", x_at), ("y", y_at), ("z", z_at)))
        return {"grp": z // 2 * 2 + 1 - core, "seq": (x * 4 + y) * 2 + lax.rem(z, 2)}

    for axis, at in (("x", x_at), ("y", y_at), ("z", z_at)):
        for step in range(1, 4):
            greet(lane(axis, lax.rem(at + step, 4)))
    n_peers = n_seq + 14 + 9

    loads[0].wait()
    loads[1].wait()

    @pl.loop(0, n_here)
    def _(b):
        x = r.x[b].astype(F32)
        centered = x - jnp.mean(x, axis=-1, keepdims=True)
        var = jnp.mean(centered * centered, axis=-1, keepdims=True)
        xn = (centered * lax.rsqrt(var + eps_norm)).astype(BF16)
        r.xn[b] = xn
        v, q, k = (activated(r, b, xn, part) for part in (1, 2, 3))
        for pair in range(PAIRS):
            cols = pair_cols(pair)
            kv = swapped(k[:, cols], v[:, cols])
            qs = swapped(q[:HEAD, cols], q[HEAD:, cols])
            for odd in range(2):
                j = b * HEADS + 2 * pair + odd
                r.send[j, :BLOCK] = kv[odd].astype(BF16)
                r.send[j, BLOCK:] = qs[odd].astype(BF16)

    pl.semaphore_wait(barrier, n_peers)
    for shift in shifts(n_seq):
        j = peer(me, shift)
        copy_to(r.send.at[j], r.got.at[me], r.send_sem.at[0], r.got_sem.at[me], {"seq": j})
    r.got[me] = r.send[me]

    before = {"seq": lax.rem(me + n_seq - 1, n_seq)}
    loads[2].wait()
    loads[3].wait()
    r.ids[:n_here] = r.history[...]
    r.ids[n_here:] = r.neg_ids[...]
    copy_to(r.x.at[:, pl.ds(0, 16)], r.first, r.send_sem.at[1], r.one_sem.at[0], before)
    copy_to(r.ids, r.next_ids, r.send_sem.at[2], r.one_sem.at[1], before)

    loads[4].wait()
    loads[5].wait()

    @pl.loop(0, n_here)
    def _(b):
        xn = r.xn[b]
        r.u[b] = activated(r, b, xn, 0).astype(BF16)
        r.xnt[:, aligned(b * BLOCK, BLOCK)] = jnp.transpose(xn.astype(F32)).astype(BF16)
        rows = aligned(b * BLOCK, BLOCK)
        emb = r.neg_emb[rows].astype(F32)
        r.negs[grp, rows] = (
            emb * lax.rsqrt(jnp.sum(emb * emb, axis=-1, keepdims=True) + eps_norm)
        ).astype(BF16)

    r.all_ids[grp] = r.ids[...]

    seq_len = r.lens[grp * n_here + me // HEADS]
    low = low_lanes((HEAD, 2 * HEAD))
    low_block = low_lanes((BLOCK, 2 * HEAD))

    @pl.loop(0, planes)
    def _(step):
        first = lax.rem(me // HEADS + planes // 2 + step, planes) * HEADS

        @pl.loop(0, HEADS)
        def _(turn):
            i = first + turn

            @pl.when(i != me)
            def _():
                await_bytes(r.got.at[0], r.got_sem.at[i])

        @pl.loop(0, HEADS, unroll=4)
        def _(turn):
            i = first + turn
            rows = aligned(i * BLOCK, BLOCK)
            pos = i * BLOCK + lax.broadcasted_iota(jnp.int32, (BLOCK, 2 * HEAD), 0)
            kv = jnp.where(pos < seq_len, r.got[i, :BLOCK].astype(F32), 0.0)
            tile, at = i // (TILE // BLOCK), lax.rem(i, TILE // BLOCK) * BLOCK
            r.kv0[tile, aligned(at, BLOCK)] = jnp.where(low_block, 0.5 * kv, 0.0).astype(BF16)
            r.kv0[tile, aligned(TILE + at, BLOCK)] = jnp.where(low_block, 0.0, kv).astype(BF16)
            r.kt[:, rows] = jnp.transpose(kv)[:HEAD].astype(BF16)
            q = r.got[i, BLOCK:].astype(F32)
            r.qa[rows] = jnp.concatenate(
                [jnp.where(low, q, 0.0), jnp.where(low, turned(q), 0.0)], axis=0
            ).astype(BF16)

    copy_to(r.negs.at[grp], r.negs.at[grp], r.send_sem.at[3], r.one_sem.at[2], mate)
    copy_to(r.all_ids.at[grp], r.all_ids.at[grp], r.send_sem.at[4], r.one_sem.at[3], mate)
    copy_to(r.negs.at[grp], r.negs.at[grp], r.send_sem.at[5], r.one_sem.at[4], other_z)
    copy_to(r.all_ids.at[grp], r.all_ids.at[grp], r.send_sem.at[6], r.one_sem.at[5], other_z)
    await_bytes(r.send.at[others], r.send_sem.at[0])
    inv_len = 1.0 / jnp.full((1, 2 * HEAD), seq_len, jnp.int32).astype(F32)

    f_tiles = length // FQ
    f_per = FQ // BLOCK

    @pl.loop(0, f_tiles)
    def _(step):
        c = tile_at(me // f_per, f_tiles - 1 - step, f_tiles)
        q = r.qa[aligned(c * FQ, FQ)]

        def piece(start, size, masked):
            rows = pl.ds(start, size)
            size = size * TILE
            half = dot_nt(q, r.kv0[rows, :TILE].reshape(size, 2 * HEAD))
            if masked:
                ahead = lax.broadcasted_iota(jnp.int32, (FQ, size), 1) - lax.broadcasted_iota(
                    jnp.int32, (FQ, size), 0
                )
                half = jnp.where(ahead <= size - FQ, half, 0.0)
            probs = (half + half * jnp.tanh(half)).astype(BF16)
            return dot_nn(probs, r.kv0[rows, TILE:].reshape(size, 2 * HEAD))

        odd = lax.rem(c, 2)

        @pl.when(odd == 0)
        def _():
            r.acc[...] = piece(c, 1, True)

        @pl.when(odd == 1)
        def _():
            r.acc[...] = piece(c - 1, 2, True)

        def more(start, size):
            r.acc[...] += piece(start, size, False)

        cover(0, c - odd, more)
        for u in range(f_per):
            out = r.acc[u * BLOCK:(u + 1) * BLOCK] * inv_len
            top, bottom = out[:HEAD], out[HEAD:]
            r.att_send[c * f_per + u] = jnp.where(low, turned(top), bottom).astype(BF16)

        @pl.loop(0, f_per)
        def _(turn):
            i = c * f_per + lax.rem(me + turn, f_per)

            @pl.when(i != me)
            def _():
                copy_to(
                    r.att_send.at[i], r.att_got.at[me], r.send_sem.at[7], r.att_sem.at[me], {"seq": i}
                )

            @pl.when(i == me)
            def _():
                r.att_got[me] = r.att_send[me]

    far = (1 - z_hi) * 2 + core
    await_bytes(r.negs.at[0], r.one_sem.at[4])
    await_bytes(r.all_ids.at[0], r.one_sem.at[5])
    copy_to(r.negs.at[far], r.negs.at[far], r.send_sem.at[8], r.one_sem.at[6], mate)
    copy_to(r.all_ids.at[far], r.all_ids.at[far], r.send_sem.at[9], r.one_sem.at[7], mate)

    total = r.lens[0] - 1
    for at in range(1, r.lens.shape[0]):
        total = total + (r.lens[at] - 1)
    both = 2
    half_rows = both * BLOCK
    weight = 1.0 / jnp.full((half_rows, 1), total, jnp.int32).astype(F32)
    r.grad_out[...] = jnp.zeros_like(r.grad_out)
    r.loss[...] = jnp.zeros_like(r.loss)
    await_bytes(r.first, r.one_sem.at[0])
    await_bytes(r.ids, r.one_sem.at[1])
    await_bytes(r.negs.at[0], r.one_sem.at[2])
    await_bytes(r.all_ids.at[0], r.one_sem.at[3])
    await_bytes(r.negs.at[0], r.one_sem.at[6])
    await_bytes(r.all_ids.at[0], r.one_sem.at[7])
    n_halves = n_here // both

    @pl.loop(0, n_halves)
    def _(step):
        middle(r, n_seq, me, grp, both * lax.rem(me // (both * HEADS) + step, n_halves), weight)

    axes = dict(x=x_at, y=y_at, z=z_at)
    plane_at = dict(x=y_at * 4 + z_at, y=x_at * 4 + z_at, z=x_at * 4 + y_at)

    def chip(axis, along, across, of_core=core):
        hi, lo = across // 4, lax.rem(across, 4)
        x, y, z = dict(x=(along, hi, lo), y=(hi, along, lo), z=(hi, lo, along))[axis]
        return {"grp": z // 2 * 2 + of_core, "seq": (x * 4 + y) * 2 + lax.rem(z, 2)}

    def reduction(name, axis, at):
        part, got, sums, got2, red, full = (
            getattr(r, name + tail) for tail in ("_part", "_got", "_sum", "_got2", "_red", "_full")
        )
        send = [r.red_send.at[at * 4 + k] for k in range(4)]
        recv = [r.red_recv.at[at * 4 + k] for k in range(4)]
        along, across = axes[axis], plane_at[axis]
        mine = core * 4 + along
        seven, fifteen = pl.ds(0, 7), pl.ds(0, 15)

        def along_axis(source, target, sems):
            @pl.loop(1, 8, unroll=7)
            def _(step):
                to = lax.rem(mine + step, 8)
                copy_to(source(to), target, *sems, chip(axis, lax.rem(to, 4), across, to // 4))

        def over_plane(source, target, sems):
            @pl.loop(1, 16, unroll=5)
            def _(step):
                to = lax.rem(across + step, 16)
                copy_to(source(to), target, *sems, chip(axis, along, to))

        def pack(grad):
            for half in range(4):
                block = grad[:, half * BLOCK:(half + 1) * BLOCK].astype(BF16)
                low, first = half % 2 * 8, half // 2 * 4
                part[first:first + 4, low:low + 8] = block.reshape(4, 8, 16, BLOCK)

        def scatter():
            along_axis(lambda to: part.at[to], got.at[mine], (send[0], recv[0]))

        def plane():
            got[mine] = part[mine]
            await_bytes(got.at[seven], recv[0])
            sums[...] = jnp.sum(got[...].astype(F32), axis=0).astype(BF16)
            over_plane(lambda to: sums.at[to], got2.at[across], (send[1], recv[1]))

        def gather():
            got2[across] = sums[across]
            await_bytes(got2.at[fifteen], recv[1])
            red[...] = jnp.sum(got2[...].astype(F32), axis=0).astype(BF16)
            full[mine, across] = red[...]
            over_plane(lambda to: red, full.at[mine, across], (send[2], recv[2]))

        def spread():
            await_bytes(got2.at[fifteen], recv[2])
            along_axis(lambda to: full.at[mine], full.at[mine], (send[3], recv[3]))

        def finish():
            await_bytes(got.at[seven], recv[3])
            await_bytes(got.at[seven], send[0])
            await_bytes(got2.at[fifteen], send[1])
            await_bytes(got2.at[fifteen], send[2])
            await_bytes(got.at[seven], send[3])

        return types.SimpleNamespace(
            pack=pack, scatter=scatter, plane=plane, gather=gather, spread=spread, finish=finish)

    early = [reduction("u", "x", 0), reduction("o", "y", 1)]
    early[0].pack(dot_nn(r.xnt[...], r.d_pre[:, :WIDTH]))
    early[1].pack(r.grad_out[...])
    copy_to(r.loss, r.loss_core, r.loss_sem.at[0], r.loss_sem.at[1], mate)

    def loss_along(axis, value, at):
        r.loss_all[at, axes[axis]] = value
        r.loss_sum[at] = value
        for step in range(1, 4):
            copy_to(
                r.loss_sum.at[at], r.loss_all.at[at, axes[axis]],
                r.loss_sem.at[2 + 2 * at], r.loss_sem.at[3 + 2 * at],
                chip(axis, lax.rem(axes[axis] + step, 4), plane_at[axis]),
            )

    def loss_over(at):
        await_bytes(r.loss_all.at[at, pl.ds(0, 3)], r.loss_sem.at[3 + 2 * at])
        return jnp.sum(r.loss_all[at], axis=0)

    @pl.loop(0, n_seq)
    def _(step):
        i = lax.rem(me + step, n_seq)

        @pl.when(i != me)
        def _():
            await_bytes(r.datt_got.at[0], r.datt_sem.at[i])

    @pl.loop(0, n_seq, unroll=4)
    def _(i):
        d_att = r.datt_got[i].astype(F32)
        rows = aligned(i * BLOCK, BLOCK)
        qa = r.qa[rows].astype(F32)
        r.qa[rows] = jnp.where(
            low_block, qa, jnp.concatenate([turned(d_att), d_att], axis=0)
        ).astype(BF16)

    early[0].scatter()
    early[1].scatter()

    r.dq[...] = jnp.zeros_like(r.dq)
    b_tiles = length // BM
    b_per = BM // BLOCK
    kv_scale = jnp.where(low_lanes((1, 2 * HEAD)), 0.5 * inv_len, inv_len)

    def send_d_q(low, high):
        @pl.loop(low, high)
        def _(c):
            for u in range(b_per):
                d_q = r.dq[:, aligned((c * b_per + u) * BLOCK, BLOCK)] * (0.5 * inv_len)
                r.grad_send[c * b_per + u, BLOCK:] = d_q.astype(BF16)

            @pl.loop(0, b_per)
            def _(turn):
                i = c * b_per + lax.rem(me + turn, b_per)

                @pl.when(i != me)
                def _():
                    copy_to(
                        r.grad_send.at[i, pl.ds(BLOCK, HEAD)], r.grad_got.at[me, pl.ds(BLOCK, HEAD)],
                        r.send_sem.at[11], r.grad_sem.at[1], {"seq": i},
                    )

                @pl.when(i == me)
                def _():
                    r.grad_got[me, BLOCK:] = r.grad_send[me, BLOCK:]

    @pl.loop(0, b_tiles)
    def _(step):
        c = tile_at(me // b_per, step, b_tiles)
        m_rows = aligned(c * BM, BM)
        low_tile = low_lanes((BM, 2 * HEAD))

        def piece(start, size, masked):
            size = size * TILE
            t_rows = pl.ds(pl.multiple_of(start * TILE, TILE), size)
            qa = r.qa[t_rows]
            products = dot_nt(r.kv0[c], qa)
            half, d_probs = products[:TILE], products[TILE:]
            if masked:
                ahead = lax.broadcasted_iota(jnp.int32, (BM, size), 0) - lax.broadcasted_iota(
                    jnp.int32, (BM, size), 1
                )
                half = jnp.where(ahead <= 0, half, 0.0)
                d_probs = jnp.where(ahead <= 0, d_probs, 0.0)
            th = jnp.tanh(half)
            up = 1.0 + th
            probs = half * up
            d_scores = (d_probs * up * (1.0 + half * (1.0 - th))).astype(BF16)
            r.dq[:, t_rows] += dot_nn(r.kt[:, m_rows], d_scores)
            return jnp.where(low_tile, dot_nn(d_scores, qa), dot_nn(probs.astype(BF16), qa))

        odd = lax.rem(b_tiles - 1 - c, 2)

        @pl.when(odd == 0)
        def _():
            r.dkv[...] = piece(c, 1, True)

        @pl.when(odd == 1)
        def _():
            r.dkv[...] = piece(c, 2, True)

        def more(start, size):
            r.dkv[...] += piece(start, size, False)

        cover(c + 1 + odd, b_tiles - 1 - c - odd, more)
        for u in range(b_per):
            r.grad_send[c * b_per + u, :BLOCK] = (
                r.dkv[u * BLOCK:(u + 1) * BLOCK] * kv_scale
            ).astype(BF16)

        @pl.loop(0, b_per)
        def _(turn):
            i = c * b_per + lax.rem(me + turn, b_per)

            @pl.when(i != me)
            def _():
                copy_to(
                    r.grad_send.at[i, pl.ds(0, BLOCK)], r.grad_got.at[me, pl.ds(0, BLOCK)],
                    r.send_sem.at[10], r.grad_sem.at[0], {"seq": i},
                )

            @pl.when(i == me)
            def _():
                r.grad_got[me, :BLOCK] = r.grad_send[me, :BLOCK]

        for at, stage in enumerate(("plane", "gather", "spread", "")):
            @pl.when(step == 2 * at + 1)
            def _(at=at, stage=stage):
                if stage:
                    for one in early:
                        getattr(one, stage)()
                if at == 0:
                    await_bytes(r.loss_core, r.loss_sem.at[1])
                    loss_along("x", r.loss[...] + r.loss_core[...], 0)
                if at == 1:
                    loss_along("y", loss_over(0), 1)
                if at == 2:
                    loss_along("z", loss_over(1), 2)
                if at == 3:
                    count = jnp.full((8, BLOCK), total, jnp.int32).astype(F32)
                    r.loss_out[0] = (loss_over(2) / count)[0, 0]

        end = tile_at(me // b_per, b_tiles - 1, b_tiles)

        @pl.when(step == b_tiles - 2)
        def _():
            send_d_q(0, end)

        @pl.when(step == b_tiles - 1)
        def _():
            send_d_q(end, b_tiles)

    late = [reduction("v", "x", 2), reduction("k", "y", 3), reduction("q", "z", 4)]
    await_bytes(r.grad_got.at[others, pl.ds(0, BLOCK)], r.grad_sem.at[0])

    @pl.loop(0, n_here)
    def _(b):
        rows = aligned(b * BLOCK, BLOCK)
        for pair in range(PAIRS):
            j = b * HEADS + 2 * pair
            d_k, d_v = swapped(r.grad_got[j, :BLOCK].astype(F32), r.grad_got[j + 1, :BLOCK].astype(F32))
            for part, grad in ((1, d_v), (3, d_k)):
                at = part * WIDTH + pair * 2 * HEAD
                slope = r.slope[b, :, at:at + 2 * HEAD].astype(F32)
                r.d_pre[rows, at:at + 2 * HEAD] = (grad * slope).astype(BF16)

    late[0].pack(dot_nn(r.xnt[...], r.d_pre[:, WIDTH:2 * WIDTH]))
    late[0].scatter()
    late[1].pack(dot_nn(r.xnt[...], r.d_pre[:, 3 * WIDTH:]))
    late[1].scatter()
    await_bytes(r.grad_got.at[others, pl.ds(BLOCK, HEAD)], r.grad_sem.at[1])

    @pl.loop(0, n_here)
    def _(b):
        rows = aligned(b * BLOCK, BLOCK)
        for pair in range(PAIRS):
            j = b * HEADS + 2 * pair
            at = 2 * WIDTH + pair * 2 * HEAD
            grad = jnp.transpose(
                jnp.concatenate([r.grad_got[j + e, BLOCK:].astype(F32) for e in range(2)], axis=0)
            )
            slope = r.slope[b, :, at:at + 2 * HEAD].astype(F32)
            r.d_pre[rows, at:at + 2 * HEAD] = (grad * slope).astype(BF16)

    late[2].pack(dot_nn(r.xnt[...], r.d_pre[:, 2 * WIDTH:3 * WIDTH]))
    late[2].scatter()
    for stage in ("plane", "gather", "spread"):
        for one in late:
            getattr(one, stage)()

    for one in early + late:
        one.finish()

    await_bytes(r.first, r.send_sem.at[1])
    await_bytes(r.ids, r.send_sem.at[2])
    for at in (3, 5, 8):
        await_bytes(r.negs.at[0], r.send_sem.at[at])
        await_bytes(r.all_ids.at[0], r.send_sem.at[at + 1])
    await_bytes(r.att_send.at[others], r.send_sem.at[7])
    await_bytes(r.datt_send.at[others], r.send_sem.at[12])
    await_bytes(r.grad_send.at[others, pl.ds(0, BLOCK)], r.send_sem.at[10])
    await_bytes(r.grad_send.at[others, pl.ds(BLOCK, HEAD)], r.send_sem.at[11])
    await_bytes(r.loss, r.loss_sem.at[0])
    for at in range(3):
        await_bytes(r.loss_all.at[at, pl.ds(0, 3)], r.loss_sem.at[2 + 2 * at])


def activated(r, b, xn, part):
    half = 0.5 * dot_nn(xn, r.w_joined[:, part * WIDTH:(part + 1) * WIDTH])
    th = jnp.tanh(half)
    slope = (0.5 + 0.5 * th) * (1.0 + half * (1.0 - th))
    r.slope[b, :, part * WIDTH:(part + 1) * WIDTH] = slope.astype(BF16)
    return half + half * th


def middle(r, n_seq, me, grp, first_b, weight):
    both = 2
    rows = both * BLOCK
    n_here = r.x.shape[0]
    n_grp, n_neg = r.negs.shape[:2]

    def joined(make):
        return jnp.concatenate([make(e) for e in range(both)], axis=0)

    @pl.loop(0, both * HEADS)
    def _(turn):
        j = first_b * HEADS + turn

        @pl.when(j != me)
        def _():
            await_bytes(r.att_got.at[0], r.att_sem.at[j])

    for e in range(both):
        for pair in range(PAIRS):
            j = (first_b + e) * HEADS + 2 * pair
            top, bottom = swapped(r.att_got[j].astype(F32), r.att_got[j + 1].astype(F32))
            r.att[e * BLOCK:e * BLOCK + HEAD, pair_cols(pair)] = top
            r.att[e * BLOCK + HEAD:(e + 1) * BLOCK, pair_cols(pair)] = bottom

    att = r.att[...]
    centered = att - jnp.mean(att, axis=-1, keepdims=True)
    inv_att = lax.rsqrt(jnp.mean(centered * centered, axis=-1, keepdims=True) + eps_norm)
    normed = centered * inv_att
    u = joined(lambda e: r.u[first_b + e]).astype(F32)
    gated = (normed * u).astype(BF16)
    x = joined(lambda e: r.x[first_b + e]).astype(F32)
    out_rows = x + dot_nn(gated, r.w_out[...])
    inv_y = lax.rsqrt(jnp.sum(out_rows * out_rows, axis=-1, keepdims=True) + eps_norm)
    unit_y = out_rows * inv_y
    unit_b = unit_y.astype(BF16)
    more = jnp.where(me == n_seq - 1, 0, 1)
    last_row = lax.broadcasted_iota(jnp.int32, (BLOCK, WIDTH), 0) == BLOCK - 1
    last_lane = lax.broadcasted_iota(jnp.int32, (1, BLOCK), 1) == BLOCK - 1

    def next_rows(e):
        shifted = pltpu.roll(r.x[first_b + e].astype(F32), BLOCK - 1, axis=0)
        return jnp.where(last_row, r.first[first_b + e].astype(F32)[:1] * more.astype(F32), shifted)

    x_next = joined(next_rows)
    pos_unit = (
        x_next * lax.rsqrt(jnp.sum(x_next * x_next, axis=-1, keepdims=True) + eps_norm)
    ).astype(BF16).astype(F32)
    pos_logit = logit_scale * jnp.sum(unit_b.astype(F32) * pos_unit, axis=-1, keepdims=True)

    def row_ids(e):
        shifted = pltpu.roll(r.ids[pl.ds(first_b + e, 1)], BLOCK - 1, axis=1)
        coming = pltpu.roll(r.next_ids[pl.ds(first_b + e, 1)], BLOCK - 1, axis=1) * more
        return jnp.transpose(jnp.broadcast_to(jnp.where(last_lane, coming, shifted), (BLOCK, BLOCK)))

    ids = joined(row_ids)
    lane_sum = jnp.zeros((rows, BLOCK), F32)
    for g in range(n_grp):
        neg_logit = logit_scale * dot_nt(unit_b, r.negs[g])
        for sub in range(n_neg // BLOCK):
            at = (g * n_neg) + sub * BLOCK
            hit = r.all_ids[g, n_here + sub:n_here + sub + 1] == ids
            exps = jnp.where(hit, 0.0, jnp.exp(neg_logit[:, sub * BLOCK:(sub + 1) * BLOCK]))
            r.exps[:, at:at + BLOCK] = exps
            lane_sum = lane_sum + exps
    pos_exp = jnp.exp(pos_logit)
    denom = pos_exp + jnp.sum(lane_sum, axis=-1, keepdims=True)

    def row_valid(e):
        pos = me * BLOCK + lax.broadcasted_iota(jnp.int32, (BLOCK, 1), 0)
        return jnp.where(pos + 1 < r.lens[grp * n_here + first_b + e], 1.0, 0.0)

    valid = joined(row_valid)
    row_loss = jnp.where(valid > 0.0, jnp.log(denom) - pos_logit, 0.0)
    r.loss[...] += jnp.broadcast_to(jnp.sum(row_loss, axis=0, keepdims=True), r.loss.shape)
    row_weight = valid * weight
    d_pos = row_weight * (pos_exp / denom - 1.0)
    scale = row_weight / denom
    neg_back = jnp.zeros((rows, WIDTH), F32)
    for g in range(n_grp):
        d_neg = (scale * r.exps[:, g * n_neg:(g + 1) * n_neg]).astype(BF16)
        neg_back = neg_back + dot_nn(d_neg, r.negs[g])
    d_unit = logit_scale * (d_pos * pos_unit + neg_back)
    d_out = (
        (d_unit - unit_y * jnp.sum(unit_y * d_unit, axis=-1, keepdims=True)) * inv_y
    ).astype(BF16)
    d_gate = dot_nt(d_out, r.w_out[...])
    d_norm = d_gate * u
    d_att = inv_att * (
        d_norm
        - jnp.mean(d_norm, axis=-1, keepdims=True)
        - normed * jnp.mean(d_norm * normed, axis=-1, keepdims=True)
    )
    for e in range(both):
        rows_e = d_att[e * BLOCK:(e + 1) * BLOCK]
        for pair in range(PAIRS):
            cols = pair_cols(pair)
            packed = swapped(rows_e[:HEAD, cols], rows_e[HEAD:, cols])
            for odd in range(2):
                r.datt_send[(first_b + e) * HEADS + 2 * pair + odd] = packed[odd].astype(BF16)

    @pl.loop(0, both * HEADS)
    def _(turn):
        j = first_b * HEADS + lax.rem(me + turn, both * HEADS)

        @pl.when(j != me)
        def _():
            copy_to(
                r.datt_send.at[j], r.datt_got.at[me], r.send_sem.at[12], r.datt_sem.at[me], {"seq": j}
            )

        @pl.when(j == me)
        def _():
            r.datt_got[me] = r.datt_send[me]

    r.grad_out[...] += dot_tn(gated, d_out)
    d_u = d_gate * normed
    for e in range(both):
        slope = r.slope[first_b + e, :, :WIDTH].astype(F32)
        r.d_pre[aligned((first_b + e) * BLOCK, BLOCK), :WIDTH] = (
            d_u[e * BLOCK:(e + 1) * BLOCK] * slope
        ).astype(BF16)


def widen(*refs):
    *blocks, joined, out = refs
    for at, block in enumerate(blocks):
        for half in range(4):
            values = block[half // 2, 0, half % 2].reshape(HEAD, BLOCK).astype(F32)
            if at < 4:
                joined[:, at * WIDTH + half * BLOCK:at * WIDTH + (half + 1) * BLOCK] = values
            else:
                out[:, half * BLOCK:(half + 1) * BLOCK] = values


def local(inputs, history, lengths, w_joined, w_out, neg_emb, neg_ids):
    n_here, block, width = inputs.shape
    n_seq = lax.axis_size("seq")
    length = n_seq * block
    lanes = 2 * HEAD
    rows = n_here * block
    n_neg = neg_emb.shape[0]
    dma = pltpu.SemaphoreType.DMA
    buffers = dict(
        xn=((n_here, block, width), BF16), xnt=((width, rows), BF16), u=((n_here, block, width), BF16),
        slope=((n_here, block, 4 * width), BF16), d_pre=((rows, 4 * width), BF16),
        send=((n_seq, BLOCK + HEAD, lanes), BF16), got=((n_seq, BLOCK + HEAD, lanes), BF16),
        att_send=((n_seq, HEAD, lanes), BF16), att_got=((n_seq, HEAD, lanes), BF16),
        datt_send=((n_seq, HEAD, lanes), BF16), datt_got=((n_seq, HEAD, lanes), BF16),
        grad_send=((n_seq, BLOCK + HEAD, lanes), BF16), grad_got=((n_seq, BLOCK + HEAD, lanes), BF16),
        first=((n_here, 16, width), BF16), ids=((2 * n_here, block), jnp.int32),
        next_ids=((2 * n_here, block), jnp.int32), negs=((4, n_neg, width), BF16),
        all_ids=((4, 2 * n_here, block), jnp.int32),
        kv0=((length // TILE, 2 * TILE, lanes), BF16), qa=((length, lanes), BF16),
        kt=((HEAD, length), BF16), acc=((FQ, lanes), F32), dq=((HEAD, length), F32), dkv=((BM, lanes), F32),
        att=((2 * block, width), F32), exps=((2 * block, 4 * n_neg), F32), grad_out=((width, width), F32),
        loss=((8, block), F32), loss_core=((8, block), F32), loss_sum=((3, 8, block), F32),
        loss_all=((3, 4, 8, block), F32), x=((n_here, block, width), BF16),
        w_joined=((width, 4 * width), BF16), w_out=((width, width), BF16), neg_emb=((n_neg, width), BF16),
        history=((n_here, block), jnp.int32), neg_ids=((n_here, block), jnp.int32),
    )
    wide = (8, 16, 16, block)
    for name in "uovkq":
        buffers[name + "_part"] = buffers[name + "_got"] = (wide, BF16)
        buffers[name + "_sum"] = buffers[name + "_got2"] = (wide[1:], BF16)
        buffers[name + "_red"] = (wide[2:], BF16)
    sems = dict(
        send_sem=13, one_sem=8, got_sem=n_seq, att_sem=n_seq, datt_sem=n_seq, grad_sem=2, loss_sem=8,
        red_send=20, red_recv=20, load_sem=6,
    )
    takes = ("lens", "x_in", "history_in", "neg_ids_in", "w_joined_in", "w_out_in", "neg_emb_in")
    gives = {name + "_full": (wide, BF16) for name in "uvqko"}
    gives["loss_out"] = ((1,), F32)
    names = takes + tuple(gives) + tuple(buffers) + tuple(sems)
    *grads, loss = pl.pallas_call(
        functools.partial(kernel, n_seq, names),
        out_shape=[jax.ShapeDtypeStruct(*kind) for kind in gives.values()],
        in_specs=[SMEM] + [pl.BlockSpec(memory_space=pl.ANY)] * (len(takes) - 1),
        out_specs=[VMEM] * 5 + [SMEM],
        scratch_shapes=[pltpu.VMEM(*kind) for kind in buffers.values()]
        + [dma((count,)) for count in sems.values()],
        compiler_params=pltpu.CompilerParams(
            collective_id=0, has_side_effects=True, vmem_limit_bytes=60 * 1024 * 1024
        ),
    )(lengths, inputs, history, neg_ids.reshape(-1, block), w_joined, w_out, neg_emb)
    taken = pl.BlockSpec((2, 1, 2, 4, 16, block), lambda at: (0, at // 2, 0, at % 2, 0, 0))
    joined, out = pl.pallas_call(
        widen,
        grid=(8,),
        out_shape=[
            jax.ShapeDtypeStruct((width, 4 * width), F32), jax.ShapeDtypeStruct((width, width), F32)
        ],
        in_specs=[taken] * 5,
        out_specs=[
            pl.BlockSpec((width // 8, 4 * width), lambda at: (at, 0)),
            pl.BlockSpec((width // 8, width), lambda at: (at, 0)),
        ],
        compiler_params=pltpu.CompilerParams(vmem_limit_bytes=60 * 1024 * 1024),
    )(*(grad.reshape((2, 4, 2, 8) + wide[2:]) for grad in grads))
    return (joined, out, loss.reshape(()))


def solution(mesh):
    placed = (
        P("grp", "seq", None),
        P("grp", "seq"),
        P(),
        P(),
        P(),
        P(("grp", "seq"), None),
        P(("grp", "seq")),
    )
    return jax.shard_map(
        local, mesh=mesh, in_specs=placed, out_specs=(P(), P(), P()), check_vma=False
    )
```

```python
import functools
import types

import jax
import jax.numpy as jnp
from jax import lax
from jax.experimental import pallas as pl
from jax.experimental.pallas import tpu as pltpu
from jax.sharding import PartitionSpec as P

HEADS = 8
HEAD = 64
WIDTH = 512
PAIRS = 4
BLOCK = 128
TILE = 512
FQ = TILE
BM = TILE
eps_norm = 1e-06
logit_scale = 64.0

MESH = pl.DeviceIdType.MESH
F32 = jnp.float32
BF16 = jnp.bfloat16
VMEM = pl.BlockSpec(memory_space=pltpu.VMEM)
SMEM = pl.BlockSpec(memory_space=pltpu.SMEM)


def dot_nn(a, b):
    return lax.dot_general(a, b, (((1,), (0,)), ((), ())), preferred_element_type=F32)


def dot_nt(a, b):
    return lax.dot_general(a, b, (((1,), (1,)), ((), ())), preferred_element_type=F32)


def dot_tn(a, b):
    return lax.dot_general(a, b, (((0,), (0,)), ((), ())), preferred_element_type=F32)


def low_lanes(shape):
    return lax.broadcasted_iota(jnp.int32, shape, 1) < HEAD


def turned(a):
    return pltpu.roll(a, HEAD, axis=1)


def swapped(a, b):
    low = low_lanes(a.shape)
    return jnp.where(low, a, turned(b)), jnp.where(low, turned(a), b)


def copy_to(src, dst, send_sem, recv_sem, where):
    pltpu.make_async_remote_copy(
        src_ref=src, dst_ref=dst, send_sem=send_sem, recv_sem=recv_sem,
        device_id=where, device_id_type=MESH,
    ).start()


def await_bytes(ref, sem):
    pltpu.make_async_copy(ref, ref, sem).wait()


def aligned(at, size):
    return pl.ds(pl.multiple_of(at, size), size)


def pair_cols(pair):
    return slice(pair * 2 * HEAD, (pair + 1) * 2 * HEAD)


def shifts(n_seq):
    side = int((n_seq // 2) ** 0.5)
    steps = [(x, y, z) for x in range(side) for y in range(side) for z in range(2)]
    return sorted(steps[1:], key=lambda at: -(min(at[0], side - at[0]) + min(at[1], side - at[1]) + at[2]))


def peer(me, shift):
    x, y, z = me // HEADS, lax.rem(me // 2, 4), lax.rem(me, 2)
    return (lax.rem(x + shift[0], 4) * 4 + lax.rem(y + shift[1], 4)) * 2 + lax.rem(z + shift[2], 2)


def cover(first, count, body):
    done = 0
    for tiles in (4, 2):
        n = count // tiles if tiles == 4 else lax.rem(count // tiles, 2)

        @pl.loop(0, n)
        def _(at, done=done, tiles=tiles):
            body(first + done + at * tiles, tiles)

        done = done + n * tiles


def tile_at(first, step, tiles):
    low = lax.rem(first + step // 2, tiles // 2)
    odd = lax.rem(step, 2)
    return low + odd * (tiles - 1 - 2 * low)


def kernel(n_seq, names, *refs):
    r = types.SimpleNamespace(**dict(zip(names, refs, strict=True)))
    me = lax.axis_index("seq")
    grp = lax.axis_index("grp")
    core, z_hi = lax.rem(grp, 2), grp // 2
    loads = [
        pltpu.make_async_copy(getattr(r, name + "_in"), getattr(r, name), r.load_sem.at[at])
        for at, name in enumerate(("x", "w_joined", "history", "neg_ids", "neg_emb", "w_out"))
    ]
    for load in loads:
        load.start()
    n_here = r.x.shape[0]
    planes = n_seq // HEADS
    length = n_seq * BLOCK
    mate = {"grp": grp + 1 - 2 * core}
    other_z = {"grp": (1 - z_hi) * 2 + core}
    others = pl.ds(0, n_seq - 1)
    x_at, y_at, z_at = me // HEADS, lax.rem(me // 2, 4), z_hi * 2 + lax.rem(me, 2)

    barrier = pltpu.get_barrier_semaphore()

    def greet(where):
        pl.semaphore_signal(barrier, inc=1, device_id=where, device_id_type=MESH)

    greet(mate)

    @pl.loop(1, n_seq)
    def _(step):
        greet({"seq": lax.rem(me + step, n_seq)})

    for step in range(4):
        for z in range(2):
            greet(dict(other_z, seq=(x_at * 4 + lax.rem(y_at + step, 4)) * 2 + z))
            if step:
                greet(dict(other_z, seq=(lax.rem(x_at + step, 4) * 4 + y_at) * 2 + z))

    def lane(axis, along):
        x, y, z = (along if axis == name else at for name, at in (("x", x_at), ("y", y_at), ("z", z_at)))
        return {"grp": z // 2 * 2 + 1 - core, "seq": (x * 4 + y) * 2 + lax.rem(z, 2)}

    for axis, at in (("x", x_at), ("y", y_at), ("z", z_at)):
        for step in range(1, 4):
            greet(lane(axis, lax.rem(at + step, 4)))
    n_peers = n_seq + 14 + 9

    loads[0].wait()
    loads[1].wait()

    @pl.loop(0, n_here)
    def _(b):
        x = r.x[b].astype(F32)
        centered = x - jnp.mean(x, axis=-1, keepdims=True)
        var = jnp.mean(centered * centered, axis=-1, keepdims=True)
        xn = (centered * lax.rsqrt(var + eps_norm)).astype(BF16)
        r.xn[b] = xn
        v, q, k = (activated(r, b, xn, part) for part in (1, 2, 3))
        for pair in range(PAIRS):
            cols = pair_cols(pair)
            kv = swapped(k[:, cols], v[:, cols])
            qs = swapped(q[:HEAD, cols], q[HEAD:, cols])
            for odd in range(2):
                j = b * HEADS + 2 * pair + odd
                r.send[j, :BLOCK] = kv[odd].astype(BF16)
                r.send[j, BLOCK:] = qs[odd].astype(BF16)

    pl.semaphore_wait(barrier, n_peers)
    for shift in shifts(n_seq):
        j = peer(me, shift)
        copy_to(r.send.at[j], r.got.at[me], r.send_sem.at[0], r.got_sem.at[me], {"seq": j})
    r.got[me] = r.send[me]

    before = {"seq": lax.rem(me + n_seq - 1, n_seq)}
    loads[2].wait()
    loads[3].wait()
    r.ids[:n_here] = r.history[...]
    r.ids[n_here:] = r.neg_ids[...]
    copy_to(r.x.at[:, pl.ds(0, 16)], r.first, r.send_sem.at[1], r.one_sem.at[0], before)
    copy_to(r.ids, r.next_ids, r.send_sem.at[2], r.one_sem.at[1], before)

    loads[4].wait()
    loads[5].wait()

    @pl.loop(0, n_here)
    def _(b):
        xn = r.xn[b]
        r.u[b] = activated(r, b, xn, 0).astype(BF16)
        r.xnt[:, aligned(b * BLOCK, BLOCK)] = jnp.transpose(xn.astype(F32)).astype(BF16)
        rows = aligned(b * BLOCK, BLOCK)
        emb = r.neg_emb[rows].astype(F32)
        r.negs[grp, rows] = (
            emb * lax.rsqrt(jnp.sum(emb * emb, axis=-1, keepdims=True) + eps_norm)
        ).astype(BF16)

    r.all_ids[grp] = r.ids[...]

    seq_len = r.lens[grp * n_here + me // HEADS]
    low = low_lanes((HEAD, 2 * HEAD))
    low_block = low_lanes((BLOCK, 2 * HEAD))

    @pl.loop(0, planes)
    def _(step):
        first = lax.rem(me // HEADS + planes // 2 + step, planes) * HEADS

        @pl.loop(0, HEADS)
        def _(turn):
            i = first + turn

            @pl.when(i != me)
            def _():
                await_bytes(r.got.at[0], r.got_sem.at[i])

        @pl.loop(0, HEADS, unroll=4)
        def _(turn):
            i = first + turn
            rows = aligned(i * BLOCK, BLOCK)
            pos = i * BLOCK + lax.broadcasted_iota(jnp.int32, (BLOCK, 2 * HEAD), 0)
            kv = jnp.where(pos < seq_len, r.got[i, :BLOCK].astype(F32), 0.0)
            tile, at = i // (TILE // BLOCK), lax.rem(i, TILE // BLOCK) * BLOCK
            r.kv0[tile, aligned(at, BLOCK)] = jnp.where(low_block, 0.5 * kv, 0.0).astype(BF16)
            r.kv0[tile, aligned(TILE + at, BLOCK)] = jnp.where(low_block, 0.0, kv).astype(BF16)
            r.kt[:, rows] = jnp.transpose(kv)[:HEAD].astype(BF16)
            q = r.got[i, BLOCK:].astype(F32)
            r.qa[rows] = jnp.concatenate(
                [jnp.where(low, q, 0.0), jnp.where(low, turned(q), 0.0)], axis=0
            ).astype(BF16)

    copy_to(r.negs.at[grp], r.negs.at[grp], r.send_sem.at[3], r.one_sem.at[2], mate)
    copy_to(r.all_ids.at[grp], r.all_ids.at[grp], r.send_sem.at[4], r.one_sem.at[3], mate)
    copy_to(r.negs.at[grp], r.negs.at[grp], r.send_sem.at[5], r.one_sem.at[4], other_z)
    copy_to(r.all_ids.at[grp], r.all_ids.at[grp], r.send_sem.at[6], r.one_sem.at[5], other_z)
    await_bytes(r.send.at[others], r.send_sem.at[0])
    inv_len = 1.0 / jnp.full((1, 2 * HEAD), seq_len, jnp.int32).astype(F32)

    f_tiles = length // FQ
    f_per = FQ // BLOCK

    @pl.loop(0, f_tiles)
    def _(step):
        c = tile_at(me // f_per, f_tiles - 1 - step, f_tiles)
        q = r.qa[aligned(c * FQ, FQ)]

        def piece(start, size, masked):
            rows = pl.ds(start, size)
            size = size * TILE
            half = dot_nt(q, r.kv0[rows, :TILE].reshape(size, 2 * HEAD))
            if masked:
                ahead = lax.broadcasted_iota(jnp.int32, (FQ, size), 1) - lax.broadcasted_iota(
                    jnp.int32, (FQ, size), 0
                )
                half = jnp.where(ahead <= size - FQ, half, 0.0)
            probs = (half + half * jnp.tanh(half)).astype(BF16)
            return dot_nn(probs, r.kv0[rows, TILE:].reshape(size, 2 * HEAD))

        odd = lax.rem(c, 2)

        @pl.when(odd == 0)
        def _():
            r.acc[...] = piece(c, 1, True)

        @pl.when(odd == 1)
        def _():
            r.acc[...] = piece(c - 1, 2, True)

        def more(start, size):
            r.acc[...] += piece(start, size, False)

        cover(0, c - odd, more)
        for u in range(f_per):
            out = r.acc[u * BLOCK:(u + 1) * BLOCK] * inv_len
            top, bottom = out[:HEAD], out[HEAD:]
            r.att_send[c * f_per + u] = jnp.where(low, turned(top), bottom).astype(BF16)

        @pl.loop(0, f_per)
        def _(turn):
            i = c * f_per + lax.rem(me + turn, f_per)

            @pl.when(i != me)
            def _():
                copy_to(
                    r.att_send.at[i], r.att_got.at[me], r.send_sem.at[7], r.att_sem.at[me], {"seq": i}
                )

            @pl.when(i == me)
            def _():
                r.att_got[me] = r.att_send[me]

    far = (1 - z_hi) * 2 + core
    await_bytes(r.negs.at[0], r.one_sem.at[4])
    await_bytes(r.all_ids.at[0], r.one_sem.at[5])
    copy_to(r.negs.at[far], r.negs.at[far], r.send_sem.at[8], r.one_sem.at[6], mate)
    copy_to(r.all_ids.at[far], r.all_ids.at[far], r.send_sem.at[9], r.one_sem.at[7], mate)

    total = r.lens[0] - 1
    for at in range(1, r.lens.shape[0]):
        total = total + (r.lens[at] - 1)
    both = 2
    half_rows = both * BLOCK
    weight = 1.0 / jnp.full((half_rows, 1), total, jnp.int32).astype(F32)
    r.grad_out[...] = jnp.zeros_like(r.grad_out)
    r.loss[...] = jnp.zeros_like(r.loss)
    await_bytes(r.first, r.one_sem.at[0])
    await_bytes(r.ids, r.one_sem.at[1])
    await_bytes(r.negs.at[0], r.one_sem.at[2])
    await_bytes(r.all_ids.at[0], r.one_sem.at[3])
    await_bytes(r.negs.at[0], r.one_sem.at[6])
    await_bytes(r.all_ids.at[0], r.one_sem.at[7])
    n_halves = n_here // both

    @pl.loop(0, n_halves)
    def _(step):
        middle(r, n_seq, me, grp, both * lax.rem(me // (both * HEADS) + step, n_halves), weight)

    axes = dict(x=x_at, y=y_at, z=z_at)
    plane_at = dict(x=y_at * 4 + z_at, y=x_at * 4 + z_at, z=x_at * 4 + y_at)

    def chip(axis, along, across, of_core=core):
        hi, lo = across // 4, lax.rem(across, 4)
        x, y, z = dict(x=(along, hi, lo), y=(hi, along, lo), z=(hi, lo, along))[axis]
        return {"grp": z // 2 * 2 + of_core, "seq": (x * 4 + y) * 2 + lax.rem(z, 2)}

    def reduction(name, axis, at):
        part, got, sums, got2, red, full = (
            getattr(r, name + tail) for tail in ("_part", "_got", "_sum", "_got2", "_red", "_full")
        )
        send = [r.red_send.at[at * 4 + k] for k in range(4)]
        recv = [r.red_recv.at[at * 4 + k] for k in range(4)]
        along, across = axes[axis], plane_at[axis]
        mine = core * 4 + along
        seven, fifteen = pl.ds(0, 7), pl.ds(0, 15)

        def along_axis(source, target, sems):
            @pl.loop(1, 8, unroll=7)
            def _(step):
                to = lax.rem(mine + step, 8)
                copy_to(source(to), target, *sems, chip(axis, lax.rem(to, 4), across, to // 4))

        def over_plane(source, target, sems):
            @pl.loop(1, 16, unroll=5)
            def _(step):
                to = lax.rem(across + step, 16)
                copy_to(source(to), target, *sems, chip(axis, along, to))

        def pack(grad):
            for half in range(4):
                block = grad[:, half * BLOCK:(half + 1) * BLOCK].astype(BF16)
                low, first = half % 2 * 8, half // 2 * 4
                part[first:first + 4, low:low + 8] = block.reshape(4, 8, 16, BLOCK)

        def scatter():
            along_axis(lambda to: part.at[to], got.at[mine], (send[0], recv[0]))

        def plane():
            got[mine] = part[mine]
            await_bytes(got.at[seven], recv[0])
            sums[...] = jnp.sum(got[...].astype(F32), axis=0).astype(BF16)
            over_plane(lambda to: sums.at[to], got2.at[across], (send[1], recv[1]))

        def gather():
            got2[across] = sums[across]
            await_bytes(got2.at[fifteen], recv[1])
            red[...] = jnp.sum(got2[...].astype(F32), axis=0).astype(BF16)
            full[mine, across] = red[...]
            over_plane(lambda to: red, full.at[mine, across], (send[2], recv[2]))

        def spread():
            await_bytes(got2.at[fifteen], recv[2])
            along_axis(lambda to: full.at[mine], full.at[mine], (send[3], recv[3]))

        def finish():
            await_bytes(got.at[seven], recv[3])
            await_bytes(got.at[seven], send[0])
            await_bytes(got2.at[fifteen], send[1])
            await_bytes(got2.at[fifteen], send[2])
            await_bytes(got.at[seven], send[3])

        return types.SimpleNamespace(
            pack=pack, scatter=scatter, plane=plane, gather=gather, spread=spread, finish=finish)

    early = [reduction("u", "x", 0), reduction("o", "y", 1)]
    early[0].pack(dot_nn(r.xnt[...], r.d_pre[:, :WIDTH]))
    early[1].pack(r.grad_out[...])
    copy_to(r.loss, r.loss_core, r.loss_sem.at[0], r.loss_sem.at[1], mate)

    def loss_along(axis, value, at):
        r.loss_all[at, axes[axis]] = value
        r.loss_sum[at] = value
        for step in range(1, 4):
            copy_to(
                r.loss_sum.at[at], r.loss_all.at[at, axes[axis]],
                r.loss_sem.at[2 + 2 * at], r.loss_sem.at[3 + 2 * at],
                chip(axis, lax.rem(axes[axis] + step, 4), plane_at[axis]),
            )

    def loss_over(at):
        await_bytes(r.loss_all.at[at, pl.ds(0, 3)], r.loss_sem.at[3 + 2 * at])
        return jnp.sum(r.loss_all[at], axis=0)

    @pl.loop(0, n_seq)
    def _(step):
        i = lax.rem(me + step, n_seq)

        @pl.when(i != me)
        def _():
            await_bytes(r.datt_got.at[0], r.datt_sem.at[i])

    @pl.loop(0, n_seq, unroll=4)
    def _(i):
        d_att = r.datt_got[i].astype(F32)
        rows = aligned(i * BLOCK, BLOCK)
        qa = r.qa[rows].astype(F32)
        r.qa[rows] = jnp.where(
            low_block, qa, jnp.concatenate([turned(d_att), d_att], axis=0)
        ).astype(BF16)

    early[0].scatter()
    early[1].scatter()

    r.dq[...] = jnp.zeros_like(r.dq)
    b_tiles = length // BM
    b_per = BM // BLOCK
    kv_scale = jnp.where(low_lanes((1, 2 * HEAD)), 0.5 * inv_len, inv_len)

    def send_d_q(low, high):
        @pl.loop(low, high)
        def _(c):
            for u in range(b_per):
                d_q = r.dq[:, aligned((c * b_per + u) * BLOCK, BLOCK)] * (0.5 * inv_len)
                r.grad_send[c * b_per + u, BLOCK:] = d_q.astype(BF16)

            @pl.loop(0, b_per)
            def _(turn):
                i = c * b_per + lax.rem(me + turn, b_per)

                @pl.when(i != me)
                def _():
                    copy_to(
                        r.grad_send.at[i, pl.ds(BLOCK, HEAD)], r.grad_got.at[me, pl.ds(BLOCK, HEAD)],
                        r.send_sem.at[11], r.grad_sem.at[1], {"seq": i},
                    )

                @pl.when(i == me)
                def _():
                    r.grad_got[me, BLOCK:] = r.grad_send[me, BLOCK:]

    @pl.loop(0, b_tiles)
    def _(step):
        c = tile_at(me // b_per, step, b_tiles)
        m_rows = aligned(c * BM, BM)
        low_tile = low_lanes((BM, 2 * HEAD))

        def piece(start, size, masked):
            size = size * TILE
            t_rows = pl.ds(pl.multiple_of(start * TILE, TILE), size)
            qa = r.qa[t_rows]
            products = dot_nt(r.kv0[c], qa)
            half, d_probs = products[:TILE], products[TILE:]
            if masked:
                ahead = lax.broadcasted_iota(jnp.int32, (BM, size), 0) - lax.broadcasted_iota(
                    jnp.int32, (BM, size), 1
                )
                half = jnp.where(ahead <= 0, half, 0.0)
                d_probs = jnp.where(ahead <= 0, d_probs, 0.0)
            th = jnp.tanh(half)
            up = 1.0 + th
            probs = half * up
            d_scores = (d_probs * up * (1.0 + half * (1.0 - th))).astype(BF16)
            r.dq[:, t_rows] += dot_nn(r.kt[:, m_rows], d_scores)
            return jnp.where(low_tile, dot_nn(d_scores, qa), dot_nn(probs.astype(BF16), qa))

        odd = lax.rem(b_tiles - 1 - c, 2)

        @pl.when(odd == 0)
        def _():
            r.dkv[...] = piece(c, 1, True)

        @pl.when(odd == 1)
        def _():
            r.dkv[...] = piece(c, 2, True)

        def more(start, size):
            r.dkv[...] += piece(start, size, False)

        cover(c + 1 + odd, b_tiles - 1 - c - odd, more)
        for u in range(b_per):
            r.grad_send[c * b_per + u, :BLOCK] = (
                r.dkv[u * BLOCK:(u + 1) * BLOCK] * kv_scale
            ).astype(BF16)

        @pl.loop(0, b_per)
        def _(turn):
            i = c * b_per + lax.rem(me + turn, b_per)

            @pl.when(i != me)
            def _():
                copy_to(
                    r.grad_send.at[i, pl.ds(0, BLOCK)], r.grad_got.at[me, pl.ds(0, BLOCK)],
                    r.send_sem.at[10], r.grad_sem.at[0], {"seq": i},
                )

            @pl.when(i == me)
            def _():
                r.grad_got[me, :BLOCK] = r.grad_send[me, :BLOCK]

        for at in range(4):
            @pl.when(step == 2 * at + 1)
            def _(at=at):
                if at == 0:
                    await_bytes(r.loss_core, r.loss_sem.at[1])
                    loss_along("x", r.loss[...] + r.loss_core[...], 0)
                if at == 1:
                    loss_along("y", loss_over(0), 1)
                if at == 2:
                    loss_along("z", loss_over(1), 2)
                if at == 3:
                    count = jnp.full((8, BLOCK), total, jnp.int32).astype(F32)
                    r.loss_out[0] = (loss_over(2) / count)[0, 0]

        end = tile_at(me // b_per, b_tiles - 1, b_tiles)

        @pl.when(step == b_tiles - 2)
        def _():
            send_d_q(0, end)

        @pl.when(step == b_tiles - 1)
        def _():
            send_d_q(end, b_tiles)

    late = [reduction("v", "x", 2), reduction("k", "y", 3), reduction("q", "z", 4)]
    for one in early:
        one.plane()
    await_bytes(r.grad_got.at[others, pl.ds(0, BLOCK)], r.grad_sem.at[0])

    @pl.loop(0, n_here)
    def _(b):
        rows = aligned(b * BLOCK, BLOCK)
        for pair in range(PAIRS):
            j = b * HEADS + 2 * pair
            d_k, d_v = swapped(r.grad_got[j, :BLOCK].astype(F32), r.grad_got[j + 1, :BLOCK].astype(F32))
            for part, grad in ((1, d_v), (3, d_k)):
                at = part * WIDTH + pair * 2 * HEAD
                slope = r.slope[b, :, at:at + 2 * HEAD].astype(F32)
                r.d_pre[rows, at:at + 2 * HEAD] = (grad * slope).astype(BF16)

    late[0].pack(dot_nn(r.xnt[...], r.d_pre[:, WIDTH:2 * WIDTH]))
    late[0].scatter()
    late[1].pack(dot_nn(r.xnt[...], r.d_pre[:, 3 * WIDTH:]))
    late[1].scatter()
    await_bytes(r.grad_got.at[others, pl.ds(BLOCK, HEAD)], r.grad_sem.at[1])

    @pl.loop(0, n_here)
    def _(b):
        rows = aligned(b * BLOCK, BLOCK)
        for pair in range(PAIRS):
            j = b * HEADS + 2 * pair
            at = 2 * WIDTH + pair * 2 * HEAD
            grad = jnp.transpose(
                jnp.concatenate([r.grad_got[j + e, BLOCK:].astype(F32) for e in range(2)], axis=0)
            )
            slope = r.slope[b, :, at:at + 2 * HEAD].astype(F32)
            r.d_pre[rows, at:at + 2 * HEAD] = (grad * slope).astype(BF16)

    late[2].pack(dot_nn(r.xnt[...], r.d_pre[:, 2 * WIDTH:3 * WIDTH]))
    late[2].scatter()
    for one in early:
        one.gather()
    for one in late:
        one.plane()
    for one in early:
        one.spread()
    for one in late:
        one.gather()
    for one in late:
        one.spread()

    for one in early + late:
        one.finish()

    await_bytes(r.first, r.send_sem.at[1])
    await_bytes(r.ids, r.send_sem.at[2])
    for at in (3, 5, 8):
        await_bytes(r.negs.at[0], r.send_sem.at[at])
        await_bytes(r.all_ids.at[0], r.send_sem.at[at + 1])
    await_bytes(r.att_send.at[others], r.send_sem.at[7])
    await_bytes(r.datt_send.at[others], r.send_sem.at[12])
    await_bytes(r.grad_send.at[others, pl.ds(0, BLOCK)], r.send_sem.at[10])
    await_bytes(r.grad_send.at[others, pl.ds(BLOCK, HEAD)], r.send_sem.at[11])
    await_bytes(r.loss, r.loss_sem.at[0])
    for at in range(3):
        await_bytes(r.loss_all.at[at, pl.ds(0, 3)], r.loss_sem.at[2 + 2 * at])


def activated(r, b, xn, part):
    half = 0.5 * dot_nn(xn, r.w_joined[:, part * WIDTH:(part + 1) * WIDTH])
    th = jnp.tanh(half)
    slope = (0.5 + 0.5 * th) * (1.0 + half * (1.0 - th))
    r.slope[b, :, part * WIDTH:(part + 1) * WIDTH] = slope.astype(BF16)
    return half + half * th


def middle(r, n_seq, me, grp, first_b, weight):
    both = 2
    rows = both * BLOCK
    n_here = r.x.shape[0]
    n_grp, n_neg = r.negs.shape[:2]

    def joined(make):
        return jnp.concatenate([make(e) for e in range(both)], axis=0)

    @pl.loop(0, both * HEADS)
    def _(turn):
        j = first_b * HEADS + turn

        @pl.when(j != me)
        def _():
            await_bytes(r.att_got.at[0], r.att_sem.at[j])

    for e in range(both):
        for pair in range(PAIRS):
            j = (first_b + e) * HEADS + 2 * pair
            top, bottom = swapped(r.att_got[j].astype(F32), r.att_got[j + 1].astype(F32))
            r.att[e * BLOCK:e * BLOCK + HEAD, pair_cols(pair)] = top
            r.att[e * BLOCK + HEAD:(e + 1) * BLOCK, pair_cols(pair)] = bottom

    att = r.att[...]
    centered = att - jnp.mean(att, axis=-1, keepdims=True)
    inv_att = lax.rsqrt(jnp.mean(centered * centered, axis=-1, keepdims=True) + eps_norm)
    normed = centered * inv_att
    u = joined(lambda e: r.u[first_b + e]).astype(F32)
    gated = (normed * u).astype(BF16)
    x = joined(lambda e: r.x[first_b + e]).astype(F32)
    out_rows = x + dot_nn(gated, r.w_out[...])
    inv_y = lax.rsqrt(jnp.sum(out_rows * out_rows, axis=-1, keepdims=True) + eps_norm)
    unit_y = out_rows * inv_y
    unit_b = unit_y.astype(BF16)
    more = jnp.where(me == n_seq - 1, 0, 1)
    last_row = lax.broadcasted_iota(jnp.int32, (BLOCK, WIDTH), 0) == BLOCK - 1
    last_lane = lax.broadcasted_iota(jnp.int32, (1, BLOCK), 1) == BLOCK - 1

    def next_rows(e):
        shifted = pltpu.roll(r.x[first_b + e].astype(F32), BLOCK - 1, axis=0)
        return jnp.where(last_row, r.first[first_b + e].astype(F32)[:1] * more.astype(F32), shifted)

    x_next = joined(next_rows)
    pos_unit = (
        x_next * lax.rsqrt(jnp.sum(x_next * x_next, axis=-1, keepdims=True) + eps_norm)
    ).astype(BF16).astype(F32)
    pos_logit = logit_scale * jnp.sum(unit_b.astype(F32) * pos_unit, axis=-1, keepdims=True)

    def row_ids(e):
        shifted = pltpu.roll(r.ids[pl.ds(first_b + e, 1)], BLOCK - 1, axis=1)
        coming = pltpu.roll(r.next_ids[pl.ds(first_b + e, 1)], BLOCK - 1, axis=1) * more
        return jnp.transpose(jnp.broadcast_to(jnp.where(last_lane, coming, shifted), (BLOCK, BLOCK)))

    ids = joined(row_ids)
    lane_sum = jnp.zeros((rows, BLOCK), F32)
    for g in range(n_grp):
        neg_logit = logit_scale * dot_nt(unit_b, r.negs[g])
        for sub in range(n_neg // BLOCK):
            at = (g * n_neg) + sub * BLOCK
            hit = r.all_ids[g, n_here + sub:n_here + sub + 1] == ids
            exps = jnp.where(hit, 0.0, jnp.exp(neg_logit[:, sub * BLOCK:(sub + 1) * BLOCK]))
            r.exps[:, at:at + BLOCK] = exps
            lane_sum = lane_sum + exps
    pos_exp = jnp.exp(pos_logit)
    denom = pos_exp + jnp.sum(lane_sum, axis=-1, keepdims=True)

    def row_valid(e):
        pos = me * BLOCK + lax.broadcasted_iota(jnp.int32, (BLOCK, 1), 0)
        return jnp.where(pos + 1 < r.lens[grp * n_here + first_b + e], 1.0, 0.0)

    valid = joined(row_valid)
    row_loss = jnp.where(valid > 0.0, jnp.log(denom) - pos_logit, 0.0)
    r.loss[...] += jnp.broadcast_to(jnp.sum(row_loss, axis=0, keepdims=True), r.loss.shape)
    row_weight = valid * weight
    d_pos = row_weight * (pos_exp / denom - 1.0)
    scale = row_weight / denom
    neg_back = jnp.zeros((rows, WIDTH), F32)
    for g in range(n_grp):
        d_neg = (scale * r.exps[:, g * n_neg:(g + 1) * n_neg]).astype(BF16)
        neg_back = neg_back + dot_nn(d_neg, r.negs[g])
    d_unit = logit_scale * (d_pos * pos_unit + neg_back)
    d_out = (
        (d_unit - unit_y * jnp.sum(unit_y * d_unit, axis=-1, keepdims=True)) * inv_y
    ).astype(BF16)
    d_gate = dot_nt(d_out, r.w_out[...])
    d_norm = d_gate * u
    d_att = inv_att * (
        d_norm
        - jnp.mean(d_norm, axis=-1, keepdims=True)
        - normed * jnp.mean(d_norm * normed, axis=-1, keepdims=True)
    )
    for e in range(both):
        rows_e = d_att[e * BLOCK:(e + 1) * BLOCK]
        for pair in range(PAIRS):
            cols = pair_cols(pair)
            packed = swapped(rows_e[:HEAD, cols], rows_e[HEAD:, cols])
            for odd in range(2):
                r.datt_send[(first_b + e) * HEADS + 2 * pair + odd] = packed[odd].astype(BF16)

    @pl.loop(0, both * HEADS)
    def _(turn):
        j = first_b * HEADS + lax.rem(me + turn, both * HEADS)

        @pl.when(j != me)
        def _():
            copy_to(
                r.datt_send.at[j], r.datt_got.at[me], r.send_sem.at[12], r.datt_sem.at[me], {"seq": j}
            )

        @pl.when(j == me)
        def _():
            r.datt_got[me] = r.datt_send[me]

    r.grad_out[...] += dot_tn(gated, d_out)
    d_u = d_gate * normed
    for e in range(both):
        slope = r.slope[first_b + e, :, :WIDTH].astype(F32)
        r.d_pre[aligned((first_b + e) * BLOCK, BLOCK), :WIDTH] = (
            d_u[e * BLOCK:(e + 1) * BLOCK] * slope
        ).astype(BF16)


def widen(*refs):
    *blocks, joined, out = refs
    for at, block in enumerate(blocks):
        for half in range(4):
            values = block[half // 2, 0, half % 2].reshape(HEAD, BLOCK).astype(F32)
            if at < 4:
                joined[:, at * WIDTH + half * BLOCK:at * WIDTH + (half + 1) * BLOCK] = values
            else:
                out[:, half * BLOCK:(half + 1) * BLOCK] = values


def local(inputs, history, lengths, w_joined, w_out, neg_emb, neg_ids):
    n_here, block, width = inputs.shape
    n_seq = lax.axis_size("seq")
    length = n_seq * block
    lanes = 2 * HEAD
    rows = n_here * block
    n_neg = neg_emb.shape[0]
    dma = pltpu.SemaphoreType.DMA
    buffers = dict(
        xn=((n_here, block, width), BF16), xnt=((width, rows), BF16), u=((n_here, block, width), BF16),
        slope=((n_here, block, 4 * width), BF16), d_pre=((rows, 4 * width), BF16),
        send=((n_seq, BLOCK + HEAD, lanes), BF16), got=((n_seq, BLOCK + HEAD, lanes), BF16),
        att_send=((n_seq, HEAD, lanes), BF16), att_got=((n_seq, HEAD, lanes), BF16),
        datt_send=((n_seq, HEAD, lanes), BF16), datt_got=((n_seq, HEAD, lanes), BF16),
        grad_send=((n_seq, BLOCK + HEAD, lanes), BF16), grad_got=((n_seq, BLOCK + HEAD, lanes), BF16),
        first=((n_here, 16, width), BF16), ids=((2 * n_here, block), jnp.int32),
        next_ids=((2 * n_here, block), jnp.int32), negs=((4, n_neg, width), BF16),
        all_ids=((4, 2 * n_here, block), jnp.int32),
        kv0=((length // TILE, 2 * TILE, lanes), BF16), qa=((length, lanes), BF16),
        kt=((HEAD, length), BF16), acc=((FQ, lanes), F32), dq=((HEAD, length), F32), dkv=((BM, lanes), F32),
        att=((2 * block, width), F32), exps=((2 * block, 4 * n_neg), F32), grad_out=((width, width), F32),
        loss=((8, block), F32), loss_core=((8, block), F32), loss_sum=((3, 8, block), F32),
        loss_all=((3, 4, 8, block), F32), x=((n_here, block, width), BF16),
        w_joined=((width, 4 * width), BF16), w_out=((width, width), BF16), neg_emb=((n_neg, width), BF16),
        history=((n_here, block), jnp.int32), neg_ids=((n_here, block), jnp.int32),
    )
    wide = (8, 16, 16, block)
    for name in "uovkq":
        buffers[name + "_part"] = buffers[name + "_got"] = (wide, BF16)
        buffers[name + "_sum"] = buffers[name + "_got2"] = (wide[1:], BF16)
        buffers[name + "_red"] = (wide[2:], BF16)
    sems = dict(
        send_sem=13, one_sem=8, got_sem=n_seq, att_sem=n_seq, datt_sem=n_seq, grad_sem=2, loss_sem=8,
        red_send=20, red_recv=20, load_sem=6,
    )
    takes = ("lens", "x_in", "history_in", "neg_ids_in", "w_joined_in", "w_out_in", "neg_emb_in")
    gives = {name + "_full": (wide, BF16) for name in "uvqko"}
    gives["loss_out"] = ((1,), F32)
    names = takes + tuple(gives) + tuple(buffers) + tuple(sems)
    *grads, loss = pl.pallas_call(
        functools.partial(kernel, n_seq, names),
        out_shape=[jax.ShapeDtypeStruct(*kind) for kind in gives.values()],
        in_specs=[SMEM] + [pl.BlockSpec(memory_space=pl.ANY)] * (len(takes) - 1),
        out_specs=[VMEM] * 5 + [SMEM],
        scratch_shapes=[pltpu.VMEM(*kind) for kind in buffers.values()]
        + [dma((count,)) for count in sems.values()],
        compiler_params=pltpu.CompilerParams(
            collective_id=0, has_side_effects=True, vmem_limit_bytes=60 * 1024 * 1024
        ),
    )(lengths, inputs, history, neg_ids.reshape(-1, block), w_joined, w_out, neg_emb)
    taken = pl.BlockSpec((2, 1, 2, 4, 16, block), lambda at: (0, at // 2, 0, at % 2, 0, 0))
    joined, out = pl.pallas_call(
        widen,
        grid=(8,),
        out_shape=[
            jax.ShapeDtypeStruct((width, 4 * width), F32), jax.ShapeDtypeStruct((width, width), F32)
        ],
        in_specs=[taken] * 5,
        out_specs=[
            pl.BlockSpec((width // 8, 4 * width), lambda at: (at, 0)),
            pl.BlockSpec((width // 8, width), lambda at: (at, 0)),
        ],
        compiler_params=pltpu.CompilerParams(vmem_limit_bytes=60 * 1024 * 1024),
    )(*(grad.reshape((2, 4, 2, 8) + wide[2:]) for grad in grads))
    return (joined, out, loss.reshape(()))


def solution(mesh):
    placed = (
        P("grp", "seq", None),
        P("grp", "seq"),
        P(),
        P(),
        P(),
        P(("grp", "seq"), None),
        P(("grp", "seq")),
    )
    return jax.shard_map(
        local, mesh=mesh, in_specs=placed, out_specs=(P(), P(), P()), check_vma=False
    )
```

```python
import functools
import types

import jax
import jax.numpy as jnp
from jax import lax
from jax.experimental import pallas as pl
from jax.experimental.pallas import tpu as pltpu
from jax.sharding import PartitionSpec as P

HEADS = 8
HEAD = 64
WIDTH = 512
PAIRS = 4
BLOCK = 128
TILE = 512
FQ = TILE
BM = TILE
eps_norm = 1e-06
logit_scale = 64.0

MESH = pl.DeviceIdType.MESH
F32 = jnp.float32
BF16 = jnp.bfloat16
VMEM = pl.BlockSpec(memory_space=pltpu.VMEM)
SMEM = pl.BlockSpec(memory_space=pltpu.SMEM)


def dot_nn(a, b):
    return lax.dot_general(a, b, (((1,), (0,)), ((), ())), preferred_element_type=F32)


def dot_nt(a, b):
    return lax.dot_general(a, b, (((1,), (1,)), ((), ())), preferred_element_type=F32)


def dot_tn(a, b):
    return lax.dot_general(a, b, (((0,), (0,)), ((), ())), preferred_element_type=F32)


def low_lanes(shape):
    return lax.broadcasted_iota(jnp.int32, shape, 1) < HEAD


def turned(a):
    return pltpu.roll(a, HEAD, axis=1)


def swapped(a, b):
    low = low_lanes(a.shape)
    return jnp.where(low, a, turned(b)), jnp.where(low, turned(a), b)


def copy_to(src, dst, send_sem, recv_sem, where):
    pltpu.make_async_remote_copy(
        src_ref=src, dst_ref=dst, send_sem=send_sem, recv_sem=recv_sem,
        device_id=where, device_id_type=MESH,
    ).start()


def await_bytes(ref, sem):
    pltpu.make_async_copy(ref, ref, sem).wait()


def aligned(at, size):
    return pl.ds(pl.multiple_of(at, size), size)


def pair_cols(pair):
    return slice(pair * 2 * HEAD, (pair + 1) * 2 * HEAD)


def shifts(n_seq):
    side = int((n_seq // 2) ** 0.5)
    steps = [(x, y, z) for x in range(side) for y in range(side) for z in range(2)]
    return sorted(steps[1:], key=lambda at: -(min(at[0], side - at[0]) + min(at[1], side - at[1]) + at[2]))


def peer(me, shift):
    x, y, z = me // HEADS, lax.rem(me // 2, 4), lax.rem(me, 2)
    return (lax.rem(x + shift[0], 4) * 4 + lax.rem(y + shift[1], 4)) * 2 + lax.rem(z + shift[2], 2)


def cover(first, count, body):
    done = 0
    for tiles in (4, 2):
        n = count // tiles if tiles == 4 else lax.rem(count // tiles, 2)

        @pl.loop(0, n)
        def _(at, done=done, tiles=tiles):
            body(first + done + at * tiles, tiles)

        done = done + n * tiles


def tile_at(first, step, tiles):
    low = lax.rem(first + step // 2, tiles // 2)
    odd = lax.rem(step, 2)
    return low + odd * (tiles - 1 - 2 * low)


def kernel(n_seq, names, *refs):
    r = types.SimpleNamespace(**dict(zip(names, refs, strict=True)))
    me = lax.axis_index("seq")
    grp = lax.axis_index("grp")
    core, z_hi = lax.rem(grp, 2), grp // 2
    loads = [
        pltpu.make_async_copy(getattr(r, name + "_in"), getattr(r, name), r.load_sem.at[at])
        for at, name in enumerate(("x", "w_joined", "history", "neg_ids", "neg_emb", "w_out"))
    ]
    for load in loads:
        load.start()
    n_here = r.x.shape[0]
    planes = n_seq // HEADS
    length = n_seq * BLOCK
    mate = {"grp": grp + 1 - 2 * core}
    other_z = {"grp": (1 - z_hi) * 2 + core}
    others = pl.ds(0, n_seq - 1)
    x_at, y_at, z_at = me // HEADS, lax.rem(me // 2, 4), z_hi * 2 + lax.rem(me, 2)

    barrier = pltpu.get_barrier_semaphore()

    def greet(where):
        pl.semaphore_signal(barrier, inc=1, device_id=where, device_id_type=MESH)

    greet(mate)

    @pl.loop(1, n_seq)
    def _(step):
        greet({"seq": lax.rem(me + step, n_seq)})

    for step in range(4):
        for z in range(2):
            greet(dict(other_z, seq=(x_at * 4 + lax.rem(y_at + step, 4)) * 2 + z))
            if step:
                greet(dict(other_z, seq=(lax.rem(x_at + step, 4) * 4 + y_at) * 2 + z))

    def lane(axis, along):
        x, y, z = (along if axis == name else at for name, at in (("x", x_at), ("y", y_at), ("z", z_at)))
        return {"grp": z // 2 * 2 + 1 - core, "seq": (x * 4 + y) * 2 + lax.rem(z, 2)}

    for axis, at in (("x", x_at), ("y", y_at), ("z", z_at)):
        for step in range(1, 4):
            greet(lane(axis, lax.rem(at + step, 4)))
    n_peers = n_seq + 14 + 9

    loads[0].wait()
    loads[1].wait()

    @pl.loop(0, n_here)
    def _(b):
        x = r.x[b].astype(F32)
        centered = x - jnp.mean(x, axis=-1, keepdims=True)
        var = jnp.mean(centered * centered, axis=-1, keepdims=True)
        xn = (centered * lax.rsqrt(var + eps_norm)).astype(BF16)
        r.xn[b] = xn
        v, q, k = (activated(r, b, xn, part) for part in (1, 2, 3))
        for pair in range(PAIRS):
            cols = pair_cols(pair)
            kv = swapped(k[:, cols], v[:, cols])
            qs = swapped(q[:HEAD, cols], q[HEAD:, cols])
            for odd in range(2):
                j = b * HEADS + 2 * pair + odd
                r.send[j, :BLOCK] = kv[odd].astype(BF16)
                r.send[j, BLOCK:] = qs[odd].astype(BF16)

    pl.semaphore_wait(barrier, n_peers)
    for shift in shifts(n_seq):
        j = peer(me, shift)
        copy_to(r.send.at[j], r.got.at[me], r.send_sem.at[0], r.got_sem.at[me], {"seq": j})
    r.got[me] = r.send[me]

    before = {"seq": lax.rem(me + n_seq - 1, n_seq)}
    loads[2].wait()
    loads[3].wait()
    r.ids[:n_here] = r.history[...]
    r.ids[n_here:] = r.neg_ids[...]
    copy_to(r.x.at[:, pl.ds(0, 16)], r.first, r.send_sem.at[1], r.one_sem.at[0], before)
    copy_to(r.ids, r.next_ids, r.send_sem.at[2], r.one_sem.at[1], before)

    loads[4].wait()
    loads[5].wait()

    @pl.loop(0, n_here)
    def _(b):
        xn = r.xn[b]
        r.u[b] = activated(r, b, xn, 0).astype(BF16)
        r.xnt[:, aligned(b * BLOCK, BLOCK)] = jnp.transpose(xn.astype(F32)).astype(BF16)
        rows = aligned(b * BLOCK, BLOCK)
        emb = r.neg_emb[rows].astype(F32)
        r.negs[grp, rows] = (
            emb * lax.rsqrt(jnp.sum(emb * emb, axis=-1, keepdims=True) + eps_norm)
        ).astype(BF16)

    r.all_ids[grp] = r.ids[...]

    seq_len = r.lens[grp * n_here + me // HEADS]
    low = low_lanes((HEAD, 2 * HEAD))
    low_block = low_lanes((BLOCK, 2 * HEAD))

    @pl.loop(0, planes)
    def _(step):
        first = lax.rem(me // HEADS + planes // 2 + step, planes) * HEADS

        @pl.loop(0, HEADS)
        def _(turn):
            i = first + turn

            @pl.when(i != me)
            def _():
                await_bytes(r.got.at[0], r.got_sem.at[i])

        @pl.loop(0, HEADS, unroll=4)
        def _(turn):
            i = first + turn
            rows = aligned(i * BLOCK, BLOCK)
            pos = i * BLOCK + lax.broadcasted_iota(jnp.int32, (BLOCK, 2 * HEAD), 0)
            kv = jnp.where(pos < seq_len, r.got[i, :BLOCK].astype(F32), 0.0)
            tile, at = i // (TILE // BLOCK), lax.rem(i, TILE // BLOCK) * BLOCK
            r.kv0[tile, aligned(at, BLOCK)] = jnp.where(low_block, 0.5 * kv, 0.0).astype(BF16)
            r.kv0[tile, aligned(TILE + at, BLOCK)] = jnp.where(low_block, 0.0, kv).astype(BF16)
            r.kt[:, rows] = jnp.transpose(kv)[:HEAD].astype(BF16)
            q = r.got[i, BLOCK:].astype(F32)
            r.qa[rows] = jnp.concatenate(
                [jnp.where(low, q, 0.0), jnp.where(low, turned(q), 0.0)], axis=0
            ).astype(BF16)

    copy_to(r.negs.at[grp], r.negs.at[grp], r.send_sem.at[3], r.one_sem.at[2], mate)
    copy_to(r.all_ids.at[grp], r.all_ids.at[grp], r.send_sem.at[4], r.one_sem.at[3], mate)
    copy_to(r.negs.at[grp], r.negs.at[grp], r.send_sem.at[5], r.one_sem.at[4], other_z)
    copy_to(r.all_ids.at[grp], r.all_ids.at[grp], r.send_sem.at[6], r.one_sem.at[5], other_z)
    await_bytes(r.send.at[others], r.send_sem.at[0])
    inv_len = 1.0 / jnp.full((1, 2 * HEAD), seq_len, jnp.int32).astype(F32)

    f_tiles = length // FQ
    f_per = FQ // BLOCK

    @pl.loop(0, f_tiles)
    def _(step):
        c = tile_at(me // f_per, step, f_tiles)
        q = r.qa[aligned(c * FQ, FQ)]

        def piece(start, size, masked):
            rows = pl.ds(start, size)
            size = size * TILE
            half = dot_nt(q, r.kv0[rows, :TILE].reshape(size, 2 * HEAD))
            if masked:
                ahead = lax.broadcasted_iota(jnp.int32, (FQ, size), 1) - lax.broadcasted_iota(
                    jnp.int32, (FQ, size), 0
                )
                half = jnp.where(ahead <= size - FQ, half, 0.0)
            probs = (half + half * jnp.tanh(half)).astype(BF16)
            return dot_nn(probs, r.kv0[rows, TILE:].reshape(size, 2 * HEAD))

        odd = lax.rem(c, 2)

        @pl.when(odd == 0)
        def _():
            r.acc[...] = piece(c, 1, True)

        @pl.when(odd == 1)
        def _():
            r.acc[...] = piece(c - 1, 2, True)

        def more(start, size):
            r.acc[...] += piece(start, size, False)

        cover(0, c - odd, more)
        for u in range(f_per):
            out = r.acc[u * BLOCK:(u + 1) * BLOCK] * inv_len
            top, bottom = out[:HEAD], out[HEAD:]
            r.att_send[c * f_per + u] = jnp.where(low, turned(top), bottom).astype(BF16)

        @pl.loop(0, f_per)
        def _(turn):
            i = c * f_per + lax.rem(me + turn, f_per)

            @pl.when(i != me)
            def _():
                copy_to(
                    r.att_send.at[i], r.att_got.at[me], r.send_sem.at[7], r.att_sem.at[me], {"seq": i}
                )

            @pl.when(i == me)
            def _():
                r.att_got[me] = r.att_send[me]

    far = (1 - z_hi) * 2 + core
    await_bytes(r.negs.at[0], r.one_sem.at[4])
    await_bytes(r.all_ids.at[0], r.one_sem.at[5])
    copy_to(r.negs.at[far], r.negs.at[far], r.send_sem.at[8], r.one_sem.at[6], mate)
    copy_to(r.all_ids.at[far], r.all_ids.at[far], r.send_sem.at[9], r.one_sem.at[7], mate)

    total = r.lens[0] - 1
    for at in range(1, r.lens.shape[0]):
        total = total + (r.lens[at] - 1)
    both = 2
    half_rows = both * BLOCK
    weight = 1.0 / jnp.full((half_rows, 1), total, jnp.int32).astype(F32)
    r.grad_out[...] = jnp.zeros_like(r.grad_out)
    r.loss[...] = jnp.zeros_like(r.loss)
    await_bytes(r.first, r.one_sem.at[0])
    await_bytes(r.ids, r.one_sem.at[1])
    await_bytes(r.negs.at[0], r.one_sem.at[2])
    await_bytes(r.all_ids.at[0], r.one_sem.at[3])
    await_bytes(r.negs.at[0], r.one_sem.at[6])
    await_bytes(r.all_ids.at[0], r.one_sem.at[7])
    n_halves = n_here // both

    @pl.loop(0, n_halves)
    def _(step):
        middle(r, n_seq, me, grp, both * lax.rem(me // (both * HEADS) + step, n_halves), weight)

    axes = dict(x=x_at, y=y_at, z=z_at)
    plane_at = dict(x=y_at * 4 + z_at, y=x_at * 4 + z_at, z=x_at * 4 + y_at)

    def chip(axis, along, across, of_core=core):
        hi, lo = across // 4, lax.rem(across, 4)
        x, y, z = dict(x=(along, hi, lo), y=(hi, along, lo), z=(hi, lo, along))[axis]
        return {"grp": z // 2 * 2 + of_core, "seq": (x * 4 + y) * 2 + lax.rem(z, 2)}

    def reduction(name, axis, at):
        part, got, sums, got2, red, full = (
            getattr(r, name + tail) for tail in ("_part", "_got", "_sum", "_got2", "_red", "_full")
        )
        send = [r.red_send.at[at * 4 + k] for k in range(4)]
        recv = [r.red_recv.at[at * 4 + k] for k in range(4)]
        along, across = axes[axis], plane_at[axis]
        mine = core * 4 + along
        seven, fifteen = pl.ds(0, 7), pl.ds(0, 15)

        def along_axis(source, target, sems):
            @pl.loop(1, 8, unroll=7)
            def _(step):
                to = lax.rem(mine + step, 8)
                copy_to(source(to), target, *sems, chip(axis, lax.rem(to, 4), across, to // 4))

        def over_plane(source, target, sems):
            @pl.loop(1, 16, unroll=5)
            def _(step):
                to = lax.rem(across + step, 16)
                copy_to(source(to), target, *sems, chip(axis, along, to))

        def pack(grad):
            for half in range(4):
                block = grad[:, half * BLOCK:(half + 1) * BLOCK].astype(BF16)
                low, first = half % 2 * 8, half // 2 * 4
                part[first:first + 4, low:low + 8] = block.reshape(4, 8, 16, BLOCK)

        def scatter():
            along_axis(lambda to: part.at[to], got.at[mine], (send[0], recv[0]))

        def plane():
            got[mine] = part[mine]
            await_bytes(got.at[seven], recv[0])
            sums[...] = jnp.sum(got[...].astype(F32), axis=0).astype(BF16)
            over_plane(lambda to: sums.at[to], got2.at[across], (send[1], recv[1]))

        def gather():
            got2[across] = sums[across]
            await_bytes(got2.at[fifteen], recv[1])
            red[...] = jnp.sum(got2[...].astype(F32), axis=0).astype(BF16)
            full[mine, across] = red[...]
            over_plane(lambda to: red, full.at[mine, across], (send[2], recv[2]))

        def spread():
            await_bytes(got2.at[fifteen], recv[2])
            along_axis(lambda to: full.at[mine], full.at[mine], (send[3], recv[3]))

        def finish():
            await_bytes(got.at[seven], recv[3])
            await_bytes(got.at[seven], send[0])
            await_bytes(got2.at[fifteen], send[1])
            await_bytes(got2.at[fifteen], send[2])
            await_bytes(got.at[seven], send[3])

        return types.SimpleNamespace(
            pack=pack, scatter=scatter, plane=plane, gather=gather, spread=spread, finish=finish)

    early = [reduction("u", "x", 0), reduction("o", "y", 1)]
    early[0].pack(dot_nn(r.xnt[...], r.d_pre[:, :WIDTH]))
    early[1].pack(r.grad_out[...])
    copy_to(r.loss, r.loss_core, r.loss_sem.at[0], r.loss_sem.at[1], mate)

    def loss_along(axis, value, at):
        r.loss_all[at, axes[axis]] = value
        r.loss_sum[at] = value
        for step in range(1, 4):
            copy_to(
                r.loss_sum.at[at], r.loss_all.at[at, axes[axis]],
                r.loss_sem.at[2 + 2 * at], r.loss_sem.at[3 + 2 * at],
                chip(axis, lax.rem(axes[axis] + step, 4), plane_at[axis]),
            )

    def loss_over(at):
        await_bytes(r.loss_all.at[at, pl.ds(0, 3)], r.loss_sem.at[3 + 2 * at])
        return jnp.sum(r.loss_all[at], axis=0)

    @pl.loop(0, n_seq)
    def _(step):
        i = lax.rem(me + step, n_seq)

        @pl.when(i != me)
        def _():
            await_bytes(r.datt_got.at[0], r.datt_sem.at[i])

    @pl.loop(0, n_seq, unroll=4)
    def _(i):
        d_att = r.datt_got[i].astype(F32)
        rows = aligned(i * BLOCK, BLOCK)
        qa = r.qa[rows].astype(F32)
        r.qa[rows] = jnp.where(
            low_block, qa, jnp.concatenate([turned(d_att), d_att], axis=0)
        ).astype(BF16)

    early[0].scatter()
    early[1].scatter()

    r.dq[...] = jnp.zeros_like(r.dq)
    b_tiles = length // BM
    b_per = BM // BLOCK
    kv_scale = jnp.where(low_lanes((1, 2 * HEAD)), 0.5 * inv_len, inv_len)

    def send_d_q(low, high):
        @pl.loop(low, high)
        def _(c):
            for u in range(b_per):
                d_q = r.dq[:, aligned((c * b_per + u) * BLOCK, BLOCK)] * (0.5 * inv_len)
                r.grad_send[c * b_per + u, BLOCK:] = d_q.astype(BF16)

            @pl.loop(0, b_per)
            def _(turn):
                i = c * b_per + lax.rem(me + turn, b_per)

                @pl.when(i != me)
                def _():
                    copy_to(
                        r.grad_send.at[i, pl.ds(BLOCK, HEAD)], r.grad_got.at[me, pl.ds(BLOCK, HEAD)],
                        r.send_sem.at[11], r.grad_sem.at[1], {"seq": i},
                    )

                @pl.when(i == me)
                def _():
                    r.grad_got[me, BLOCK:] = r.grad_send[me, BLOCK:]

    @pl.loop(0, b_tiles)
    def _(step):
        c = tile_at(me // b_per, step, b_tiles)
        m_rows = aligned(c * BM, BM)
        low_tile = low_lanes((BM, 2 * HEAD))

        def piece(start, size, masked):
            size = size * TILE
            t_rows = pl.ds(pl.multiple_of(start * TILE, TILE), size)
            qa = r.qa[t_rows]
            products = dot_nt(r.kv0[c], qa)
            half, d_probs = products[:TILE], products[TILE:]
            if masked:
                ahead = lax.broadcasted_iota(jnp.int32, (BM, size), 0) - lax.broadcasted_iota(
                    jnp.int32, (BM, size), 1
                )
                half = jnp.where(ahead <= 0, half, 0.0)
                d_probs = jnp.where(ahead <= 0, d_probs, 0.0)
            th = jnp.tanh(half)
            up = 1.0 + th
            probs = half * up
            d_scores = (d_probs * up * (1.0 + half * (1.0 - th))).astype(BF16)
            r.dq[:, t_rows] += dot_nn(r.kt[:, m_rows], d_scores)
            return jnp.where(low_tile, dot_nn(d_scores, qa), dot_nn(probs.astype(BF16), qa))

        odd = lax.rem(b_tiles - 1 - c, 2)

        @pl.when(odd == 0)
        def _():
            r.dkv[...] = piece(c, 1, True)

        @pl.when(odd == 1)
        def _():
            r.dkv[...] = piece(c, 2, True)

        def more(start, size):
            r.dkv[...] += piece(start, size, False)

        cover(c + 1 + odd, b_tiles - 1 - c - odd, more)
        for u in range(b_per):
            r.grad_send[c * b_per + u, :BLOCK] = (
                r.dkv[u * BLOCK:(u + 1) * BLOCK] * kv_scale
            ).astype(BF16)

        @pl.loop(0, b_per)
        def _(turn):
            i = c * b_per + lax.rem(me + turn, b_per)

            @pl.when(i != me)
            def _():
                copy_to(
                    r.grad_send.at[i, pl.ds(0, BLOCK)], r.grad_got.at[me, pl.ds(0, BLOCK)],
                    r.send_sem.at[10], r.grad_sem.at[0], {"seq": i},
                )

            @pl.when(i == me)
            def _():
                r.grad_got[me, :BLOCK] = r.grad_send[me, :BLOCK]

        for at, stage in enumerate(("plane", "gather", "spread", "")):
            @pl.when(step == 2 * at + 1)
            def _(at=at, stage=stage):
                if stage:
                    for one in early:
                        getattr(one, stage)()
                if at == 0:
                    await_bytes(r.loss_core, r.loss_sem.at[1])
                    loss_along("x", r.loss[...] + r.loss_core[...], 0)
                if at == 1:
                    loss_along("y", loss_over(0), 1)
                if at == 2:
                    loss_along("z", loss_over(1), 2)
                if at == 3:
                    count = jnp.full((8, BLOCK), total, jnp.int32).astype(F32)
                    r.loss_out[0] = (loss_over(2) / count)[0, 0]

        end = tile_at(me // b_per, b_tiles - 1, b_tiles)

        @pl.when(step == b_tiles - 2)
        def _():
            send_d_q(0, end)

        @pl.when(step == b_tiles - 1)
        def _():
            send_d_q(end, b_tiles)

    late = [reduction("v", "x", 2), reduction("k", "y", 3), reduction("q", "z", 4)]
    await_bytes(r.grad_got.at[others, pl.ds(0, BLOCK)], r.grad_sem.at[0])

    @pl.loop(0, n_here)
    def _(b):
        rows = aligned(b * BLOCK, BLOCK)
        for pair in range(PAIRS):
            j = b * HEADS + 2 * pair
            d_k, d_v = swapped(r.grad_got[j, :BLOCK].astype(F32), r.grad_got[j + 1, :BLOCK].astype(F32))
            for part, grad in ((1, d_v), (3, d_k)):
                at = part * WIDTH + pair * 2 * HEAD
                slope = r.slope[b, :, at:at + 2 * HEAD].astype(F32)
                r.d_pre[rows, at:at + 2 * HEAD] = (grad * slope).astype(BF16)

    late[0].pack(dot_nn(r.xnt[...], r.d_pre[:, WIDTH:2 * WIDTH]))
    late[0].scatter()
    late[1].pack(dot_nn(r.xnt[...], r.d_pre[:, 3 * WIDTH:]))
    late[1].scatter()
    await_bytes(r.grad_got.at[others, pl.ds(BLOCK, HEAD)], r.grad_sem.at[1])

    @pl.loop(0, n_here)
    def _(b):
        rows = aligned(b * BLOCK, BLOCK)
        for pair in range(PAIRS):
            j = b * HEADS + 2 * pair
            at = 2 * WIDTH + pair * 2 * HEAD
            grad = jnp.transpose(
                jnp.concatenate([r.grad_got[j + e, BLOCK:].astype(F32) for e in range(2)], axis=0)
            )
            slope = r.slope[b, :, at:at + 2 * HEAD].astype(F32)
            r.d_pre[rows, at:at + 2 * HEAD] = (grad * slope).astype(BF16)

    late[2].pack(dot_nn(r.xnt[...], r.d_pre[:, 2 * WIDTH:3 * WIDTH]))
    late[2].scatter()
    for stage in ("plane", "gather", "spread"):
        for one in late:
            getattr(one, stage)()

    for one in early + late:
        one.finish()

    await_bytes(r.first, r.send_sem.at[1])
    await_bytes(r.ids, r.send_sem.at[2])
    for at in (3, 5, 8):
        await_bytes(r.negs.at[0], r.send_sem.at[at])
        await_bytes(r.all_ids.at[0], r.send_sem.at[at + 1])
    await_bytes(r.att_send.at[others], r.send_sem.at[7])
    await_bytes(r.datt_send.at[others], r.send_sem.at[12])
    await_bytes(r.grad_send.at[others, pl.ds(0, BLOCK)], r.send_sem.at[10])
    await_bytes(r.grad_send.at[others, pl.ds(BLOCK, HEAD)], r.send_sem.at[11])
    await_bytes(r.loss, r.loss_sem.at[0])
    for at in range(3):
        await_bytes(r.loss_all.at[at, pl.ds(0, 3)], r.loss_sem.at[2 + 2 * at])


def activated(r, b, xn, part):
    half = 0.5 * dot_nn(xn, r.w_joined[:, part * WIDTH:(part + 1) * WIDTH])
    th = jnp.tanh(half)
    slope = (0.5 + 0.5 * th) * (1.0 + half * (1.0 - th))
    r.slope[b, :, part * WIDTH:(part + 1) * WIDTH] = slope.astype(BF16)
    return half + half * th


def middle(r, n_seq, me, grp, first_b, weight):
    both = 2
    rows = both * BLOCK
    n_here = r.x.shape[0]
    n_grp, n_neg = r.negs.shape[:2]

    def joined(make):
        return jnp.concatenate([make(e) for e in range(both)], axis=0)

    @pl.loop(0, both * HEADS)
    def _(turn):
        j = first_b * HEADS + turn

        @pl.when(j != me)
        def _():
            await_bytes(r.att_got.at[0], r.att_sem.at[j])

    for e in range(both):
        for pair in range(PAIRS):
            j = (first_b + e) * HEADS + 2 * pair
            top, bottom = swapped(r.att_got[j].astype(F32), r.att_got[j + 1].astype(F32))
            r.att[e * BLOCK:e * BLOCK + HEAD, pair_cols(pair)] = top
            r.att[e * BLOCK + HEAD:(e + 1) * BLOCK, pair_cols(pair)] = bottom

    att = r.att[...]
    centered = att - jnp.mean(att, axis=-1, keepdims=True)
    inv_att = lax.rsqrt(jnp.mean(centered * centered, axis=-1, keepdims=True) + eps_norm)
    normed = centered * inv_att
    u = joined(lambda e: r.u[first_b + e]).astype(F32)
    gated = (normed * u).astype(BF16)
    x = joined(lambda e: r.x[first_b + e]).astype(F32)
    out_rows = x + dot_nn(gated, r.w_out[...])
    inv_y = lax.rsqrt(jnp.sum(out_rows * out_rows, axis=-1, keepdims=True) + eps_norm)
    unit_y = out_rows * inv_y
    unit_b = unit_y.astype(BF16)
    more = jnp.where(me == n_seq - 1, 0, 1)
    last_row = lax.broadcasted_iota(jnp.int32, (BLOCK, WIDTH), 0) == BLOCK - 1
    last_lane = lax.broadcasted_iota(jnp.int32, (1, BLOCK), 1) == BLOCK - 1

    def next_rows(e):
        shifted = pltpu.roll(r.x[first_b + e].astype(F32), BLOCK - 1, axis=0)
        return jnp.where(last_row, r.first[first_b + e].astype(F32)[:1] * more.astype(F32), shifted)

    x_next = joined(next_rows)
    pos_unit = (
        x_next * lax.rsqrt(jnp.sum(x_next * x_next, axis=-1, keepdims=True) + eps_norm)
    ).astype(BF16).astype(F32)
    pos_logit = logit_scale * jnp.sum(unit_b.astype(F32) * pos_unit, axis=-1, keepdims=True)

    def row_ids(e):
        shifted = pltpu.roll(r.ids[pl.ds(first_b + e, 1)], BLOCK - 1, axis=1)
        coming = pltpu.roll(r.next_ids[pl.ds(first_b + e, 1)], BLOCK - 1, axis=1) * more
        return jnp.transpose(jnp.broadcast_to(jnp.where(last_lane, coming, shifted), (BLOCK, BLOCK)))

    ids = joined(row_ids)
    lane_sum = jnp.zeros((rows, BLOCK), F32)
    for g in range(n_grp):
        neg_logit = logit_scale * dot_nt(unit_b, r.negs[g])
        for sub in range(n_neg // BLOCK):
            at = (g * n_neg) + sub * BLOCK
            hit = r.all_ids[g, n_here + sub:n_here + sub + 1] == ids
            exps = jnp.where(hit, 0.0, jnp.exp(neg_logit[:, sub * BLOCK:(sub + 1) * BLOCK]))
            r.exps[:, at:at + BLOCK] = exps
            lane_sum = lane_sum + exps
    pos_exp = jnp.exp(pos_logit)
    denom = pos_exp + jnp.sum(lane_sum, axis=-1, keepdims=True)

    def row_valid(e):
        pos = me * BLOCK + lax.broadcasted_iota(jnp.int32, (BLOCK, 1), 0)
        return jnp.where(pos + 1 < r.lens[grp * n_here + first_b + e], 1.0, 0.0)

    valid = joined(row_valid)
    row_loss = jnp.where(valid > 0.0, jnp.log(denom) - pos_logit, 0.0)
    r.loss[...] += jnp.broadcast_to(jnp.sum(row_loss, axis=0, keepdims=True), r.loss.shape)
    row_weight = valid * weight
    d_pos = row_weight * (pos_exp / denom - 1.0)
    scale = row_weight / denom
    neg_back = jnp.zeros((rows, WIDTH), F32)
    for g in range(n_grp):
        d_neg = (scale * r.exps[:, g * n_neg:(g + 1) * n_neg]).astype(BF16)
        neg_back = neg_back + dot_nn(d_neg, r.negs[g])
    d_unit = logit_scale * (d_pos * pos_unit + neg_back)
    d_out = (
        (d_unit - unit_y * jnp.sum(unit_y * d_unit, axis=-1, keepdims=True)) * inv_y
    ).astype(BF16)
    d_gate = dot_nt(d_out, r.w_out[...])
    d_norm = d_gate * u
    d_att = inv_att * (
        d_norm
        - jnp.mean(d_norm, axis=-1, keepdims=True)
        - normed * jnp.mean(d_norm * normed, axis=-1, keepdims=True)
    )
    for e in range(both):
        rows_e = d_att[e * BLOCK:(e + 1) * BLOCK]
        for pair in range(PAIRS):
            cols = pair_cols(pair)
            packed = swapped(rows_e[:HEAD, cols], rows_e[HEAD:, cols])
            for odd in range(2):
                r.datt_send[(first_b + e) * HEADS + 2 * pair + odd] = packed[odd].astype(BF16)

    @pl.loop(0, both * HEADS)
    def _(turn):
        j = first_b * HEADS + lax.rem(me + turn, both * HEADS)

        @pl.when(j != me)
        def _():
            copy_to(
                r.datt_send.at[j], r.datt_got.at[me], r.send_sem.at[12], r.datt_sem.at[me], {"seq": j}
            )

        @pl.when(j == me)
        def _():
            r.datt_got[me] = r.datt_send[me]

    r.grad_out[...] += dot_tn(gated, d_out)
    d_u = d_gate * normed
    for e in range(both):
        slope = r.slope[first_b + e, :, :WIDTH].astype(F32)
        r.d_pre[aligned((first_b + e) * BLOCK, BLOCK), :WIDTH] = (
            d_u[e * BLOCK:(e + 1) * BLOCK] * slope
        ).astype(BF16)


def widen(*refs):
    *blocks, joined, out = refs
    for at, block in enumerate(blocks):
        for half in range(4):
            values = block[half // 2, 0, half % 2].reshape(HEAD, BLOCK).astype(F32)
            if at < 4:
                joined[:, at * WIDTH + half * BLOCK:at * WIDTH + (half + 1) * BLOCK] = values
            else:
                out[:, half * BLOCK:(half + 1) * BLOCK] = values


def local(inputs, history, lengths, w_joined, w_out, neg_emb, neg_ids):
    n_here, block, width = inputs.shape
    n_seq = lax.axis_size("seq")
    length = n_seq * block
    lanes = 2 * HEAD
    rows = n_here * block
    n_neg = neg_emb.shape[0]
    dma = pltpu.SemaphoreType.DMA
    buffers = dict(
        xn=((n_here, block, width), BF16), xnt=((width, rows), BF16), u=((n_here, block, width), BF16),
        slope=((n_here, block, 4 * width), BF16), d_pre=((rows, 4 * width), BF16),
        send=((n_seq, BLOCK + HEAD, lanes), BF16), got=((n_seq, BLOCK + HEAD, lanes), BF16),
        att_send=((n_seq, HEAD, lanes), BF16), att_got=((n_seq, HEAD, lanes), BF16),
        datt_send=((n_seq, HEAD, lanes), BF16), datt_got=((n_seq, HEAD, lanes), BF16),
        grad_send=((n_seq, BLOCK + HEAD, lanes), BF16), grad_got=((n_seq, BLOCK + HEAD, lanes), BF16),
        first=((n_here, 16, width), BF16), ids=((2 * n_here, block), jnp.int32),
        next_ids=((2 * n_here, block), jnp.int32), negs=((4, n_neg, width), BF16),
        all_ids=((4, 2 * n_here, block), jnp.int32),
        kv0=((length // TILE, 2 * TILE, lanes), BF16), qa=((length, lanes), BF16),
        kt=((HEAD, length), BF16), acc=((FQ, lanes), F32), dq=((HEAD, length), F32), dkv=((BM, lanes), F32),
        att=((2 * block, width), F32), exps=((2 * block, 4 * n_neg), F32), grad_out=((width, width), F32),
        loss=((8, block), F32), loss_core=((8, block), F32), loss_sum=((3, 8, block), F32),
        loss_all=((3, 4, 8, block), F32), x=((n_here, block, width), BF16),
        w_joined=((width, 4 * width), BF16), w_out=((width, width), BF16), neg_emb=((n_neg, width), BF16),
        history=((n_here, block), jnp.int32), neg_ids=((n_here, block), jnp.int32),
    )
    wide = (8, 16, 16, block)
    for name in "uovkq":
        buffers[name + "_part"] = buffers[name + "_got"] = (wide, BF16)
        buffers[name + "_sum"] = buffers[name + "_got2"] = (wide[1:], BF16)
        buffers[name + "_red"] = (wide[2:], BF16)
    sems = dict(
        send_sem=13, one_sem=8, got_sem=n_seq, att_sem=n_seq, datt_sem=n_seq, grad_sem=2, loss_sem=8,
        red_send=20, red_recv=20, load_sem=6,
    )
    takes = ("lens", "x_in", "history_in", "neg_ids_in", "w_joined_in", "w_out_in", "neg_emb_in")
    gives = {name + "_full": (wide, BF16) for name in "uvqko"}
    gives["loss_out"] = ((1,), F32)
    names = takes + tuple(gives) + tuple(buffers) + tuple(sems)
    *grads, loss = pl.pallas_call(
        functools.partial(kernel, n_seq, names),
        out_shape=[jax.ShapeDtypeStruct(*kind) for kind in gives.values()],
        in_specs=[SMEM] + [pl.BlockSpec(memory_space=pl.ANY)] * (len(takes) - 1),
        out_specs=[VMEM] * 5 + [SMEM],
        scratch_shapes=[pltpu.VMEM(*kind) for kind in buffers.values()]
        + [dma((count,)) for count in sems.values()],
        compiler_params=pltpu.CompilerParams(
            collective_id=0, has_side_effects=True, vmem_limit_bytes=60 * 1024 * 1024
        ),
    )(lengths, inputs, history, neg_ids.reshape(-1, block), w_joined, w_out, neg_emb)
    taken = pl.BlockSpec((2, 1, 2, 4, 16, block), lambda at: (0, at // 2, 0, at % 2, 0, 0))
    joined, out = pl.pallas_call(
        widen,
        grid=(8,),
        out_shape=[
            jax.ShapeDtypeStruct((width, 4 * width), F32), jax.ShapeDtypeStruct((width, width), F32)
        ],
        in_specs=[taken] * 5,
        out_specs=[
            pl.BlockSpec((width // 8, 4 * width), lambda at: (at, 0)),
            pl.BlockSpec((width // 8, width), lambda at: (at, 0)),
        ],
        compiler_params=pltpu.CompilerParams(vmem_limit_bytes=60 * 1024 * 1024),
    )(*(grad.reshape((2, 4, 2, 8) + wide[2:]) for grad in grads))
    return (joined, out, loss.reshape(()))


def solution(mesh):
    placed = (
        P("grp", "seq", None),
        P("grp", "seq"),
        P(),
        P(),
        P(),
        P(("grp", "seq"), None),
        P(("grp", "seq")),
    )
    return jax.shard_map(
        local, mesh=mesh, in_specs=placed, out_specs=(P(), P(), P()), check_vma=False
    )
```
